32 devices in a mesh: section: 2 (over core), head: 4 (over z), rows: 4 (over y, x).
Axes of the slice: x: 2, y: 2, z: 4, core: 2. Of those that a mesh axis runs over, the one named last changes fastest.
Arguments:
- stream_in: bfloat16 [2, 2, 4, 512, 1024], P('section', None, None, 'rows', 'head'), may hold values from -6 to 6
- attn_gain: float32 [2, 1024], P('section'), may hold values from 0.5 to 1.5
- attn_shift: float32 [2, 1024], P('section'), may hold values from -1.5 to 1.5
- w_qk: bfloat16 [2, 1024, 1024], P('section', None, 'head'), may hold values from -0.25 to 0.25
- w_value: bfloat16 [2, 1024, 1024], P('section', None, 'head'), may hold values from -0.1875 to 0.1875
- w_out: bfloat16 [2, 1024, 1024], P('section', 'head'), may hold values from -0.75 to 0.75
- ffn_gain: float32 [2, 1024], P('section'), may hold values from 0.5 to 1.5
- ffn_shift: float32 [2, 1024], P('section'), may hold values from -1.5 to 1.5
- w_in: bfloat16 [2, 1024, 4096], P('section', None, 'head'), may hold values from -0.1875 to 0.1875
- b_in: float32 [2, 4096], P('section', 'head'), may hold values from -2.5 to 2.5
- w_back: bfloat16 [2, 4096, 1024], P('section', 'head'), may hold values from -0.09375 to 0.09375
- b_back: float32 [2, 1024], P('section', 'head'), may hold values from -1.5 to 1.5
- seq_ids: int32 [4, 512], P(None, 'rows'), may hold values from 0 to 2, as said below
- bucket_ids: int32 [4, 4, 512], P(None, None, 'rows'), may hold values from 0 to 7
- sort_order: int32 [4, 4, 512], P(None, None, 'rows'), may hold values from 0 to 511, as said below
Outputs:
- stream_out: float32 [2, 2, 4, 512, 1024], P('section', None, None, 'rows', 'head')
- grad_attn_gain: float32 [2, 1024], P('section')
- grad_attn_shift: float32 [2, 1024], P('section')
- grad_w_qk: float32 [2, 1024, 1024], P('section', None, 'head')
- grad_w_value: float32 [2, 1024, 1024], P('section', None, 'head')
- grad_w_out: float32 [2, 1024, 1024], P('section', 'head')
- grad_ffn_gain: float32 [2, 1024], P('section')
- grad_ffn_shift: float32 [2, 1024], P('section')
- grad_w_in: float32 [2, 1024, 4096], P('section', None, 'head')
- grad_b_in: float32 [2, 4096], P('section', 'head')
- grad_w_back: float32 [2, 4096, 1024], P('section', 'head')
- grad_b_back: float32 [2, 1024], P('section', 'head')
The draws below stay inside these ranges and needn't reach their ends.
Inputs may be any that keep to these rules, and one draw needn't show every extreme that they name: `seq_ids`: never falling along a micro-batch; a new sequence begins only at a multiple of 64 positions and only within the first or the last 128 positions, so one sequence runs from before position 128 to past position 384. `sort_order`: for each micro-batch and round a permutation of the positions, ordering the tokens by sequence, then by bucket in that round, then by position.
All inputs are finite; a program needn't handle non-finite values.
Results may differ from the reference program's by a relative error of at most 0.025.
Values may be sent and summed in bfloat16 or wider, within the bound.
No kernel may reach another device: no remote copies, remote signals or barrier semaphores. Data moves between devices by JAX's collectives and lax.ppermute only.
A program may use at most 192 MiB of HBM per device.

```python
import jax
import jax.numpy as jnp
from jax import lax

D = 1024
HEADS = 8
HDIM = 128
FF = 4096
ROUNDS = 4
BLOCK = 64
MB = 4
TOK_DEV = 128
SEQ = 512
NBUCK = 8
N_SECTION = 2


def layout_tables(key):
    n_blocks = SEQ // BLOCK
    per_device = TOK_DEV // BLOCK
    flags = jax.random.randint(jax.random.fold_in(key, 11), (MB, n_blocks), 0, 2)
    full_row = jax.random.randint(jax.random.fold_in(key, 13), (), 0, MB)
    flags = jnp.where(jnp.arange(MB)[:, None] == full_row, 1, flags)
    block_ids = jnp.arange(n_blocks)
    at_edge = (block_ids >= 1) & (block_ids < per_device) | (block_ids > n_blocks - per_device)
    block_seq = jnp.cumsum(flags * at_edge.astype(jnp.int32), axis=1)
    seq_table = jnp.repeat(block_seq, BLOCK, axis=1).astype(jnp.int32)
    bucket_table = jax.random.randint(jax.random.fold_in(key, 12), (MB, ROUNDS, SEQ), 0, NBUCK).astype(jnp.int32)
    position = jnp.arange(SEQ)
    sort_key = seq_table[:, None, :] * (NBUCK * SEQ) + bucket_table * SEQ + position
    order_table = jnp.argsort(sort_key, axis=-1, stable=True).astype(jnp.int32)
    return (seq_table, bucket_table, order_table)


def draw_seq_ids(key, part):
    return layout_tables(key)[0]


def draw_bucket_ids(key, part):
    return layout_tables(key)[1]


def draw_sort_order(key, part):
    return layout_tables(key)[2]


def shard_levels(rng, dims, cuts, low, top_value):
    gain, own = 1.0, jax.random.fold_in(rng, 6)
    for dim, blocks in cuts:
        draws = jnp.exp(jax.random.uniform(jax.random.fold_in(own, dim), (blocks,), jnp.float32, low / len(cuts), top_value / len(cuts)))
        gain = gain * jnp.repeat(draws, dims[dim] // blocks).reshape([-1 if axis == dim else 1 for axis in range(len(dims))])
    return gain


def gaussian(rng, extent, deviation, limit, shards=(), held_as=jnp.bfloat16):
    loudness = shard_levels(rng, extent, shards, -0.22, 0.18) if shards else 1.0
    entries = jax.random.normal(rng, extent, jnp.float32) * deviation * loudness
    return jnp.minimum(jnp.maximum(entries, -limit), limit).astype(held_as)


def setup_inputs(seed: int = 0) -> dict:
    seeds = jax.random.split(jax.random.key(seed), 16)
    return {
        "stream_in": gaussian(seeds[0], (2, 2, MB, SEQ, D), 1.0, 6.0, ((0, 2), (3, 4), (4, 4))),
        "attn_gain": jnp.clip(1.0 + 0.1 * jax.random.normal(seeds[1], (N_SECTION, D), jnp.float32), 0.5, 1.5),
        "attn_shift": gaussian(seeds[2], (N_SECTION, D), 0.3, 1.5, ((0, 2),), jnp.float32),
        "w_qk": gaussian(seeds[3], (N_SECTION, D, HEADS * HDIM), (D // 2) ** -0.5, 0.25, ((0, 2), (2, 4))),
        "w_value": gaussian(seeds[4], (N_SECTION, D, HEADS * HDIM), D ** -0.5, 0.1875, ((0, 2), (2, 4))),
        "w_out": gaussian(seeds[5], (N_SECTION, HEADS * HDIM, D), (HEADS * HDIM // 16) ** -0.5, 0.75, ((0, 2), (1, 4))),
        "ffn_gain": jnp.clip(1.0 + 0.1 * jax.random.normal(seeds[6], (N_SECTION, D), jnp.float32), 0.5, 1.5),
        "ffn_shift": gaussian(seeds[7], (N_SECTION, D), 0.3, 1.5, ((0, 2),), jnp.float32),
        "w_in": gaussian(seeds[8], (N_SECTION, D, FF), D ** -0.5, 0.1875, ((0, 2), (2, 4))),
        "b_in": gaussian(seeds[9], (N_SECTION, FF), 0.5, 2.5, ((0, 2), (1, 4)), jnp.float32),
        "w_back": gaussian(seeds[10], (N_SECTION, FF, D), FF ** -0.5, 0.09375, ((0, 2), (1, 4))),
        "b_back": gaussian(seeds[11], (N_SECTION, D), 0.3, 1.5, ((0, 2), (1, 4)), jnp.float32),
        "seq_ids": draw_seq_ids(jax.random.fold_in(seeds[15], 71), 0),
        "bucket_ids": draw_bucket_ids(jax.random.fold_in(seeds[15], 71), 0),
        "sort_order": draw_sort_order(jax.random.fold_in(seeds[15], 71), 0),
    }


@jax.custom_vjp
def low(v):
    return lax.optimization_barrier(v.astype(jnp.bfloat16)).astype(jnp.float32)

@jax.custom_vjp
def low_back(v):
    return v

def low_keep(v):
    return (low(v), None)

def low_pass(kept, grad):
    return (grad,)

def back_keep(v):
    return (v, None)

def back_low(kept, grad):
    return (low(grad),)
low.defvjp(low_keep, low_pass)
low_back.defvjp(back_keep, back_low)

def matmul(left_op, right_op):
    return jnp.dot(left_op, right_op, precision=lax.Precision.HIGHEST)

def layer_norm(rows_in, norm_gain, norm_shift):
    centre = lax.optimization_barrier(jnp.mean(rows_in, axis=-1, keepdims=True))
    centred = rows_in - centre
    spread = lax.optimization_barrier(jnp.mean(centred * centred, axis=-1, keepdims=True))
    return centred * lax.rsqrt(spread + 1e-05) * norm_gain + norm_shift

def windowed(blocks):
    earlier = jnp.concatenate([jnp.zeros_like(blocks[:1]), blocks[:-1]], axis=0)
    return jnp.concatenate([earlier, blocks], axis=1)

def hashed_round(queries, values, order_r, seq_row, bucket_row):
    seq_len = order_r.shape[0]
    n_blocks = seq_len // BLOCK
    q_sorted = queries[order_r]
    v_sorted = values[order_r]
    keys_norm = low(q_sorted * lax.rsqrt(lax.optimization_barrier(jnp.sum(q_sorted * q_sorted, axis=-1, keepdims=True)) + 1e-06))
    q_blocks = q_sorted.reshape(n_blocks, BLOCK, HEADS, HDIM)
    key_win = windowed(keys_norm.reshape(n_blocks, BLOCK, HEADS, HDIM))
    value_win = windowed(v_sorted.reshape(n_blocks, BLOCK, HEADS, HDIM))
    place_q = order_r.reshape(n_blocks, BLOCK)
    seq_q = seq_row[order_r].reshape(n_blocks, BLOCK)
    bucket_q = bucket_row[order_r].reshape(n_blocks, BLOCK)
    live_win = windowed(jnp.ones((n_blocks, BLOCK), jnp.int32))[:, None, :] > 0
    place_win = windowed(place_q)[:, None, :]
    same_group = live_win & (windowed(seq_q)[:, None, :] == seq_q[:, :, None])
    same_group = same_group & (windowed(bucket_q)[:, None, :] == bucket_q[:, :, None])
    allowed = same_group & (place_win < place_q[:, :, None])
    itself = live_win & (place_win == place_q[:, :, None])
    masking = jnp.where(allowed, 0.0, jnp.where(itself, -100000.0, -1000000000.0))
    scores = low_back(jnp.einsum('cqhd,ckhd->chqk', q_blocks, key_win, precision=lax.Precision.HIGHEST))
    scores = scores + masking[:, None]
    highest = lax.optimization_barrier(jnp.max(scores, axis=-1, keepdims=True))
    log_total = highest + jnp.log(lax.optimization_barrier(jnp.sum(jnp.exp(scores - highest), axis=-1, keepdims=True)))
    attn_prob = low(jnp.exp(scores - log_total))
    mixed_r = jnp.einsum('chqk,ckhd->cqhd', attn_prob, value_win, precision=lax.Precision.HIGHEST)
    mixed_r = mixed_r.reshape(seq_len, HEADS, HDIM)
    return (mixed_r, jnp.transpose(log_total[..., 0], (0, 2, 1)).reshape(seq_len, HEADS))

def hashed_branch(second_in, norm_gain, norm_shift, w_qk, w_value, w_out, seq_row, bucket_rows, order_rows):
    seq_len = second_in.shape[0]
    normed = low(layer_norm(second_in, norm_gain, norm_shift))
    queries = low_back(low(matmul(normed, w_qk))).reshape(seq_len, HEADS, HDIM)
    values = low_back(low(matmul(normed, w_value))).reshape(seq_len, HEADS, HDIM)
    round_outs = []
    round_stats = []
    for round_no in range(ROUNDS):
        order_r = order_rows[round_no]
        mixed_r, stats_r = hashed_round(queries, values, order_r, seq_row, bucket_rows[round_no])
        round_outs.append(low_back(jnp.zeros_like(mixed_r).at[order_r].set(mixed_r)))
        round_stats.append(jnp.zeros_like(stats_r).at[order_r].set(stats_r))
    stats_all = jnp.stack(round_stats)
    top_stat = lax.optimization_barrier(jnp.max(stats_all, axis=0, keepdims=True))
    shares = jnp.exp(stats_all - top_stat)
    shares = shares / lax.optimization_barrier(jnp.sum(shares, axis=0, keepdims=True))
    mixed_out = lax.optimization_barrier(jnp.sum(shares[..., None] * jnp.stack(round_outs), axis=0)).reshape(seq_len, HEADS * HDIM)
    mixed_out = low_back(low(mixed_out))
    return low_back(matmul(mixed_out, w_out))

def feed_forward(first_out, norm_gain, norm_shift, w_in, b_in, w_back, b_back):
    normed = low(layer_norm(first_out, norm_gain, norm_shift))
    pre_act = low_back(matmul(normed, w_in) + b_in)
    active = low(jax.nn.gelu(pre_act))
    return low_back(matmul(active, w_back)) + b_back

def reference(stream_in, attn_gain, attn_shift, w_qk, w_value, w_out, ffn_gain, ffn_shift, w_in, b_in, w_back, b_back, seq_ids, bucket_ids, sort_order):
    params = tuple((weight_arr.astype(jnp.float32) for weight_arr in (attn_gain, attn_shift, w_qk, w_value, w_out, ffn_gain, ffn_shift, w_in, b_in, w_back, b_back)))

    def stack_forward(stream_arg, weight_arg, seq_row, bucket_rows, order_rows):
        first_in, second_in = (stream_arg[0], stream_arg[1])
        for layer_no in range(N_SECTION):
            layer_w = [weight_one[layer_no] for weight_one in weight_arg]
            first_out = first_in + hashed_branch(second_in, *layer_w[:5], seq_row, bucket_rows, order_rows)
            second_out = second_in + feed_forward(first_out, *layer_w[5:])
            first_in, second_in = (first_out, second_out)
        return jnp.stack([first_in, second_in])

    def micro_step(totals, batch_no):
        stream_arg = stream_in[0, :, batch_no].astype(jnp.float32)
        cotangent = stream_in[1, :, batch_no].astype(jnp.float32)
        seq_row = seq_ids[batch_no]
        bucket_rows = bucket_ids[batch_no]
        order_rows = sort_order[batch_no]
        outputs, pull_back = jax.vjp(lambda stream_var, weight_var: stack_forward(stream_var, weight_var, seq_row, bucket_rows, order_rows), stream_arg, params)
        grad_stream, grad_params = pull_back(cotangent)
        totals = tuple((total_one + grad_one for total_one, grad_one in zip(totals, grad_params)))
        return (totals, (outputs, grad_stream))
    zero_grads = tuple((jnp.zeros_like(weight_arr) for weight_arr in params))
    totals, (outputs, grads_in) = lax.scan(micro_step, zero_grads, jnp.arange(MB))
    stream_out = jnp.stack([jnp.transpose(grads_in, (1, 0, 2, 3)), jnp.transpose(outputs, (1, 0, 2, 3))])
    return (stream_out, totals[0], totals[1], totals[2], totals[3], totals[4], totals[5], totals[6], totals[7], totals[8], totals[9], totals[10])
```

```python
import jax
import jax.numpy as jnp
from jax import lax
from jax.experimental import pallas as pl
from jax.experimental.pallas import tpu as pltpu
from jax.sharding import PartitionSpec as P

HDIM = 128
BLOCK = 64


def from_behind(x, axis, by):
    length = lax.axis_size(axis)
    pairs = [(i, i + by) for i in range(length) if 0 <= i + by < length]
    return lax.ppermute(x, axis, pairs)


def shortened(x):

    def short(part):
        return part.astype(jnp.bfloat16) if part.dtype == jnp.float32 else part

    return jax.tree.map(short, x)


def dot_plain(left_op, right_op):
    return jnp.dot(left_op, right_op, preferred_element_type=jnp.float32)


def dot_right_t(left_op, right_op):
    return lax.dot_general(
        left_op, right_op, (((1,), (1,)), ((), ())), preferred_element_type=jnp.float32
    )


def dot_left_t(left_op, right_op):
    return lax.dot_general(
        left_op, right_op, (((0,), (0,)), ((), ())), preferred_element_type=jnp.float32
    )


def norm_parts(rows_in, norm_gain, norm_shift):
    centre = jnp.mean(rows_in, axis=-1, keepdims=True)
    centred = rows_in - centre
    inv_std = lax.rsqrt(jnp.mean(centred * centred, axis=-1, keepdims=True) + 1e-05)
    scaled = centred * inv_std
    return (scaled * norm_gain + norm_shift, scaled, inv_std)


def norm_back(grad_out, scaled, inv_std, norm_gain):
    grad_scaled = grad_out * norm_gain
    centred_grad = grad_scaled - jnp.mean(grad_scaled, axis=-1, keepdims=True)
    centred_grad = centred_grad - scaled * jnp.mean(grad_scaled * scaled, axis=-1, keepdims=True)
    return (inv_std * centred_grad, jnp.sum(grad_out * scaled, axis=0), jnp.sum(grad_out, axis=0))


def own_columns(full_rows, col_width):
    return lax.dynamic_slice_in_dim(full_rows, lax.axis_index("head") * col_width, col_width, 1)


def full_features(local_rows):
    return lax.all_gather(local_rows, "head", axis=1, tiled=True)


def head_reduce(partial_rows):
    return lax.psum_scatter(partial_rows, "head", scatter_dimension=1, tiled=True)


def grad_features(local_grad):
    return lax.all_gather(local_grad.astype(jnp.bfloat16), "head", axis=1, tiled=True)


def grad_reduce(partial_grad):
    return lax.psum(partial_grad, "head")


def slot_table(slot_ids, seq_rows):
    return (slot_ids[..., None] == jnp.arange(seq_rows, dtype=jnp.int32)).astype(jnp.float32)


def span_blocks(extended, n_blocks):
    blocks = extended.reshape((extended.shape[0], n_blocks + 1, BLOCK) + extended.shape[2:])
    return jnp.concatenate([blocks[:, :-1], blocks[:, 1:]], axis=2)


def fold_blocks(windows):
    front_half = windows[:, :, :BLOCK]
    back_half = windows[:, :, BLOCK:]
    zero_blk = jnp.zeros_like(front_half[:, :1])
    folded = jnp.concatenate([front_half, zero_blk], axis=1) + jnp.concatenate(
        [zero_blk, back_half], axis=1
    )
    return folded.reshape((folded.shape[0], -1) + folded.shape[3:])


def window_scores(gathered, slots, live_prev):
    qv_all, seq_all, bucket_all = gathered
    rounds_n, extended = slots.shape
    n_blocks = extended // BLOCK - 1
    half_width = qv_all.shape[1] // 2
    heads_here = half_width // HDIM
    picked = qv_all[slots]
    query_ext = picked[..., :half_width].reshape(rounds_n, extended, heads_here, HDIM)
    value_ext = picked[..., half_width:].reshape(rounds_n, extended, heads_here, HDIM)
    query_wide = query_ext.astype(jnp.float32)
    inv_norm = lax.rsqrt(jnp.sum(query_wide * query_wide, axis=-1, keepdims=True) + 1e-06)
    key_win = span_blocks((query_wide * inv_norm).astype(jnp.bfloat16), n_blocks)
    value_win = span_blocks(value_ext, n_blocks)
    query_blocks = query_ext[:, BLOCK:].reshape(rounds_n, n_blocks, BLOCK, heads_here, HDIM)
    seq_ext = seq_all[slots]
    bucket_ext = jnp.take_along_axis(bucket_all, slots, axis=1)
    live_ext = jnp.concatenate(
        [
            jnp.broadcast_to(live_prev, (rounds_n, BLOCK)),
            jnp.ones((rounds_n, extended - BLOCK), jnp.bool_),
        ],
        axis=1,
    )

    def query_part(int_table):
        return int_table[:, BLOCK:].reshape(rounds_n, n_blocks, BLOCK)[..., None]

    def key_part(int_table):
        return span_blocks(int_table, n_blocks)[:, :, None, :]

    same_group = key_part(live_ext) & (key_part(seq_ext) == query_part(seq_ext))
    same_group = same_group & (key_part(bucket_ext) == query_part(bucket_ext))
    allowed = same_group & (key_part(slots) < query_part(slots))
    itself = key_part(live_ext) & (key_part(slots) == query_part(slots))
    masking = jnp.where(allowed, 0.0, jnp.where(itself, -100000.0, -1000000000.0)).astype(
        jnp.float32
    )
    scores = jnp.einsum(
        "rcqhd,rckhd->rchqk", query_blocks, key_win, preferred_element_type=jnp.float32
    )
    scores = scores + masking[:, :, None]
    highest = jnp.max(scores, axis=-1, keepdims=True)
    log_total = highest + jnp.log(jnp.sum(jnp.exp(scores - highest), axis=-1, keepdims=True))
    attn_prob = jnp.exp(scores - log_total)
    return (query_wide, inv_norm, query_blocks, key_win, value_win, attn_prob, log_total)


def sorted_forward(gathered, slots, live_prev):
    query_wide, inv_norm, query_blocks, key_win, value_win, attn_prob, log_total = window_scores(
        gathered, slots, live_prev
    )
    rounds_n = slots.shape[0]
    round_mix = jnp.einsum(
        "rchqk,rckhd->rcqhd",
        attn_prob.astype(jnp.bfloat16),
        value_win,
        preferred_element_type=jnp.float32,
    )
    results = round_mix.reshape(rounds_n, -1, round_mix.shape[3] * HDIM)
    round_stats = jnp.transpose(log_total[..., 0], (0, 1, 3, 2)).reshape(
        rounds_n, results.shape[1], -1
    )
    return (results, round_stats)


def to_owners(results, round_stats, own_slots, rows_n):
    rounds_n, tok_rows, feat_width = results.shape
    seq_rows = rows_n * tok_rows
    placing = slot_table(own_slots, seq_rows)
    joined = jnp.concatenate([results, round_stats], axis=-1)
    spread_all = jnp.einsum("rsp,rsf->rpf", placing, joined, precision=lax.Precision.HIGHEST)
    spread_out = spread_all[..., :feat_width]
    spread_stats = spread_all[..., feat_width:]
    back_out, back_stats = (
        lax.all_to_all(
            spread_out.reshape(rounds_n, rows_n, tok_rows, feat_width),
            "rows",
            split_axis=1,
            concat_axis=1,
            tiled=True,
        ),
        lax.all_to_all(
            spread_stats.reshape(rounds_n, rows_n, tok_rows, -1),
            "rows",
            split_axis=1,
            concat_axis=1,
            tiled=True,
        ),
    )
    return (jnp.sum(back_out, axis=1), jnp.sum(back_stats, axis=1))


def sorted_backward(gathered, slots, live_prev, received):
    query_wide, inv_norm, query_blocks, key_win, value_win, attn_prob, log_total = window_scores(
        gathered, slots, live_prev
    )
    grad_all, share_all, stat_all = received
    own_slots = slots[:, BLOCK:]
    rounds_n, n_blocks, heads_here = (attn_prob.shape[0], attn_prob.shape[1], attn_prob.shape[2])
    grad_pick = grad_all[own_slots].reshape(rounds_n, n_blocks, BLOCK, heads_here, HDIM)
    share_pick = jnp.take_along_axis(share_all, own_slots[..., None], axis=1).reshape(
        rounds_n, n_blocks, BLOCK, heads_here
    )
    stat_pick = jnp.take_along_axis(stat_all, own_slots[..., None], axis=1).reshape(
        rounds_n, n_blocks, BLOCK, heads_here
    )
    grad_round = (share_pick[..., None] * grad_pick).astype(jnp.bfloat16)
    grad_prob = jnp.einsum(
        "rcqhd,rckhd->rchqk", grad_round, value_win, preferred_element_type=jnp.float32
    )
    row_dot = jnp.sum(attn_prob * grad_prob, axis=-1, keepdims=True)
    stat_term = jnp.transpose(stat_pick, (0, 1, 3, 2))[..., None]
    grad_scores = (attn_prob * (grad_prob - row_dot + stat_term)).astype(jnp.bfloat16)
    grad_query = jnp.einsum(
        "rchqk,rckhd->rcqhd", grad_scores, key_win, preferred_element_type=jnp.float32
    )
    grad_key = fold_blocks(
        jnp.einsum(
            "rchqk,rcqhd->rckhd", grad_scores, query_blocks, preferred_element_type=jnp.float32
        )
    )
    grad_value = fold_blocks(
        jnp.einsum(
            "rchqk,rcqhd->rckhd",
            attn_prob.astype(jnp.bfloat16),
            grad_round,
            preferred_element_type=jnp.float32,
        )
    )
    norm_cubed = inv_norm * inv_norm * inv_norm
    grad_query_ext = (
        inv_norm * grad_key
        - norm_cubed * jnp.sum(query_wide * grad_key, axis=-1, keepdims=True) * query_wide
    )
    grad_query_own = grad_query.reshape(rounds_n, n_blocks * BLOCK, heads_here, HDIM)
    grad_query_ext = grad_query_ext + jnp.pad(grad_query_own, ((0, 0), (BLOCK, 0), (0, 0), (0, 0)))
    extended = slots.shape[1]
    stacked = jnp.concatenate(
        [
            grad_query_ext.reshape(rounds_n, extended, -1),
            grad_value.reshape(rounds_n, extended, -1),
        ],
        axis=-1,
    )
    placing = slot_table(slots, share_all.shape[1])
    buffer = jnp.einsum("rep,ref->pf", placing, stacked, precision=lax.Precision.HIGHEST)
    return lax.psum_scatter(buffer, "rows", scatter_dimension=0, tiled=True)


def attention_inputs(second_in, params):
    normed, scaled, inv_std = norm_parts(full_features(second_in), params[0], params[1])
    low_in = normed.astype(jnp.bfloat16)
    qv_pairs = jnp.concatenate(
        [dot_plain(low_in, params[2]), dot_plain(low_in, params[3])], axis=1
    ).astype(jnp.bfloat16)
    return (low_in, scaled, inv_std, qv_pairs)


def attention_rounds(qv_pairs, int_here, live_prev, rows_n):
    seq_here, bucket_here, order_here, prev_here = int_here
    gathered = (
        lax.all_gather(qv_pairs, "rows", axis=0, tiled=True),
        lax.all_gather(seq_here, "rows", axis=0, tiled=True),
        lax.all_gather(bucket_here, "rows", axis=1, tiled=True),
    )
    slots = jnp.concatenate([prev_here, order_here], axis=1)
    results, round_stats = sorted_forward(gathered, slots, live_prev)
    owned_out, owned_stats = to_owners(results, round_stats, order_here, rows_n)
    return (gathered, owned_out, owned_stats)


def combine_rounds(owned_out, owned_stats):
    rounds_n, tok_rows, feat_width = owned_out.shape
    heads_here = owned_stats.shape[2]
    top_stat = jnp.max(owned_stats, axis=0, keepdims=True)
    shares = jnp.exp(owned_stats - top_stat)
    shares = shares / jnp.sum(shares, axis=0, keepdims=True)
    mixed_out = jnp.sum(
        shares[..., None] * owned_out.reshape(rounds_n, tok_rows, heads_here, HDIM), axis=0
    )
    return (mixed_out.reshape(tok_rows, feat_width).astype(jnp.bfloat16), shares)


def ffn_forward(first_out, params):
    normed, scaled, inv_std = norm_parts(full_features(first_out), params[5], params[6])
    low_in = normed.astype(jnp.bfloat16)
    pre_act = dot_plain(low_in, params[7]) + params[8]
    active = jax.nn.gelu(pre_act).astype(jnp.bfloat16)
    branch = head_reduce(dot_plain(active, params[9])) + params[10]
    return (branch, (low_in, scaled, inv_std, pre_act, active))


def layer_forward(first_in, second_in, params, int_here, live_prev, rows_n):
    low_in, scaled, inv_std, qv_pairs = attention_inputs(second_in, params)
    kept_state = attention_rounds(qv_pairs, int_here, live_prev, rows_n)
    mixed_low, shares = combine_rounds(kept_state[1], kept_state[2])
    first_out = first_in + head_reduce(dot_plain(mixed_low, params[4]))
    second_out = second_in + ffn_forward(first_out, params)[0]
    return (first_out, second_out, kept_state)


def layer_backward(first_out, second_out, grad_one, grad_two, params, int_here, live_prev, rows_n):
    ffn_branch, (ffn_low, ffn_scaled, ffn_inv, pre_act, active) = ffn_forward(first_out, params)
    second_in = second_out - ffn_branch
    grad_full = grad_features(grad_two)
    gelu_value, gelu_pull = jax.vjp(jax.nn.gelu, pre_act)
    grad_pre = gelu_pull(dot_right_t(grad_full, params[9]))[0].astype(jnp.bfloat16)
    grad_w_back = dot_left_t(active, grad_full)
    grad_b_back = jnp.sum(grad_two, axis=0)
    grad_w_in = dot_left_t(ffn_low, grad_pre)
    grad_b_in = jnp.sum(grad_pre.astype(jnp.float32), axis=0)
    grad_normed = grad_reduce(dot_right_t(grad_pre, params[7]))
    grad_rows, grad_ffn_gain, grad_ffn_shift = norm_back(
        grad_normed, ffn_scaled, ffn_inv, params[5]
    )
    grad_one = grad_one + own_columns(grad_rows, grad_one.shape[1])
    low_in, scaled, inv_std, qv_pairs = attention_inputs(second_in, params)
    state_here = attention_rounds(qv_pairs, int_here, live_prev, rows_n)
    gathered, owned_out, owned_stats = state_here
    mixed_low, shares = combine_rounds(owned_out, owned_stats)
    first_in = first_out - head_reduce(dot_plain(mixed_low, params[4]))
    grad_full = grad_features(grad_one)
    grad_w_out = dot_left_t(mixed_low, grad_full)
    grad_mixed = dot_right_t(grad_full, params[4]).astype(jnp.bfloat16)
    rounds_n, tok_rows, heads_here = owned_stats.shape
    grad_wide = grad_mixed.astype(jnp.float32)
    per_round = jnp.sum(
        grad_wide.reshape(1, tok_rows, heads_here, HDIM)
        * owned_out.reshape(rounds_n, tok_rows, heads_here, HDIM),
        axis=-1,
    )
    grad_stats = shares * (per_round - jnp.sum(shares * per_round, axis=0, keepdims=True))
    received = (
        lax.all_gather(grad_wide, "rows", axis=0, tiled=True),
        lax.all_gather(shares, "rows", axis=1, tiled=True),
        lax.all_gather(grad_stats, "rows", axis=1, tiled=True),
    )
    slots = jnp.concatenate([int_here[3], int_here[2]], axis=1)
    owned_grad = sorted_backward(gathered, slots, live_prev, received)
    qk_width = grad_mixed.shape[1]
    grad_query = owned_grad[:, :qk_width].astype(jnp.bfloat16)
    grad_value = owned_grad[:, qk_width:].astype(jnp.bfloat16)
    grad_w_qk = dot_left_t(low_in, grad_query)
    grad_w_value = dot_left_t(low_in, grad_value)
    grad_normed = grad_reduce(
        dot_right_t(grad_query, params[2]) + dot_right_t(grad_value, params[3])
    )
    grad_rows, grad_attn_gain, grad_attn_shift = norm_back(grad_normed, scaled, inv_std, params[0])
    grad_second = grad_two + own_columns(grad_rows, grad_two.shape[1])
    grads = (
        grad_attn_gain,
        grad_attn_shift,
        grad_w_qk,
        grad_w_value,
        grad_w_out,
        grad_ffn_gain,
        grad_ffn_shift,
        grad_w_in,
        grad_b_in,
        grad_w_back,
        grad_b_back,
    )
    return (first_in, second_in, grad_one, grad_second, grads)


def local(
    stream_in,
    attn_gain,
    attn_shift,
    w_qk,
    w_value,
    w_out,
    ffn_gain,
    ffn_shift,
    w_in,
    b_in,
    w_back,
    b_back,
    seq_ids,
    bucket_ids,
    sort_order,
):
    section_pos = lax.axis_index("section")
    is_first = section_pos == 0
    rows_n = lax.axis_size("rows")
    live_prev = lax.axis_index("rows") > 0
    micro_n = stream_in.shape[2]
    params = tuple(
        (
            weight_arr[0]
            for weight_arr in (
                attn_gain,
                attn_shift,
                w_qk,
                w_value,
                w_out,
                ffn_gain,
                ffn_shift,
                w_in,
                b_in,
                w_back,
                b_back,
            )
        )
    )
    prev_all = from_behind(sort_order[:, :, sort_order.shape[2] - BLOCK :], "rows", 1)
    own_stream = stream_in[0].astype(jnp.float32)

    def pick_batch(int_table, batch_no):
        return lax.dynamic_index_in_dim(int_table, batch_no, 0, keepdims=False)

    def ints_for(batch_no):
        return (
            pick_batch(seq_ids, batch_no),
            pick_batch(bucket_ids, batch_no),
            pick_batch(sort_order, batch_no),
            pick_batch(prev_all, batch_no),
        )

    message = jnp.zeros_like(own_stream[:, 0])
    outputs_fwd = []
    kept_list = []
    for tick_no in range(micro_n + 1):
        batch_no = jnp.clip(tick_no - section_pos, 0, micro_n - 1)
        source = jnp.where(is_first, own_stream[:, min(tick_no, micro_n - 1)], message)
        first_out, second_out, kept_state = layer_forward(
            source[0], source[1], params, ints_for(batch_no), live_prev, rows_n
        )
        outputs_fwd.append(jnp.stack([first_out, second_out]))
        kept_list.append(kept_state)
        if tick_no < micro_n:
            message = from_behind(outputs_fwd[-1], "section", 1)
    grads_total = tuple((jnp.zeros(weight_arr.shape, jnp.float32) for weight_arr in params))
    back_msg = jnp.zeros((4,) + own_stream.shape[2:], jnp.float32)
    dx_list = []
    for tick_no in range(micro_n + 1):
        batch_raw = tick_no - 1 + section_pos
        is_live = (batch_raw >= 0) & (batch_raw < micro_n)
        batch_no = jnp.clip(batch_raw, 0, micro_n - 1)
        outs_here = jnp.where(is_first, back_msg[:2], outputs_fwd[min(tick_no + 1, micro_n)])
        grads_here = jnp.where(is_first, back_msg[2:], own_stream[:, min(tick_no, micro_n - 1)])
        first_in, second_in, grad_first, grad_second, grads = layer_backward(
            outs_here[0],
            outs_here[1],
            grads_here[0],
            grads_here[1],
            params,
            ints_for(batch_no),
            live_prev,
            rows_n,
        )
        dx_list.append(jnp.stack([grad_first, grad_second]))
        grads = tuple((jnp.where(is_live, grad_one, 0.0) for grad_one in grads))
        grads_total = tuple(
            (total_one + grad_one for total_one, grad_one in zip(grads_total, grads))
        )
        if tick_no < micro_n:
            back_msg = from_behind(
                jnp.stack([first_in, second_in, grad_first, grad_second]), "section", -1
            )
    grads_total = jax.tree.map(
        lambda part: part.astype(jnp.float32), lax.psum(shortened(grads_total), "rows")
    )
    stream_out = jnp.where(
        is_first, jnp.stack(dx_list[1:], axis=1), jnp.stack(outputs_fwd[1:], axis=1)
    )[None]
    return (
        stream_out,
        grads_total[0][None],
        grads_total[1][None],
        grads_total[2][None],
        grads_total[3][None],
        grads_total[4][None],
        grads_total[5][None],
        grads_total[6][None],
        grads_total[7][None],
        grads_total[8][None],
        grads_total[9][None],
        grads_total[10][None],
    )


VMEM_ROOM = 48 * 1024 * 1024
TILE = 128
GELU_C = 0.7978845608


def kernel_call(body, out_types, args, scalars=None, scratch=(), flops=0):
    specs = [pl.BlockSpec(memory_space=pltpu.VMEM) for _ in args]
    if scalars is not None:
        args = (scalars, *args)
        specs = [pl.BlockSpec(memory_space=pltpu.SMEM)] + specs
    outs = tuple(jax.ShapeDtypeStruct(shape, dtype) for shape, dtype in out_types)
    moved = sum(a.size * a.dtype.itemsize for a in (*args, *outs))
    return pl.pallas_call(
        body,
        out_shape=outs,
        in_specs=specs,
        out_specs=tuple(pl.BlockSpec(memory_space=pltpu.VMEM) for _ in outs),
        scratch_shapes=list(scratch),
        compiler_params=pltpu.CompilerParams(vmem_limit_bytes=VMEM_ROOM),
        cost_estimate=pl.CostEstimate(flops=flops, bytes_accessed=moved, transcendentals=0),
    )(*args)


def flip_pairs(n, by):
    return [(i, i ^ by) for i in range(n)]


def swap_cores(x):
    return lax.ppermute(x, "section", [(0, 1), (1, 0)])


def xor_recv(parts, axis):
    return [lax.ppermute(part, axis, flip_pairs(4, k + 1)) for k, part in enumerate(parts)]


def gather_tokens(own, axis):
    near = jnp.concatenate([own] + xor_recv([own] * 3, axis), axis=0)
    return near, swap_cores(near)


def scatter_tokens(far_part, near_part, axis):
    arrived = swap_cores(far_part)
    n_own = near_part.shape[0] // 4
    width = near_part.shape[1]

    def body(near, far, *outs):
        for k in range(4):
            rows = pl.ds(k * n_own, n_own)
            outs[k][...] = (near[rows, :] + far[rows, :].astype(jnp.float32)).astype(outs[k].dtype)

    kept, *sent = kernel_call(
        body,
        [((n_own, width), jnp.float32)] + [((n_own, width), jnp.bfloat16)] * 3,
        (near_part, arrived),
    )
    return [kept] + xor_recv(sent, axis)


def rows_norm(rows_in):
    centred = rows_in - jnp.mean(rows_in, axis=-1, keepdims=True)
    inv_std = lax.rsqrt(jnp.mean(centred * centred, axis=-1, keepdims=True) + 1e-05)
    return centred * inv_std, inv_std


def sum_parts(parts):
    total = parts[0][...]
    for part in parts[1:]:
        total = total + part[...].astype(jnp.float32)
    return total


def residual_norm(resid, parts, shift_out, gain, shift):
    n_own, width = resid.shape

    def body(resid, gain, shift, shift_out, p0, p1, p2, p3, stream, low):
        rows = resid[...] + sum_parts((p0, p1, p2, p3)) + shift_out[...]
        stream[...] = rows
        scaled, _ = rows_norm(rows)
        low[...] = (scaled * gain[...] + shift[...]).astype(jnp.bfloat16)

    return kernel_call(
        body,
        [((n_own, width), jnp.float32), ((n_own, width), jnp.bfloat16)],
        (resid, gain, shift, shift_out, *parts),
    )


def residual_only(resid, parts, shift_out):
    def body(resid, shift_out, p0, p1, p2, p3, stream):
        stream[...] = resid[...] + sum_parts((p0, p1, p2, p3)) + shift_out[...]

    return kernel_call(body, [(resid.shape, jnp.float32)], (resid, shift_out, *parts))[0]


def norm_backward(resid, parts, stream, gain):
    n_own, width = resid.shape

    def body(resid, stream, gain, p0, p1, p2, p3, out, low, small):
        grad_out = sum_parts((p0, p1, p2, p3))
        scaled, inv_std = rows_norm(stream[...])
        grad_scaled = grad_out * gain[...]
        centred = grad_scaled - jnp.mean(grad_scaled, axis=-1, keepdims=True)
        centred = centred - scaled * jnp.mean(grad_scaled * scaled, axis=-1, keepdims=True)
        total = resid[...] + inv_std * centred
        out[...] = total
        low[...] = total.astype(jnp.bfloat16)
        small[0:1, :] = jnp.sum(grad_out * scaled, axis=0, keepdims=True)
        small[1:2, :] = jnp.sum(grad_out, axis=0, keepdims=True)
        small[2:3, :] = jnp.sum(total, axis=0, keepdims=True)
        small[3:8, :] = jnp.zeros((5, width), jnp.float32)

    return kernel_call(
        body,
        [
            ((n_own, width), jnp.float32),
            ((n_own, width), jnp.bfloat16),
            ((8, width), jnp.float32),
        ],
        (resid, stream, gain, *parts),
    )


def token_tiles(near, far):
    half = near.shape[0]
    for start in range(0, 2 * half, TILE):
        rows = pl.ds(start, TILE)
        if start < half:
            yield rows, near, pl.ds(start, TILE), True
        else:
            yield rows, far, pl.ds(start - half, TILE), False


def attention_forward(near, far, w_qv, w_out, masking):
    half, width = near.shape
    n_tok = 2 * half
    dim = w_out.shape[0]

    def body(near, far, w_qv, w_out, masking, far_part, near_part, qv, prob, mixed, keys):
        for rows, src, local_rows, _ in token_tiles(near, far):
            low = dot_plain(src[local_rows, :], w_qv[...]).astype(jnp.bfloat16)
            qv[rows, :] = low
            query = low[:, :dim].astype(jnp.float32)
            inv = lax.rsqrt(jnp.sum(query * query, axis=-1, keepdims=True) + 1e-06)
            keys[rows, :] = (query * inv).astype(jnp.bfloat16)
        for rows, _, local_rows, is_near in token_tiles(near, far):
            scores = dot_right_t(qv[rows, :dim], keys[...]) + masking[rows, :]
            scores = jnp.exp(scores - jnp.max(scores, axis=-1, keepdims=True))
            total = jnp.sum(scores, axis=-1, keepdims=True)
            low = (scores * (1.0 / total)).astype(jnp.bfloat16)
            prob[rows, :] = low
            mix = dot_plain(low, qv[:, dim:]).astype(jnp.bfloat16)
            mixed[rows, :] = mix
            part = dot_plain(mix, w_out[...])
            if is_near:
                near_part[local_rows, :] = part
            else:
                far_part[local_rows, :] = part.astype(jnp.bfloat16)

    return kernel_call(
        body,
        [
            ((half, width), jnp.bfloat16),
            ((half, width), jnp.float32),
            ((n_tok, 2 * dim), jnp.bfloat16),
            ((n_tok, n_tok), jnp.bfloat16),
            ((n_tok, dim), jnp.bfloat16),
        ],
        (near, far, w_qv, w_out, masking),
        scratch=[pltpu.VMEM((n_tok, dim), jnp.bfloat16)],
        flops=2 * n_tok * (3 * width * dim + 2 * n_tok * dim),
    )


def attention_backward(near, far, w_qv, w_out, qv, prob):
    half, width = near.shape
    n_tok = 2 * half
    dim = w_out.shape[0]

    def body(near, far, w_qv, w_out, qv, prob, far_part, near_part, dqv, keys, dmix, dscore, dquery):
        for rows, src, local_rows, _ in token_tiles(near, far):
            dmix[rows, :] = dot_right_t(src[local_rows, :], w_out[...]).astype(jnp.bfloat16)
            query = qv[rows, :dim].astype(jnp.float32)
            inv = lax.rsqrt(jnp.sum(query * query, axis=-1, keepdims=True) + 1e-06)
            keys[rows, :] = (query * inv).astype(jnp.bfloat16)
        for rows, _, _, _ in token_tiles(near, far):
            dprob = dot_right_t(dmix[rows, :], qv[:, dim:])
            weights = prob[rows, :].astype(jnp.float32)
            centre = jnp.sum(weights * dprob, axis=-1, keepdims=True)
            low = (weights * (dprob - centre)).astype(jnp.bfloat16)
            dscore[rows, :] = low
            dquery[rows, :] = dot_plain(low, keys[...])
        for rows, _, local_rows, is_near in token_tiles(near, far):
            dkey = dot_left_t(dscore[:, rows], qv[:, :dim])
            dval = dot_left_t(prob[:, rows], dmix[...])
            query = qv[rows, :dim].astype(jnp.float32)
            inv = lax.rsqrt(jnp.sum(query * query, axis=-1, keepdims=True) + 1e-06)
            along = jnp.sum(query * dkey, axis=-1, keepdims=True)
            total = dquery[rows, :] + inv * dkey - inv * inv * inv * along * query
            low = jnp.concatenate(
                [total.astype(jnp.bfloat16), dval.astype(jnp.bfloat16)], axis=1
            )
            dqv[rows, :] = low
            part = dot_right_t(low, w_qv[...])
            if is_near:
                near_part[local_rows, :] = part
            else:
                far_part[local_rows, :] = part.astype(jnp.bfloat16)

    return kernel_call(
        body,
        [
            ((half, width), jnp.bfloat16),
            ((half, width), jnp.float32),
            ((n_tok, 2 * dim), jnp.bfloat16),
        ],
        (near, far, w_qv, w_out, qv, prob),
        scratch=[
            pltpu.VMEM((n_tok, dim), jnp.bfloat16),
            pltpu.VMEM((n_tok, dim), jnp.bfloat16),
            pltpu.VMEM((n_tok, n_tok), jnp.bfloat16),
            pltpu.VMEM((n_tok, dim), jnp.float32),
        ],
        flops=2 * n_tok * (3 * width * dim + 4 * n_tok * dim),
    )


def feed_forward(near, far, w_in, b_in, w_back):
    half, width = near.shape
    n_tok = 2 * half
    hidden = w_in.shape[1]

    def body(near, far, w_in, b_in, w_back, far_part, near_part, active, slope):
        for rows, src, local_rows, is_near in token_tiles(near, far):
            pre = dot_plain(src[local_rows, :], w_in[...]) + b_in[...]
            square = pre * pre
            bent = jnp.tanh(GELU_C * (pre + 0.044715 * pre * square))
            low = (0.5 * pre * (1.0 + bent)).astype(jnp.bfloat16)
            active[rows, :] = low
            slope[rows, :] = 0.5 * (1.0 + bent) + 0.5 * pre * (1.0 - bent * bent) * (
                GELU_C * (1.0 + 3.0 * 0.044715 * square)
            )
            part = dot_plain(low, w_back[...])
            if is_near:
                near_part[local_rows, :] = part
            else:
                far_part[local_rows, :] = part.astype(jnp.bfloat16)

    return kernel_call(
        body,
        [
            ((half, width), jnp.bfloat16),
            ((half, width), jnp.float32),
            ((n_tok, hidden), jnp.bfloat16),
            ((n_tok, hidden), jnp.float32),
        ],
        (near, far, w_in, b_in, w_back),
        flops=4 * n_tok * width * hidden,
    )


def feed_backward(near, far, w_in, w_back, slope):
    half, width = near.shape
    n_tok = 2 * half
    hidden = w_in.shape[1]

    def body(near, far, w_in, w_back, slope, far_part, near_part, dpre):
        for rows, src, local_rows, is_near in token_tiles(near, far):
            grad = dot_right_t(src[local_rows, :], w_back[...]) * slope[rows, :]
            low = grad.astype(jnp.bfloat16)
            dpre[rows, :] = low
            part = dot_right_t(low, w_in[...])
            if is_near:
                near_part[local_rows, :] = part
            else:
                far_part[local_rows, :] = part.astype(jnp.bfloat16)

    return kernel_call(
        body,
        [
            ((half, width), jnp.bfloat16),
            ((half, width), jnp.float32),
            ((n_tok, hidden), jnp.bfloat16),
        ],
        (near, far, w_in, w_back, slope),
        flops=4 * n_tok * width * hidden,
    )


def two_part_grad(left, near, far):
    half = near.shape[0]
    return dot_left_t(left[pl.ds(0, half), :], near[...]) + dot_left_t(
        left[pl.ds(half, half), :], far[...]
    )


def grad_pieces(shape):
    return [(shape, jnp.float32)] + [(shape, jnp.bfloat16)] * 3


def feed_grads(place, norm_near, norm_far, grad_near, grad_far, active, dpre):
    half, width = norm_near.shape
    hidden = active.shape[1]
    in_rows, back_rows = width // 4, hidden // 4

    def body(place, norm_near, norm_far, grad_near, grad_far, active, dpre, *outs):
        for k in range(4):
            chunk = place[0] ^ k
            cols = pl.ds(pl.multiple_of(chunk * in_rows, in_rows), in_rows)
            out = outs[k]
            out[...] = (
                dot_left_t(norm_near[:, cols], dpre[pl.ds(0, half), :])
                + dot_left_t(norm_far[:, cols], dpre[pl.ds(half, half), :])
            ).astype(out.dtype)
            cols = pl.ds(pl.multiple_of(chunk * back_rows, back_rows), back_rows)
            out = outs[4 + k]
            out[...] = (
                dot_left_t(active[pl.ds(0, half), cols], grad_near[...])
                + dot_left_t(active[pl.ds(half, half), cols], grad_far[...])
            ).astype(out.dtype)
        outs[8][...] = jnp.sum(dpre[...].astype(jnp.float32), axis=0, keepdims=True)

    outs = kernel_call(
        body,
        grad_pieces((in_rows, hidden)) + grad_pieces((back_rows, width)) + [((1, hidden), jnp.float32)],
        (norm_near, norm_far, grad_near, grad_far, active, dpre),
        scalars=place,
        flops=8 * half * width * hidden,
    )
    return outs[:4], outs[4:8], outs[8]


def attention_grads(place, norm_near, norm_far, grad_near, grad_far, mixed, dqv):
    half, width = norm_near.shape
    dim = mixed.shape[1]
    qv_rows, out_rows = width // 4, dim // 4

    def body(place, norm_near, norm_far, grad_near, grad_far, mixed, dqv, *outs):
        whole = outs[8]
        whole[...] = dot_left_t(mixed[pl.ds(0, half), :], grad_near[...]) + dot_left_t(
            mixed[pl.ds(half, half), :], grad_far[...]
        )
        for k in range(4):
            chunk = place[0] ^ k
            cols = pl.ds(pl.multiple_of(chunk * qv_rows, qv_rows), qv_rows)
            out = outs[k]
            out[...] = (
                dot_left_t(norm_near[:, cols], dqv[pl.ds(0, half), :])
                + dot_left_t(norm_far[:, cols], dqv[pl.ds(half, half), :])
            ).astype(out.dtype)
            rows = pl.ds(pl.multiple_of(chunk * out_rows, out_rows), out_rows)
            out = outs[4 + k]
            out[...] = whole[rows, :].astype(out.dtype)

    outs = kernel_call(
        body,
        grad_pieces((qv_rows, 2 * dim)) + grad_pieces((out_rows, width)),
        (norm_near, norm_far, grad_near, grad_far, mixed, dqv),
        scalars=place,
        scratch=[pltpu.VMEM((dim, width), jnp.float32)],
        flops=4 * half * width * 3 * dim,
    )
    return outs[:4], outs[4:8]


def reduce_grads(place, layer, first_pieces, second_pieces, join_first, join_second):
    first = [first_pieces[0]] + xor_recv(first_pieces[1:], "rows")
    second = [second_pieces[0]] + xor_recv(second_pieces[1:], "rows")

    def add_body(*refs):
        refs[8][...] = sum_parts(refs[0:4]).astype(jnp.bfloat16)
        refs[9][...] = sum_parts(refs[4:8]).astype(jnp.bfloat16)

    sums = kernel_call(
        add_body,
        [(first[0].shape, jnp.bfloat16), (second[0].shape, jnp.bfloat16)],
        (*first, *second),
    )
    others = [lax.ppermute(part, "section", [(1 - layer, layer)]) for part in sums]
    joined_types = []
    for part, join in ((sums[0], join_first), (sums[1], join_second)):
        rows, cols = part.shape
        joined_types.append(((rows, 2 * cols) if join == "cols" else (2, rows, cols), jnp.bfloat16))

    def join_body(own_a, own_b, other_a, other_b, out_a, out_b):
        for own, other, out, join in (
            (own_a, other_a, out_a, join_first),
            (own_b, other_b, out_b, join_second),
        ):
            halves = (own[...], other[...]) if layer == 0 else (other[...], own[...])
            if join == "cols":
                cols = own.shape[1]
                out[:, :cols] = halves[0]
                out[:, cols:] = halves[1]
            else:
                out[0] = halves[0]
                out[1] = halves[1]

    joined = kernel_call(join_body, joined_types, (*sums, *others))
    pieces = []
    for part in joined:
        got = [part]
        for k in (1, 2, 3):
            pairs = [(layer * 4 + i, layer * 4 + (i ^ k)) for i in range(4)]
            got.append(lax.ppermute(part, ("section", "rows"), pairs))
        pieces.append(got)
    return pieces


def place_pieces(place, low_layer, high_layer, out_types, store):
    def body(place, *refs):
        for k in range(4):
            value = jnp.where(
                place[1] == 0,
                refs[k][...].astype(jnp.float32),
                refs[4 + k][...].astype(jnp.float32),
            )
            store(refs[8:], place[0] ^ k, value)

    return kernel_call(body, out_types, (*low_layer, *high_layer), scalars=place)


def all_devices_sum(value):
    for axis in ("rows", "head"):
        value = value + sum(xor_recv([value] * 3, axis))
    return value + swap_cores(value)


def device_pairs(link):
    pairs = []
    for core in range(2):
        for col in range(4):
            for row in range(4):
                there = link(core, col, row)
                if there is not None:
                    pairs.append(((core * 4 + col) * 4 + row, (there[0] * 4 + there[1]) * 4 + there[2]))
    return pairs


def everywhere(x, link):
    return lax.ppermute(x, ("section", "head", "rows"), device_pairs(link))


def to_own_tokens(stream, coords):
    micro_n, tok_rows, feats = stream.shape
    half = tok_rows // 2

    def body(coords, stream, *outs):
        for t in range(2):
            for m in range(4):
                rows = pl.ds(pl.multiple_of((coords[0] ^ t) * half, half), half)
                outs[4 * t + m][...] = stream[coords[1] ^ m, rows, :]

    sent = kernel_call(body, [((half, feats), stream.dtype)] * 8, (stream,), scalars=coords)

    def link(t, m):
        return lambda core, col, row: (row // 2, 2 * (row % 2) + (core ^ t), col ^ m)

    return [everywhere(sent[4 * t + m], link(t, m)) for t in range(2) for m in range(4)]


def own_rows(pieces, coords, norm=None):
    half, feats = pieces[0].shape
    width = 4 * feats
    gain_args = () if norm is None else norm

    def body(coords, *refs):
        got = refs[:8]
        outs = refs[8 + len(gain_args) :]
        flipped = (coords[2] & 1) == 1
        for c in range(4):
            from_low = jnp.zeros((half, feats), jnp.float32)
            from_high = from_low
            for m in range(4):
                here = (coords[3] ^ m) == c
                even = got[m][...].astype(jnp.float32)
                odd = got[4 + m][...].astype(jnp.float32)
                from_low = jnp.where(here, jnp.where(flipped, odd, even), from_low)
                from_high = jnp.where(here, jnp.where(flipped, even, odd), from_high)
            outs[0][:, c * feats : (c + 1) * feats] = from_low
            outs[1][:, c * feats : (c + 1) * feats] = from_high
        if norm is not None:
            scaled, _ = rows_norm(outs[0][...])
            outs[2][...] = (scaled * refs[8][...] + refs[9][...]).astype(jnp.bfloat16)
            outs[3][...] = outs[1][...].astype(jnp.bfloat16)
            outs[4][...] = jnp.zeros((8, width), jnp.float32)
            outs[4][2:3, :] = jnp.sum(outs[1][...], axis=0, keepdims=True)

    types = [((half, width), jnp.float32)] * 2
    if norm is not None:
        types = types + [((half, width), jnp.bfloat16)] * 2 + [((8, width), jnp.float32)]
    return kernel_call(body, types, (*pieces, *gain_args), scalars=coords)


def from_own_tokens(values, coords, section):
    half, width = values[0].shape
    feats = width // 4
    n_val = len(values)

    def body(coords, *refs):
        for m in range(4):
            cols = pl.ds(pl.multiple_of((coords[3] ^ m) * feats, feats), feats)
            for i in range(n_val):
                refs[n_val + m][i] = refs[i][:, cols]

    sent = kernel_call(body, [((n_val, half, feats), jnp.float32)] * 4, values, scalars=coords)

    def link(side, m):
        return lambda core, col, row: (
            (section, row ^ m, 2 * core + col // 2) if col % 2 == side else None
        )

    return [everywhere(sent[m], link(side, m)) for side in range(2) for m in range(4)]


def stream_result(later, first_grad, second_grad, coords, micro_n):
    _, half, feats = later[0].shape

    def body(coords, *refs):
        out = refs[24]
        for side in range(2):
            for m in range(4):
                i = 4 * side + m
                rows = pl.ds(side * half, half)
                batch = coords[1] ^ m
                is_low = coords[0] == 0
                out[0, batch, rows, :] = jnp.where(is_low, refs[8 + i][0], refs[i][0])
                out[1, batch, rows, :] = jnp.where(is_low, refs[16 + i][0], refs[i][1])

    return kernel_call(
        body,
        [((2, micro_n, 2 * half, feats), jnp.float32)],
        (*later, *first_grad, *second_grad),
        scalars=coords,
    )[0]


def flip_if(x, axis, flag):
    return jnp.where(flag == 1, jnp.flip(x, axis), x)


def score_masking(seq_ids, bucket_ids, core, col, row):
    rounds_n, tok_rows = bucket_ids.shape[1:]
    n_tok = 4 * tok_rows
    half = tok_rows // 2
    n_blocks = n_tok // BLOCK
    ints = jnp.concatenate([seq_ids[:, None], bucket_ids], axis=1)

    def batch(k):
        return lax.dynamic_index_in_dim(ints, row ^ k, 0, keepdims=False)

    pieces = [batch(0)] + xor_recv([batch(k) for k in (1, 2, 3)], "rows")
    table = jnp.stack(pieces).reshape(2, 2, rounds_n + 1, 2, half)
    table = flip_if(table, 0, core ^ (row >> 1))
    table = flip_if(table, 1, (row & 1) ^ (col >> 1))
    table = flip_if(table, 3, col & 1)
    table = jnp.transpose(table, (2, 0, 1, 3, 4)).reshape(rounds_n + 1, n_tok)
    index = jnp.arange(8, dtype=jnp.int32)
    block = 4 * (core ^ (index // 4)) + (col ^ (index % 4))
    position = (block[:, None] * half + jnp.arange(half, dtype=jnp.int32)).reshape(1, n_tok)
    keys = table[:1] * 1024 + table[1:]
    codes = keys * n_tok + position
    both = jnp.concatenate([codes, keys], axis=0).astype(jnp.float32)

    def body(by_lane, by_row, masking):
        for start in range(0, n_tok, TILE):
            masking[pl.ds(start, TILE), :] = jnp.zeros((TILE, n_tok), jnp.float32)
        for r in range(rounds_n):
            lane_code = by_lane[r : r + 1, :]
            lane_key = by_lane[rounds_n + r : rounds_n + r + 1, :]
            behind = jnp.zeros((1, n_tok), jnp.float32)
            for start in range(0, n_tok, TILE):
                rows = pl.ds(start, TILE)
                less = (lane_code < by_row[rows, r : r + 1]).astype(jnp.float32)
                behind = behind + jnp.sum(less, axis=0, keepdims=True)
            lane_block = jnp.floor((n_tok - 1.0 - behind) * (1.0 / BLOCK))
            lane_place = lane_key * (2.0 * n_blocks) + lane_block
            for start in range(0, n_tok, TILE):
                rows = pl.ds(start, TILE)
                less = lane_code < by_row[rows, r : r + 1]
                rank = jnp.sum(less.astype(jnp.float32), axis=1, keepdims=True)
                row_place = by_row[rows, rounds_n + r : rounds_n + r + 1] * (
                    2.0 * n_blocks
                ) + jnp.floor(rank * (1.0 / BLOCK))
                seen = less & (row_place - lane_place < 1.5)
                masking[rows, :] += seen.astype(jnp.float32)
        for start in range(0, n_tok, TILE):
            rows = pl.ds(start, TILE)
            count = masking[rows, :]
            itself = by_lane[0:1, :] == by_row[rows, 0:1]
            other = jnp.where(itself, -100000.0, -1000000000.0)
            masking[rows, :] = jnp.where(count > 0.5, jnp.log(jnp.maximum(count, 1.0)), other)

    return kernel_call(
        body, [((n_tok, n_tok), jnp.float32)], (both, jnp.transpose(both))
    )[0]


def cut_half(weight, which, dim):
    size = weight.shape[dim] // 2
    return lax.dynamic_slice_in_dim(weight, which * size, size, dim)


def parallel_local(
    stream_in,
    attn_gain,
    attn_shift,
    w_qk,
    w_value,
    w_out,
    ffn_gain,
    ffn_shift,
    w_in,
    b_in,
    w_back,
    b_back,
    seq_ids,
    bucket_ids,
    sort_order,
):
    core = lax.axis_index("section")
    col = lax.axis_index("head")
    row = lax.axis_index("rows")
    micro_n = stream_in.shape[2]
    width = attn_gain.shape[1]
    coords = jnp.stack([core, col, col, row]).astype(jnp.int32)
    place = jnp.stack([row, core]).astype(jnp.int32)
    is_first = core == 0

    second_pieces = to_own_tokens(stream_in[0, 1], coords)

    def halves(which):
        return (
            jnp.concatenate([cut_half(w_qk[0], which, 1), cut_half(w_value[0], which, 1)], axis=1),
            cut_half(w_out[0], which, 0),
            cut_half(w_in[0], which, 1),
            cut_half(w_back[0], which, 0),
        )

    vectors = jnp.concatenate([attn_gain, attn_shift, ffn_gain, ffn_shift], axis=0)
    mine = halves(core)
    other = [swap_cores(part) for part in halves(1 - core)]
    vectors_other = swap_cores(vectors)
    bias_other = swap_cores(cut_half(b_in, 1 - core, 1))
    bias_mine = cut_half(b_in, core, 1)

    back_parts = [b_back] + xor_recv([b_back] * 3, "head")
    back_own = jnp.stack(back_parts).reshape(2, 2, -1)
    back_own = flip_if(flip_if(back_own, 0, col >> 1), 1, col & 1).reshape(1, width)
    back_other = swap_cores(back_own)

    def by_layer(own, got):
        return (jnp.where(is_first, own, got), jnp.where(is_first, got, own))

    weights = [by_layer(own, got) for own, got in zip(mine, other)]
    norms = by_layer(vectors, vectors_other)
    biases_in = by_layer(bias_mine, bias_other)
    biases_back = by_layer(back_own, back_other)

    def weight(index, layer):
        return weights[index][layer]

    def vector(index, layer):
        return norms[layer][index : index + 1]

    masking = score_masking(seq_ids, bucket_ids, core, col, row)
    second, grad_second, low, grad_low, small_back = own_rows(
        second_pieces, coords, norm=(vector(0, 0), vector(1, 0))
    )
    first_pieces = to_own_tokens(stream_in[0, 0], coords)
    first, grad_first = own_rows(first_pieces, coords)
    zero_shift = jnp.zeros((1, width), jnp.float32)

    kept = []
    for layer in range(2):
        attn_in = gather_tokens(low, "head")
        far_part, near_part, qv, prob, mixed = attention_forward(
            *attn_in, weight(0, layer), weight(1, layer), masking
        )
        parts = scatter_tokens(far_part, near_part, "head")
        attn_stream = second
        first, low = residual_norm(first, parts, zero_shift, vector(2, layer), vector(3, layer))
        ffn_in = gather_tokens(low, "head")
        far_part, near_part, active, slope = feed_forward(
            *ffn_in, weight(2, layer), biases_in[layer], weight(3, layer)
        )
        parts = scatter_tokens(far_part, near_part, "head")
        kept.append((attn_in, qv, prob, mixed, attn_stream, ffn_in, active, slope, first))
        if layer == 0:
            second, low = residual_norm(
                second, parts, biases_back[layer], vector(0, 1), vector(1, 1)
            )
        else:
            second = residual_only(second, parts, biases_back[layer])
    later = from_own_tokens((first, second), coords, 1)

    feed_sums, attn_sums, feed_small, attn_small = [None] * 2, [None] * 2, [None] * 2, [None] * 2
    for layer in (1, 0):
        attn_in, qv, prob, mixed, attn_stream, ffn_in, active, slope, ffn_stream = kept[layer]
        grad_in = gather_tokens(grad_low, "head")
        far_part, near_part, dpre = feed_backward(
            *grad_in, weight(2, layer), weight(3, layer), slope
        )
        parts = scatter_tokens(far_part, near_part, "head")
        in_pieces, back_pieces, bias_grad = feed_grads(
            place, *ffn_in, *grad_in, active, dpre
        )
        feed_sums[layer] = reduce_grads(place, layer, in_pieces, back_pieces, "cols", "rows")
        grad_first, grad_low, small = norm_backward(
            grad_first, parts, ffn_stream, vector(2, layer)
        )
        small = small.at[2:3].set(small_back[2:3])
        feed_small[layer] = all_devices_sum(small)
        bias_rows = bias_grad + sum(xor_recv([bias_grad] * 3, "rows"))
        bias_there = swap_cores(bias_rows)
        bias_rows = jnp.where(
            is_first,
            jnp.concatenate([bias_rows, bias_there], axis=1),
            jnp.concatenate([bias_there, bias_rows], axis=1),
        )
        grad_out = gather_tokens(grad_low, "head")
        far_part, near_part, dqv = attention_backward(
            *grad_out, weight(0, layer), weight(1, layer), qv, prob
        )
        parts = scatter_tokens(far_part, near_part, "head")
        qv_pieces, out_pieces = attention_grads(place, *attn_in, *grad_out, mixed, dqv)
        attn_sums[layer] = reduce_grads(place, layer, qv_pieces, out_pieces, "cols", "rows")
        grad_second, grad_low, small_back = norm_backward(
            grad_second, parts, attn_stream, vector(0, layer)
        )
        attn_small[layer] = all_devices_sum(small_back[:2])
        feed_small[layer] = (feed_small[layer], bias_rows)
        if layer == 0:
            first_done = from_own_tokens((grad_first,), coords, 0)
            second_done = from_own_tokens((grad_second,), coords, 0)

    stream_out = stream_result(later, first_done, second_done, coords, micro_n)
    dim = w_qk.shape[2] // 2
    hidden = w_in.shape[2] // 2

    def store_in(outs, chunk, value):
        rows = value.shape[0]
        outs[0][pl.ds(pl.multiple_of(chunk * rows, rows), rows), :] = value

    def store_back(outs, chunk, value):
        rows = value.shape[1]
        for i in range(2):
            outs[0][i, pl.ds(pl.multiple_of(chunk * rows, rows), rows), :] = value[i]

    def store_qv(outs, chunk, value):
        rows = value.shape[0]
        there = pl.ds(pl.multiple_of(chunk * rows, rows), rows)
        for i in range(2):
            outs[0][there, i * dim : (i + 1) * dim] = value[:, 2 * i * dim : (2 * i + 1) * dim]
            outs[1][there, i * dim : (i + 1) * dim] = value[:, (2 * i + 1) * dim : (2 * i + 2) * dim]

    f32 = jnp.float32
    (grad_w_in,) = place_pieces(
        place, feed_sums[0][0], feed_sums[1][0], [((width, 2 * hidden), f32)], store_in
    )
    (grad_w_back,) = place_pieces(
        place, feed_sums[0][1], feed_sums[1][1], [((2, hidden, width), f32)], store_back
    )
    grad_w_qk, grad_w_value = place_pieces(
        place, attn_sums[0][0], attn_sums[1][0], [((width, 2 * dim), f32)] * 2, store_qv
    )
    (grad_w_out,) = place_pieces(
        place, attn_sums[0][1], attn_sums[1][1], [((2, dim, width), f32)], store_back
    )
    attn_vec = jnp.where(is_first, attn_small[0], attn_small[1])
    feed_vec = jnp.where(is_first, feed_small[0][0], feed_small[1][0])
    bias_vec = jnp.where(is_first, feed_small[0][1], feed_small[1][1])
    back_vec = own_columns(feed_vec[2:3], b_back.shape[1])
    return (
        stream_out[None],
        attn_vec[0:1],
        attn_vec[1:2],
        grad_w_qk[None],
        grad_w_value[None],
        grad_w_out.reshape(1, 2 * dim, width),
        feed_vec[0:1],
        feed_vec[1:2],
        grad_w_in[None],
        bias_vec,
        grad_w_back.reshape(1, 2 * hidden, width),
        back_vec,
    )


def solution(mesh):
    placed = (
        P("section", None, None, "rows", "head"),
        P("section", None),
        P("section", None),
        P("section", None, "head"),
        P("section", None, "head"),
        P("section", "head", None),
        P("section", None),
        P("section", None),
        P("section", None, "head"),
        P("section", "head"),
        P("section", "head", None),
        P("section", "head"),
        P(None, "rows"),
        P(None, None, "rows"),
        P(None, None, "rows"),
    )
    sizes = mesh.shape
    grid_fits = (sizes["section"], sizes["head"], sizes["rows"]) == (2, 4, 4)
    return jax.shard_map(
        parallel_local if grid_fits else local,
        mesh=mesh,
        in_specs=placed,
        out_specs=(
            P("section", None, None, "rows", "head"),
            P("section", None),
            P("section", None),
            P("section", None, "head"),
            P("section", None, "head"),
            P("section", "head", None),
            P("section", None),
            P("section", None),
            P("section", None, "head"),
            P("section", "head"),
            P("section", "head", None),
            P("section", "head"),
        ),
        check_vma=False,
    )
```

```python
import functools

import jax
import jax.numpy as jnp
from jax import lax
from jax.experimental import pallas as pl
from jax.experimental.pallas import tpu as pltpu
from jax.sharding import PartitionSpec as P

HDIM = 128
BLOCK = 64


def from_behind(x, axis, by):
    length = lax.axis_size(axis)
    pairs = [(i, i + by) for i in range(length) if 0 <= i + by < length]
    return lax.ppermute(x, axis, pairs)


def shortened(x):

    def short(part):
        return part.astype(jnp.bfloat16) if part.dtype == jnp.float32 else part

    return jax.tree.map(short, x)


def dot_plain(left_op, right_op):
    return jnp.dot(left_op, right_op, preferred_element_type=jnp.float32)


def dot_right_t(left_op, right_op):
    return lax.dot_general(
        left_op, right_op, (((1,), (1,)), ((), ())), preferred_element_type=jnp.float32
    )


def dot_left_t(left_op, right_op):
    return lax.dot_general(
        left_op, right_op, (((0,), (0,)), ((), ())), preferred_element_type=jnp.float32
    )


def norm_parts(rows_in, norm_gain, norm_shift):
    centre = jnp.mean(rows_in, axis=-1, keepdims=True)
    centred = rows_in - centre
    inv_std = lax.rsqrt(jnp.mean(centred * centred, axis=-1, keepdims=True) + 1e-05)
    scaled = centred * inv_std
    return (scaled * norm_gain + norm_shift, scaled, inv_std)


def norm_back(grad_out, scaled, inv_std, norm_gain):
    grad_scaled = grad_out * norm_gain
    centred_grad = grad_scaled - jnp.mean(grad_scaled, axis=-1, keepdims=True)
    centred_grad = centred_grad - scaled * jnp.mean(grad_scaled * scaled, axis=-1, keepdims=True)
    return (inv_std * centred_grad, jnp.sum(grad_out * scaled, axis=0), jnp.sum(grad_out, axis=0))


def own_columns(full_rows, col_width):
    return lax.dynamic_slice_in_dim(full_rows, lax.axis_index("head") * col_width, col_width, 1)


def full_features(local_rows):
    return lax.all_gather(local_rows, "head", axis=1, tiled=True)


def head_reduce(partial_rows):
    return lax.psum_scatter(partial_rows, "head", scatter_dimension=1, tiled=True)


def grad_features(local_grad):
    return lax.all_gather(local_grad.astype(jnp.bfloat16), "head", axis=1, tiled=True)


def grad_reduce(partial_grad):
    return lax.psum(partial_grad, "head")


def slot_table(slot_ids, seq_rows):
    return (slot_ids[..., None] == jnp.arange(seq_rows, dtype=jnp.int32)).astype(jnp.float32)


def span_blocks(extended, n_blocks):
    blocks = extended.reshape((extended.shape[0], n_blocks + 1, BLOCK) + extended.shape[2:])
    return jnp.concatenate([blocks[:, :-1], blocks[:, 1:]], axis=2)


def fold_blocks(windows):
    front_half = windows[:, :, :BLOCK]
    back_half = windows[:, :, BLOCK:]
    zero_blk = jnp.zeros_like(front_half[:, :1])
    folded = jnp.concatenate([front_half, zero_blk], axis=1) + jnp.concatenate(
        [zero_blk, back_half], axis=1
    )
    return folded.reshape((folded.shape[0], -1) + folded.shape[3:])


def window_scores(gathered, slots, live_prev):
    qv_all, seq_all, bucket_all = gathered
    rounds_n, extended = slots.shape
    n_blocks = extended // BLOCK - 1
    half_width = qv_all.shape[1] // 2
    heads_here = half_width // HDIM
    picked = qv_all[slots]
    query_ext = picked[..., :half_width].reshape(rounds_n, extended, heads_here, HDIM)
    value_ext = picked[..., half_width:].reshape(rounds_n, extended, heads_here, HDIM)
    query_wide = query_ext.astype(jnp.float32)
    inv_norm = lax.rsqrt(jnp.sum(query_wide * query_wide, axis=-1, keepdims=True) + 1e-06)
    key_win = span_blocks((query_wide * inv_norm).astype(jnp.bfloat16), n_blocks)
    value_win = span_blocks(value_ext, n_blocks)
    query_blocks = query_ext[:, BLOCK:].reshape(rounds_n, n_blocks, BLOCK, heads_here, HDIM)
    seq_ext = seq_all[slots]
    bucket_ext = jnp.take_along_axis(bucket_all, slots, axis=1)
    live_ext = jnp.concatenate(
        [
            jnp.broadcast_to(live_prev, (rounds_n, BLOCK)),
            jnp.ones((rounds_n, extended - BLOCK), jnp.bool_),
        ],
        axis=1,
    )

    def query_part(int_table):
        return int_table[:, BLOCK:].reshape(rounds_n, n_blocks, BLOCK)[..., None]

    def key_part(int_table):
        return span_blocks(int_table, n_blocks)[:, :, None, :]

    same_group = key_part(live_ext) & (key_part(seq_ext) == query_part(seq_ext))
    same_group = same_group & (key_part(bucket_ext) == query_part(bucket_ext))
    allowed = same_group & (key_part(slots) < query_part(slots))
    itself = key_part(live_ext) & (key_part(slots) == query_part(slots))
    masking = jnp.where(allowed, 0.0, jnp.where(itself, -100000.0, -1000000000.0)).astype(
        jnp.float32
    )
    scores = jnp.einsum(
        "rcqhd,rckhd->rchqk", query_blocks, key_win, preferred_element_type=jnp.float32
    )
    scores = scores + masking[:, :, None]
    highest = jnp.max(scores, axis=-1, keepdims=True)
    log_total = highest + jnp.log(jnp.sum(jnp.exp(scores - highest), axis=-1, keepdims=True))
    attn_prob = jnp.exp(scores - log_total)
    return (query_wide, inv_norm, query_blocks, key_win, value_win, attn_prob, log_total)


def sorted_forward(gathered, slots, live_prev):
    query_wide, inv_norm, query_blocks, key_win, value_win, attn_prob, log_total = window_scores(
        gathered, slots, live_prev
    )
    rounds_n = slots.shape[0]
    round_mix = jnp.einsum(
        "rchqk,rckhd->rcqhd",
        attn_prob.astype(jnp.bfloat16),
        value_win,
        preferred_element_type=jnp.float32,
    )
    results = round_mix.reshape(rounds_n, -1, round_mix.shape[3] * HDIM)
    round_stats = jnp.transpose(log_total[..., 0], (0, 1, 3, 2)).reshape(
        rounds_n, results.shape[1], -1
    )
    return (results, round_stats)


def to_owners(results, round_stats, own_slots, rows_n):
    rounds_n, tok_rows, feat_width = results.shape
    seq_rows = rows_n * tok_rows
    placing = slot_table(own_slots, seq_rows)
    joined = jnp.concatenate([results, round_stats], axis=-1)
    spread_all = jnp.einsum("rsp,rsf->rpf", placing, joined, precision=lax.Precision.HIGHEST)
    spread_out = spread_all[..., :feat_width]
    spread_stats = spread_all[..., feat_width:]
    back_out, back_stats = (
        lax.all_to_all(
            spread_out.reshape(rounds_n, rows_n, tok_rows, feat_width),
            "rows",
            split_axis=1,
            concat_axis=1,
            tiled=True,
        ),
        lax.all_to_all(
            spread_stats.reshape(rounds_n, rows_n, tok_rows, -1),
            "rows",
            split_axis=1,
            concat_axis=1,
            tiled=True,
        ),
    )
    return (jnp.sum(back_out, axis=1), jnp.sum(back_stats, axis=1))


def sorted_backward(gathered, slots, live_prev, received):
    query_wide, inv_norm, query_blocks, key_win, value_win, attn_prob, log_total = window_scores(
        gathered, slots, live_prev
    )
    grad_all, share_all, stat_all = received
    own_slots = slots[:, BLOCK:]
    rounds_n, n_blocks, heads_here = (attn_prob.shape[0], attn_prob.shape[1], attn_prob.shape[2])
    grad_pick = grad_all[own_slots].reshape(rounds_n, n_blocks, BLOCK, heads_here, HDIM)
    share_pick = jnp.take_along_axis(share_all, own_slots[..., None], axis=1).reshape(
        rounds_n, n_blocks, BLOCK, heads_here
    )
    stat_pick = jnp.take_along_axis(stat_all, own_slots[..., None], axis=1).reshape(
        rounds_n, n_blocks, BLOCK, heads_here
    )
    grad_round = (share_pick[..., None] * grad_pick).astype(jnp.bfloat16)
    grad_prob = jnp.einsum(
        "rcqhd,rckhd->rchqk", grad_round, value_win, preferred_element_type=jnp.float32
    )
    row_dot = jnp.sum(attn_prob * grad_prob, axis=-1, keepdims=True)
    stat_term = jnp.transpose(stat_pick, (0, 1, 3, 2))[..., None]
    grad_scores = (attn_prob * (grad_prob - row_dot + stat_term)).astype(jnp.bfloat16)
    grad_query = jnp.einsum(
        "rchqk,rckhd->rcqhd", grad_scores, key_win, preferred_element_type=jnp.float32
    )
    grad_key = fold_blocks(
        jnp.einsum(
            "rchqk,rcqhd->rckhd", grad_scores, query_blocks, preferred_element_type=jnp.float32
        )
    )
    grad_value = fold_blocks(
        jnp.einsum(
            "rchqk,rcqhd->rckhd",
            attn_prob.astype(jnp.bfloat16),
            grad_round,
            preferred_element_type=jnp.float32,
        )
    )
    norm_cubed = inv_norm * inv_norm * inv_norm
    grad_query_ext = (
        inv_norm * grad_key
        - norm_cubed * jnp.sum(query_wide * grad_key, axis=-1, keepdims=True) * query_wide
    )
    grad_query_own = grad_query.reshape(rounds_n, n_blocks * BLOCK, heads_here, HDIM)
    grad_query_ext = grad_query_ext + jnp.pad(grad_query_own, ((0, 0), (BLOCK, 0), (0, 0), (0, 0)))
    extended = slots.shape[1]
    stacked = jnp.concatenate(
        [
            grad_query_ext.reshape(rounds_n, extended, -1),
            grad_value.reshape(rounds_n, extended, -1),
        ],
        axis=-1,
    )
    placing = slot_table(slots, share_all.shape[1])
    buffer = jnp.einsum("rep,ref->pf", placing, stacked, precision=lax.Precision.HIGHEST)
    return lax.psum_scatter(buffer, "rows", scatter_dimension=0, tiled=True)


def attention_inputs(second_in, params):
    normed, scaled, inv_std = norm_parts(full_features(second_in), params[0], params[1])
    low_in = normed.astype(jnp.bfloat16)
    qv_pairs = jnp.concatenate(
        [dot_plain(low_in, params[2]), dot_plain(low_in, params[3])], axis=1
    ).astype(jnp.bfloat16)
    return (low_in, scaled, inv_std, qv_pairs)


def attention_rounds(qv_pairs, int_here, live_prev, rows_n):
    seq_here, bucket_here, order_here, prev_here = int_here
    gathered = (
        lax.all_gather(qv_pairs, "rows", axis=0, tiled=True),
        lax.all_gather(seq_here, "rows", axis=0, tiled=True),
        lax.all_gather(bucket_here, "rows", axis=1, tiled=True),
    )
    slots = jnp.concatenate([prev_here, order_here], axis=1)
    results, round_stats = sorted_forward(gathered, slots, live_prev)
    owned_out, owned_stats = to_owners(results, round_stats, order_here, rows_n)
    return (gathered, owned_out, owned_stats)


def combine_rounds(owned_out, owned_stats):
    rounds_n, tok_rows, feat_width = owned_out.shape
    heads_here = owned_stats.shape[2]
    top_stat = jnp.max(owned_stats, axis=0, keepdims=True)
    shares = jnp.exp(owned_stats - top_stat)
    shares = shares / jnp.sum(shares, axis=0, keepdims=True)
    mixed_out = jnp.sum(
        shares[..., None] * owned_out.reshape(rounds_n, tok_rows, heads_here, HDIM), axis=0
    )
    return (mixed_out.reshape(tok_rows, feat_width).astype(jnp.bfloat16), shares)


def ffn_forward(first_out, params):
    normed, scaled, inv_std = norm_parts(full_features(first_out), params[5], params[6])
    low_in = normed.astype(jnp.bfloat16)
    pre_act = dot_plain(low_in, params[7]) + params[8]
    active = jax.nn.gelu(pre_act).astype(jnp.bfloat16)
    branch = head_reduce(dot_plain(active, params[9])) + params[10]
    return (branch, (low_in, scaled, inv_std, pre_act, active))


def layer_forward(first_in, second_in, params, int_here, live_prev, rows_n):
    low_in, scaled, inv_std, qv_pairs = attention_inputs(second_in, params)
    kept_state = attention_rounds(qv_pairs, int_here, live_prev, rows_n)
    mixed_low, shares = combine_rounds(kept_state[1], kept_state[2])
    first_out = first_in + head_reduce(dot_plain(mixed_low, params[4]))
    second_out = second_in + ffn_forward(first_out, params)[0]
    return (first_out, second_out, kept_state)


def layer_backward(first_out, second_out, grad_one, grad_two, params, int_here, live_prev, rows_n):
    ffn_branch, (ffn_low, ffn_scaled, ffn_inv, pre_act, active) = ffn_forward(first_out, params)
    second_in = second_out - ffn_branch
    grad_full = grad_features(grad_two)
    gelu_value, gelu_pull = jax.vjp(jax.nn.gelu, pre_act)
    grad_pre = gelu_pull(dot_right_t(grad_full, params[9]))[0].astype(jnp.bfloat16)
    grad_w_back = dot_left_t(active, grad_full)
    grad_b_back = jnp.sum(grad_two, axis=0)
    grad_w_in = dot_left_t(ffn_low, grad_pre)
    grad_b_in = jnp.sum(grad_pre.astype(jnp.float32), axis=0)
    grad_normed = grad_reduce(dot_right_t(grad_pre, params[7]))
    grad_rows, grad_ffn_gain, grad_ffn_shift = norm_back(
        grad_normed, ffn_scaled, ffn_inv, params[5]
    )
    grad_one = grad_one + own_columns(grad_rows, grad_one.shape[1])
    low_in, scaled, inv_std, qv_pairs = attention_inputs(second_in, params)
    state_here = attention_rounds(qv_pairs, int_here, live_prev, rows_n)
    gathered, owned_out, owned_stats = state_here
    mixed_low, shares = combine_rounds(owned_out, owned_stats)
    first_in = first_out - head_reduce(dot_plain(mixed_low, params[4]))
    grad_full = grad_features(grad_one)
    grad_w_out = dot_left_t(mixed_low, grad_full)
    grad_mixed = dot_right_t(grad_full, params[4]).astype(jnp.bfloat16)
    rounds_n, tok_rows, heads_here = owned_stats.shape
    grad_wide = grad_mixed.astype(jnp.float32)
    per_round = jnp.sum(
        grad_wide.reshape(1, tok_rows, heads_here, HDIM)
        * owned_out.reshape(rounds_n, tok_rows, heads_here, HDIM),
        axis=-1,
    )
    grad_stats = shares * (per_round - jnp.sum(shares * per_round, axis=0, keepdims=True))
    received = (
        lax.all_gather(grad_wide, "rows", axis=0, tiled=True),
        lax.all_gather(shares, "rows", axis=1, tiled=True),
        lax.all_gather(grad_stats, "rows", axis=1, tiled=True),
    )
    slots = jnp.concatenate([int_here[3], int_here[2]], axis=1)
    owned_grad = sorted_backward(gathered, slots, live_prev, received)
    qk_width = grad_mixed.shape[1]
    grad_query = owned_grad[:, :qk_width].astype(jnp.bfloat16)
    grad_value = owned_grad[:, qk_width:].astype(jnp.bfloat16)
    grad_w_qk = dot_left_t(low_in, grad_query)
    grad_w_value = dot_left_t(low_in, grad_value)
    grad_normed = grad_reduce(
        dot_right_t(grad_query, params[2]) + dot_right_t(grad_value, params[3])
    )
    grad_rows, grad_attn_gain, grad_attn_shift = norm_back(grad_normed, scaled, inv_std, params[0])
    grad_second = grad_two + own_columns(grad_rows, grad_two.shape[1])
    grads = (
        grad_attn_gain,
        grad_attn_shift,
        grad_w_qk,
        grad_w_value,
        grad_w_out,
        grad_ffn_gain,
        grad_ffn_shift,
        grad_w_in,
        grad_b_in,
        grad_w_back,
        grad_b_back,
    )
    return (first_in, second_in, grad_one, grad_second, grads)


def local(
    stream_in,
    attn_gain,
    attn_shift,
    w_qk,
    w_value,
    w_out,
    ffn_gain,
    ffn_shift,
    w_in,
    b_in,
    w_back,
    b_back,
    seq_ids,
    bucket_ids,
    sort_order,
):
    section_pos = lax.axis_index("section")
    is_first = section_pos == 0
    rows_n = lax.axis_size("rows")
    live_prev = lax.axis_index("rows") > 0
    micro_n = stream_in.shape[2]
    params = tuple(
        (
            weight_arr[0]
            for weight_arr in (
                attn_gain,
                attn_shift,
                w_qk,
                w_value,
                w_out,
                ffn_gain,
                ffn_shift,
                w_in,
                b_in,
                w_back,
                b_back,
            )
        )
    )
    prev_all = from_behind(sort_order[:, :, sort_order.shape[2] - BLOCK :], "rows", 1)
    own_stream = stream_in[0].astype(jnp.float32)

    def pick_batch(int_table, batch_no):
        return lax.dynamic_index_in_dim(int_table, batch_no, 0, keepdims=False)

    def ints_for(batch_no):
        return (
            pick_batch(seq_ids, batch_no),
            pick_batch(bucket_ids, batch_no),
            pick_batch(sort_order, batch_no),
            pick_batch(prev_all, batch_no),
        )

    message = jnp.zeros_like(own_stream[:, 0])
    outputs_fwd = []
    kept_list = []
    for tick_no in range(micro_n + 1):
        batch_no = jnp.clip(tick_no - section_pos, 0, micro_n - 1)
        source = jnp.where(is_first, own_stream[:, min(tick_no, micro_n - 1)], message)
        first_out, second_out, kept_state = layer_forward(
            source[0], source[1], params, ints_for(batch_no), live_prev, rows_n
        )
        outputs_fwd.append(jnp.stack([first_out, second_out]))
        kept_list.append(kept_state)
        if tick_no < micro_n:
            message = from_behind(outputs_fwd[-1], "section", 1)
    grads_total = tuple((jnp.zeros(weight_arr.shape, jnp.float32) for weight_arr in params))
    back_msg = jnp.zeros((4,) + own_stream.shape[2:], jnp.float32)
    dx_list = []
    for tick_no in range(micro_n + 1):
        batch_raw = tick_no - 1 + section_pos
        is_live = (batch_raw >= 0) & (batch_raw < micro_n)
        batch_no = jnp.clip(batch_raw, 0, micro_n - 1)
        outs_here = jnp.where(is_first, back_msg[:2], outputs_fwd[min(tick_no + 1, micro_n)])
        grads_here = jnp.where(is_first, back_msg[2:], own_stream[:, min(tick_no, micro_n - 1)])
        first_in, second_in, grad_first, grad_second, grads = layer_backward(
            outs_here[0],
            outs_here[1],
            grads_here[0],
            grads_here[1],
            params,
            ints_for(batch_no),
            live_prev,
            rows_n,
        )
        dx_list.append(jnp.stack([grad_first, grad_second]))
        grads = tuple((jnp.where(is_live, grad_one, 0.0) for grad_one in grads))
        grads_total = tuple(
            (total_one + grad_one for total_one, grad_one in zip(grads_total, grads))
        )
        if tick_no < micro_n:
            back_msg = from_behind(
                jnp.stack([first_in, second_in, grad_first, grad_second]), "section", -1
            )
    grads_total = jax.tree.map(
        lambda part: part.astype(jnp.float32), lax.psum(shortened(grads_total), "rows")
    )
    stream_out = jnp.where(
        is_first, jnp.stack(dx_list[1:], axis=1), jnp.stack(outputs_fwd[1:], axis=1)
    )[None]
    return (
        stream_out,
        grads_total[0][None],
        grads_total[1][None],
        grads_total[2][None],
        grads_total[3][None],
        grads_total[4][None],
        grads_total[5][None],
        grads_total[6][None],
        grads_total[7][None],
        grads_total[8][None],
        grads_total[9][None],
        grads_total[10][None],
    )


VMEM_ROOM = 32 * 1024 * 1024
WHOLE_VMEM = 64 * 1024 * 1024
TILE = 128
GELU_C = 0.7978845608


def kernel_call(
    body, out_types, args, scalars=None, scratch=(), flops=0, hbm=(), after=(), label=None, mark=False, room=VMEM_ROOM
):
    n_in = len(args) + len(hbm)
    specs = [pl.BlockSpec(memory_space=pltpu.VMEM) for _ in args]
    specs = specs + [pl.BlockSpec(memory_space=pl.ANY) for _ in (*hbm, *after)]
    args = (*args, *hbm, *after)
    if scalars is not None:
        args = (scalars, *args)
        specs = [pl.BlockSpec(memory_space=pltpu.SMEM)] + specs
        n_in += 1
    n_out = len(out_types)
    if mark:
        out_types = [*out_types, ((8, 128), jnp.float32)]
    outs = tuple(jax.ShapeDtypeStruct(shape, dtype) for shape, dtype in out_types)
    moved = sum(a.size * a.dtype.itemsize for a in (*args[: len(args) - len(after)], *outs))

    def run(*refs):
        first_out = n_in + len(after)
        last_out = first_out + n_out
        if mark:
            refs[last_out][...] = jnp.zeros((8, 128), jnp.float32)
        rest = refs[last_out + (1 if mark else 0) :]
        body(*refs[:n_in], *refs[first_out:last_out], *rest)

    return pl.pallas_call(
        run,
        out_shape=outs,
        in_specs=specs,
        out_specs=tuple(pl.BlockSpec(memory_space=pltpu.VMEM) for _ in outs),
        scratch_shapes=list(scratch),
        name=label,
        compiler_params=pltpu.CompilerParams(vmem_limit_bytes=room),
        cost_estimate=pl.CostEstimate(flops=flops, bytes_accessed=moved, transcendentals=0),
    )(*args)


def flip_pairs(n, by):
    return [(i, i ^ by) for i in range(n)]


def swap_cores(x):
    return lax.ppermute(x, "section", [(0, 1), (1, 0)])


def xor_recv(parts, axis):
    return [lax.ppermute(part, axis, flip_pairs(4, k + 1)) for k, part in enumerate(parts)]


def xor_recv_core(parts, core):
    got = []
    for k, part in enumerate(parts):
        pairs = [(core * 4 + i, core * 4 + (i ^ (k + 1))) for i in range(4)]
        got.append(lax.ppermute(part, ("section", "rows"), pairs))
    return got


def gather_four(own, axis):
    return [own] + xor_recv([own] * 3, axis)


def both_halves(near):
    return near + [swap_cores(part) for part in near]


def gather_tokens(own, axis):
    return both_halves(gather_four(own, axis))


def scatter_tokens(far_part, near_part, axis):
    arrived = swap_cores(far_part)
    n_own = near_part.shape[0] // 4
    width = near_part.shape[1]

    def body(near, far, *outs):
        for k in range(4):
            rows = pl.ds(k * n_own, n_own)
            outs[k][...] = (near[rows, :] + far[rows, :].astype(jnp.float32)).astype(outs[k].dtype)

    kept, *sent = kernel_call(
        body,
        [((n_own, width), jnp.float32)] + [((n_own, width), jnp.bfloat16)] * 3,
        (near_part, arrived),
        label="scatter_tokens",
    )
    return [kept] + xor_recv(sent, axis)


def rows_norm(rows_in):
    centred = rows_in - jnp.mean(rows_in, axis=-1, keepdims=True)
    inv_std = lax.rsqrt(jnp.mean(centred * centred, axis=-1, keepdims=True) + 1e-05)
    return centred * inv_std, inv_std


def sum_parts(parts):
    total = parts[0][...]
    for part in parts[1:]:
        total = total + part[...].astype(jnp.float32)
    return total


def residual_norm(resid, parts, after, vectors, rows, shifts=None):
    n_own, width = resid.shape
    n_shift = 0 if shifts is None else 1

    def body(resid, vectors, p0, p1, p2, p3, *refs):
        total = resid[...] + sum_parts((p0, p1, p2, p3))
        if n_shift:
            total = total + refs[0][shifts[1] : shifts[1] + 1, :]
        refs[n_shift][...] = total
        if rows is not None:
            scaled, _ = rows_norm(total)
            gain, shift = (vectors[i : i + 1, :] for i in rows)
            refs[n_shift + 1][...] = (scaled * gain + shift).astype(jnp.bfloat16)

    types = [((n_own, width), jnp.float32)]
    if rows is not None:
        types.append(((n_own, width), jnp.bfloat16))
    return kernel_call(
        body,
        types,
        (resid, vectors, *parts) + (() if shifts is None else (shifts[0],)),
        after=after,
        label="residual_norm",
    )


def norm_backward(resid, parts, stream, vectors, row, after):
    n_own, width = resid.shape

    def body(resid, stream, vectors, p0, p1, p2, p3, out, low, small):
        gain = vectors[row : row + 1, :]
        grad_out = sum_parts((p0, p1, p2, p3))
        scaled, inv_std = rows_norm(stream[...])
        grad_scaled = grad_out * gain
        centred = grad_scaled - jnp.mean(grad_scaled, axis=-1, keepdims=True)
        centred = centred - scaled * jnp.mean(grad_scaled * scaled, axis=-1, keepdims=True)
        total = resid[...] + inv_std * centred
        out[...] = total
        low[...] = total.astype(jnp.bfloat16)
        small[0:1, :] = jnp.sum(grad_out * scaled, axis=0, keepdims=True)
        small[1:2, :] = jnp.sum(grad_out, axis=0, keepdims=True)
        small[2:3, :] = jnp.sum(total, axis=0, keepdims=True)
        small[3:8, :] = jnp.zeros((5, width), jnp.float32)

    return kernel_call(
        body,
        [
            ((n_own, width), jnp.float32),
            ((n_own, width), jnp.bfloat16),
            ((8, width), jnp.float32),
        ],
        (resid, stream, vectors, *parts),
        after=after,
        label="norm_backward",
    )


def join_tokens(parts, tokens):
    rows = parts[0].shape[0]
    for k, part in enumerate(parts):
        tokens[pl.ds(k * rows, rows), :] = part[...]


def attention_forward(layer, pieces, qv_pair, out_pair, masking):
    n_own, width = pieces[0].shape
    n_tok = 8 * n_own
    half = n_tok // 2
    dim = out_pair[0].shape[0]

    def body(*refs):
        masking, own_qv, got_qv, own_out, got_out, *refs_out = refs[8:]
        far_part, near_part, tokens, qv, prob, mixed, keys, w_qv, w_out, sems = refs_out
        sources = ((own_qv, got_qv), (own_out, got_out))
        waits = fetch_layer(layer, sources, (w_qv, w_out), sems)
        join_tokens(refs[:8], tokens)
        waits[0].wait()
        for start in range(0, n_tok, TILE):
            rows = pl.ds(start, TILE)
            low = dot_plain(tokens[rows, :], w_qv[...]).astype(jnp.bfloat16)
            qv[rows, :] = low
            query = low[:, :dim].astype(jnp.float32)
            inv = lax.rsqrt(jnp.sum(query * query, axis=-1, keepdims=True) + 1e-06)
            keys[rows, :] = (query * inv).astype(jnp.bfloat16)
        for start in range(0, n_tok, TILE):
            rows = pl.ds(start, TILE)
            scores = dot_right_t(qv[rows, :dim], keys[...]) + masking[rows, :]
            scores = jnp.exp(scores - jnp.max(scores, axis=-1, keepdims=True))
            total = jnp.sum(scores, axis=-1, keepdims=True)
            low = (scores * (1.0 / total)).astype(jnp.bfloat16)
            prob[rows, :] = low
            mix = dot_plain(low, qv[:, dim:]).astype(jnp.bfloat16)
            mixed[rows, :] = mix
            if start == 0:
                waits[1].wait()
            part = dot_plain(mix, w_out[...])
            if start < half:
                near_part[rows, :] = part
            else:
                far_part[pl.ds(start - half, TILE), :] = part.astype(jnp.bfloat16)

    return kernel_call(
        body,
        [
            ((half, width), jnp.bfloat16),
            ((half, width), jnp.float32),
            ((n_tok, width), jnp.bfloat16),
            ((n_tok, 2 * dim), jnp.bfloat16),
            ((n_tok, n_tok), jnp.bfloat16),
            ((n_tok, dim), jnp.bfloat16),
        ],
        (*pieces, masking),
        hbm=(*qv_pair, *out_pair),
        scratch=[
            pltpu.VMEM((n_tok, dim), jnp.bfloat16),
            pltpu.VMEM((width, 2 * dim), jnp.bfloat16),
            pltpu.VMEM((dim, width), jnp.bfloat16),
            pltpu.SemaphoreType.DMA((2,)),
        ],
        flops=2 * n_tok * (3 * width * dim + 2 * n_tok * dim),
        label="attention_forward",
    )


def attention_backward(layer, pieces, qv_pair, out_pair, qv, prob, after):
    n_own, width = pieces[0].shape
    n_tok = 8 * n_own
    half = n_tok // 2
    dim = out_pair[0].shape[0]

    def body(*refs):
        qv, prob, own_qv, got_qv, own_out, got_out, *refs_out = refs[8:]
        far_part, near_part, tokens, dqv, keys, dmix, dscore, dquery, w_qv, w_out, sems = refs_out
        sources = ((own_out, got_out), (own_qv, got_qv))
        waits = fetch_layer(layer, sources, (w_out, w_qv), sems)
        join_tokens(refs[:8], tokens)
        waits[0].wait()
        for start in range(0, n_tok, TILE):
            rows = pl.ds(start, TILE)
            dmix[rows, :] = dot_right_t(tokens[rows, :], w_out[...]).astype(jnp.bfloat16)
            query = qv[rows, :dim].astype(jnp.float32)
            inv = lax.rsqrt(jnp.sum(query * query, axis=-1, keepdims=True) + 1e-06)
            keys[rows, :] = (query * inv).astype(jnp.bfloat16)
        for start in range(0, n_tok, TILE):
            rows = pl.ds(start, TILE)
            dprob = dot_right_t(dmix[rows, :], qv[:, dim:])
            weights = prob[rows, :].astype(jnp.float32)
            centre = jnp.sum(weights * dprob, axis=-1, keepdims=True)
            low = (weights * (dprob - centre)).astype(jnp.bfloat16)
            dscore[rows, :] = low
            dquery[rows, :] = dot_plain(low, keys[...])
        waits[1].wait()
        for start in range(0, n_tok, TILE):
            rows = pl.ds(start, TILE)
            dkey = dot_left_t(dscore[:, rows], qv[:, :dim])
            dval = dot_left_t(prob[:, rows], dmix[...])
            query = qv[rows, :dim].astype(jnp.float32)
            inv = lax.rsqrt(jnp.sum(query * query, axis=-1, keepdims=True) + 1e-06)
            along = jnp.sum(query * dkey, axis=-1, keepdims=True)
            total = dquery[rows, :] + inv * dkey - inv * inv * inv * along * query
            low = jnp.concatenate(
                [total.astype(jnp.bfloat16), dval.astype(jnp.bfloat16)], axis=1
            )
            dqv[rows, :] = low
            part = dot_right_t(low, w_qv[...])
            if start < half:
                near_part[rows, :] = part
            else:
                far_part[pl.ds(start - half, TILE), :] = part.astype(jnp.bfloat16)

    return kernel_call(
        body,
        [
            ((half, width), jnp.bfloat16),
            ((half, width), jnp.float32),
            ((n_tok, width), jnp.bfloat16),
            ((n_tok, 2 * dim), jnp.bfloat16),
        ],
        (*pieces, qv, prob),
        hbm=(*qv_pair, *out_pair),
        after=after,
        scratch=[
            pltpu.VMEM((n_tok, dim), jnp.bfloat16),
            pltpu.VMEM((n_tok, dim), jnp.bfloat16),
            pltpu.VMEM((n_tok, n_tok), jnp.bfloat16),
            pltpu.VMEM((n_tok, dim), jnp.float32),
            pltpu.VMEM((width, 2 * dim), jnp.bfloat16),
            pltpu.VMEM((dim, width), jnp.bfloat16),
            pltpu.SemaphoreType.DMA((2,)),
        ],
        flops=2 * n_tok * (3 * width * dim + 4 * n_tok * dim),
        label="attention_backward",
    )


def fetch_layer(layer, sources, targets, sems):
    held_here = lax.axis_index("section") == layer

    @pl.when(held_here)
    def _():
        for i, (own, _) in enumerate(sources):
            pltpu.make_async_copy(own, targets[i], sems.at[i]).start()

    @pl.when(jnp.logical_not(held_here))
    def _():
        for i, (_, got) in enumerate(sources):
            pltpu.make_async_copy(got, targets[i], sems.at[i]).start()

    return [
        pltpu.make_async_copy(own, targets[i], sems.at[i]) for i, (own, _) in enumerate(sources)
    ]


def scattered_types(n_own, width):
    return [((n_own, width), jnp.float32)] + [((n_own, width), jnp.bfloat16)] * 3


def store_scattered(outs, start, part):
    n_own = outs[0].shape[0]
    for at in range(0, part.shape[0], n_own):
        out = outs[(start + at) // n_own]
        out[...] = part[at : at + n_own, :].astype(out.dtype)


def feed_forward(layer, pieces, vectors, row, w_in, w_back):
    n_own, width = pieces[0].shape
    n_tok = 4 * n_own
    hidden = w_in[0].shape[1]

    def body(*refs):
        vectors, own_in, got_in, own_back, got_back = refs[4:9]
        bias = vectors[row : row + 1, :]
        outs, (tokens, active, slope, wide_in, wide_back, sems) = refs[9:13], refs[13:]
        sources = ((own_in, got_in), (own_back, got_back))
        waits = fetch_layer(layer, sources, (wide_in, wide_back), sems)
        join_tokens(refs[:4], tokens)
        waits[0].wait()
        for start in range(0, n_tok, TILE):
            rows = pl.ds(start, TILE)
            pre = dot_plain(tokens[rows, :], wide_in[...]) + bias
            square = pre * pre
            bent = jnp.tanh(GELU_C * (pre + 0.044715 * pre * square))
            low = (0.5 * pre * (1.0 + bent)).astype(jnp.bfloat16)
            active[rows, :] = low
            slope[rows, :] = 0.5 * (1.0 + bent) + 0.5 * pre * (1.0 - bent * bent) * (
                GELU_C * (1.0 + 3.0 * 0.044715 * square)
            )
            if start == 0:
                waits[1].wait()
            store_scattered(outs, start, dot_plain(low, wide_back[...]))

    outs = kernel_call(
        body,
        scattered_types(n_own, width)
        + [
            ((n_tok, width), jnp.bfloat16),
            ((n_tok, hidden), jnp.bfloat16),
            ((n_tok, hidden), jnp.float32),
        ],
        (*pieces, vectors),
        hbm=(*w_in, *w_back),
        scratch=[
            pltpu.VMEM((width, hidden), jnp.bfloat16),
            pltpu.VMEM((hidden, width), jnp.bfloat16),
            pltpu.SemaphoreType.DMA((2,)),
        ],
        flops=4 * n_tok * width * hidden,
        label="feed_forward",
    )
    return outs[:4], outs[4], outs[5], outs[6]


def feed_backward(layer, pieces, slope, w_in, w_back, after):
    n_own, width = pieces[0].shape
    n_tok = 4 * n_own
    hidden = slope.shape[1]

    def body(*refs):
        slope, own_in, got_in, own_back, got_back = refs[4:9]
        outs, (tokens, dpre, wide_in, wide_back, sems) = refs[9:13], refs[13:]
        sources = ((own_back, got_back), (own_in, got_in))
        waits = fetch_layer(layer, sources, (wide_back, wide_in), sems)
        join_tokens(refs[:4], tokens)
        waits[0].wait()
        for start in range(0, n_tok, TILE):
            rows = pl.ds(start, TILE)
            grad = dot_right_t(tokens[rows, :], wide_back[...]) * slope[rows, :]
            low = grad.astype(jnp.bfloat16)
            dpre[rows, :] = low
            if start == 0:
                waits[1].wait()
            store_scattered(outs, start, dot_right_t(low, wide_in[...]))

    outs = kernel_call(
        body,
        scattered_types(n_own, width)
        + [((n_tok, width), jnp.bfloat16), ((n_tok, hidden), jnp.bfloat16)],
        (*pieces, slope),
        hbm=(*w_in, *w_back),
        after=after,
        scratch=[
            pltpu.VMEM((width, hidden), jnp.bfloat16),
            pltpu.VMEM((hidden, width), jnp.bfloat16),
            pltpu.SemaphoreType.DMA((2,)),
        ],
        flops=4 * n_tok * width * hidden,
        label="feed_backward",
    )
    return outs[:4], outs[4], outs[5]


def feed_grads(coords, norm_in, grad_in, active, dpre, turned, after):
    n_tok, width = norm_in.shape
    hidden = active.shape[1]
    in_rows, back_rows = width // 8, hidden // 8
    shape = (4, in_rows + back_rows + 16, width)

    def body(coords, norm_in, grad_in, active, dpre, *outs):
        bias = jnp.sum(dpre[...].astype(jnp.float32), axis=0, keepdims=True)
        tail = jnp.concatenate([bias, jnp.zeros((15, hidden), jnp.float32)], axis=0)
        for k in range(4):
            for part in range(2):
                chunk, half = (coords[2] ^ k, coords[0] ^ part) if turned else (k, part)
                at = 2 * chunk + half
                out = outs[part] if turned else outs[0].at[part]
                cols = pl.ds(pl.multiple_of(at * in_rows, in_rows), in_rows)
                out[k, :in_rows, :] = dot_left_t(norm_in[:, cols], dpre[...]).astype(jnp.bfloat16)
                cols = pl.ds(pl.multiple_of(at * back_rows, back_rows), back_rows)
                out[k, in_rows : in_rows + back_rows, :] = dot_left_t(
                    active[:, cols], grad_in[...]
                ).astype(jnp.bfloat16)
                out[k, in_rows + back_rows :, :] = tail.astype(jnp.bfloat16)

    return kernel_call(
        body,
        [(shape, jnp.bfloat16)] * 2 if turned else [((2,) + shape, jnp.bfloat16)],
        (norm_in, grad_in, active, dpre),
        scalars=coords,
        after=after,
        flops=4 * n_tok * width * hidden,
        label="feed_grads",
        mark=True,
    )


def add_cores(parts, other, after):
    shape = parts.shape[1:]

    def body(parts, other, *outs):
        for k in range(4):
            total = parts[k].astype(jnp.float32) + other[k].astype(jnp.float32)
            outs[k][...] = total.astype(jnp.bfloat16)

    return kernel_call(
        body, [(shape, jnp.bfloat16)] * 4, (parts, other), after=after, label="add_cores", mark=True
    )


def permute_one(x, by):
    return lax.ppermute(x, "rows", flip_pairs(4, by))


def sum_four(parts):
    total = parts[0][...].astype(jnp.float32) + parts[1][...].astype(jnp.float32)
    return total + parts[2][...].astype(jnp.float32) + parts[3][...].astype(jnp.float32)


def add_four(parts, after, label):
    def body(p0, p1, p2, p3, out):
        out[...] = sum_four((p0, p1, p2, p3)).astype(jnp.bfloat16)

    return kernel_call(
        body, [(parts[0].shape, jnp.bfloat16)], parts, after=after, label=label, mark=True
    )


def pair_heads(coords, own_low, own_high):
    shape = own_low.shape

    def split_body(coords, own_low, own_high, kept, sent):
        is_low = coords[0] == 0
        kept[...] = jnp.where(is_low, own_low[...], own_high[...])
        sent[...] = jnp.where(is_low, own_high[...], own_low[...])

    kept, sent = kernel_call(
        split_body,
        [(shape, own_low.dtype)] * 2,
        (own_low, own_high),
        scalars=coords,
        label="split_heads",
    )

    def join_body(coords, kept, got, out):
        out[coords[0]] = kept[...]
        out[1 - coords[0]] = got[...]

    return kernel_call(
        join_body,
        [((2,) + shape, own_low.dtype)],
        (kept, swap_cores(sent)),
        scalars=coords,
        label="join_heads",
    )[0]


def head_grads(coords, norm_in, grad_in, mixed, dqv, after):
    n_tok, width = norm_in.shape
    dim = mixed.shape[1]
    part = width // 4

    def body(coords, norm_in, grad_in, mixed, dqv, *outs):
        for k in range(4):
            cols = pl.ds(pl.multiple_of((coords[2] ^ k) * part, part), part)
            outs[k][:part, :] = dot_left_t(norm_in[:, cols], dqv[...]).astype(jnp.bfloat16)
            outs[k][part:, :] = dot_left_t(mixed[...], grad_in[:, cols]).astype(jnp.bfloat16)

    return kernel_call(
        body,
        [((part + dim, part), jnp.bfloat16)] * 4,
        (norm_in, grad_in, mixed, dqv),
        scalars=coords,
        after=after,
        flops=2 * n_tok * width * 3 * dim,
        label="head_grads",
        mark=True,
    )


def to_layer(parts, layer, after):
    def body(p0, p1, p2, p3, out):
        for k, part in enumerate((p0, p1, p2, p3)):
            out[k] = part[...]

    whole, mark = kernel_call(
        body,
        [((4,) + parts[0].shape, parts[0].dtype)],
        parts,
        after=after,
        label="pack_four",
        mark=True,
    )
    return (whole, lax.ppermute(whole, "section", [(1 - layer, layer)])), mark


def place_heads(coords, parts, dim):
    _, rows, part = parts[0].shape

    def body(coords, p0, p1, p2, p3, w_qk, w_value, w_out):
        for k, piece in enumerate((p0, p1, p2, p3)):
            there = pl.ds(pl.multiple_of((coords[2] ^ k) * part, part), part)
            for head in range(2):
                here = slice(head * dim, (head + 1) * dim)
                value = piece[head].astype(jnp.float32)
                w_qk[there, here] = value[:part, :dim]
                w_value[there, here] = value[:part, dim:]
                w_out[here, there] = value[part:, :]

    f32 = jnp.float32
    return kernel_call(
        body,
        [((4 * part, 2 * dim), f32)] * 2 + [((2 * dim, 4 * part), f32)],
        parts,
        scalars=coords,
        label="place_heads",
        mark=True,
    )


def place_hidden(coords, low_hidden, high_layer, after):
    feed_rows, width = low_hidden.shape[2:]
    block = (feed_rows - 16) // 2

    def body(coords, hidden, *refs):
        high = refs[:2]
        w_in, w_back, b_in, held, wide, in_sems, out_sems = refs[2 + len(after) :]
        is_low = coords[0] == 0

        @pl.when(is_low)
        def _():
            for i in range(8):
                there = held.at[i]
                source = hidden.at[i // 4, coords[2] ^ (i % 4)]
                pltpu.make_async_copy(source, there, in_sems.at[i]).start()

        @pl.when(jnp.logical_not(is_low))
        def _():
            for i in range(8):
                there = held.at[i]
                source = high[i // 4].at[i % 4]
                pltpu.make_async_copy(source, there, in_sems.at[i]).start()

        sends = []
        for i in range(8):
            there = held.at[i]
            pltpu.make_async_copy(hidden.at[0, 0], there, in_sems.at[i]).wait()
            half = (i // 4) ^ coords[0]
            chunk = coords[2] ^ (i % 4)
            there = pl.ds(pl.multiple_of((2 * chunk + half) * block, block), block)
            for j, out in enumerate((w_in, w_back)):
                wide[i, j] = held[i, pl.ds(j * block, block), :].astype(jnp.float32)
                sends.append(
                    pltpu.make_async_copy(wide.at[i, j], out.at[there, :], out_sems.at[2 * i + j])
                )
                sends[-1].start()
        b_in[...] = held[0, pl.ds(2 * block, 16), :].astype(jnp.float32)[0:1, :]
        for send in sends:
            send.wait()

    f32 = jnp.float32
    outs = [((width, width), f32), ((8 * block, width), f32), ((1, width), f32)]
    spaces = [pltpu.HBM, pltpu.HBM, pltpu.VMEM]
    return pl.pallas_call(
        body,
        out_shape=tuple(jax.ShapeDtypeStruct(*out) for out in outs),
        in_specs=[pl.BlockSpec(memory_space=pltpu.SMEM)]
        + [pl.BlockSpec(memory_space=pltpu.HBM)] * 3
        + [pl.BlockSpec(memory_space=pl.ANY)] * len(after),
        out_specs=tuple(pl.BlockSpec(memory_space=space) for space in spaces),
        scratch_shapes=[
            pltpu.VMEM((8, feed_rows, width), jnp.bfloat16),
            pltpu.VMEM((8, 2, block, width), f32),
            pltpu.SemaphoreType.DMA((8,)),
            pltpu.SemaphoreType.DMA((16,)),
        ],
        name="place_hidden",
        compiler_params=pltpu.CompilerParams(vmem_limit_bytes=VMEM_ROOM),
    )(coords, low_hidden, *high_layer, *after)


def split_three(value):
    first = value.astype(jnp.bfloat16).astype(jnp.float32)
    rest = value - first
    second = rest.astype(jnp.bfloat16).astype(jnp.float32)
    return jnp.concatenate(
        [first, second, rest - second, jnp.zeros((13, value.shape[1]), jnp.float32)], axis=0
    ).astype(jnp.bfloat16)


def own_weights(w_qk, w_value, w_out, rows, after):
    width, cols = w_qk.shape[1:]
    dim = cols // 2
    dtype = w_qk.dtype

    def body(w_qk, w_value, w_out, *refs):
        sources = refs[: len(rows)]
        qv_mine, qv_other, out_mine, out_other, vectors, sems, row_sems = refs[len(rows) :]
        core = lax.axis_index("section")
        copies = []
        for side, (qv, out) in enumerate(((qv_mine, out_mine), (qv_other, out_other))):
            which = core if side == 0 else 1 - core
            here = pl.ds(pl.multiple_of(which * dim, dim), dim)
            for i, (source, target) in enumerate(
                (
                    (w_qk.at[0, :, here], qv.at[:, pl.ds(0, dim)]),
                    (w_value.at[0, :, here], qv.at[:, pl.ds(dim, dim)]),
                    (w_out.at[0, here, :], out),
                )
            ):
                copies.append(pltpu.make_async_copy(source, target, sems.at[3 * side + i]))
        vectors[...] = jnp.zeros(vectors.shape, jnp.float32)
        for i, source in enumerate(sources):
            there = vectors.at[pl.ds(i, 1), pl.ds(0, source.shape[1])]
            copies.append(pltpu.make_async_copy(source, there, row_sems.at[i]))
        for copy in copies:
            copy.start()
        for copy in copies:
            copy.wait()

    return kernel_call(
        body,
        [((width, cols), dtype)] * 2 + [((dim, width), dtype)] * 2 + [((8, width), jnp.float32)],
        (),
        hbm=(w_qk, w_value, w_out, *rows),
        after=after,
        scratch=[pltpu.SemaphoreType.DMA((6,)), pltpu.SemaphoreType.DMA((len(rows),))],
        label="own_weights",
        room=WHOLE_VMEM,
    )


def batch_parts(stream, seq_ids, bucket_ids):
    _, n_val, micro_n, tok_rows, feats = stream.shape
    rounds_n = bucket_ids.shape[1]
    base = n_val * tok_rows
    per_row = feats // tok_rows

    def body(seq_ids, bucket_ids, stream, out, sems):
        copies = []
        for m in range(micro_n):
            for i in range(n_val):
                there = out.at[m, pl.ds(i * tok_rows, tok_rows)]
                copies.append(
                    pltpu.make_async_copy(stream.at[0, i, m], there, sems.at[n_val * m + i])
                )
                copies[-1].start()
        for m in range(micro_n):
            tables = [seq_ids[m : m + 1, :]]
            tables += [bucket_ids[m, r : r + 1, :] for r in range(rounds_n)]
            tables = [table.astype(jnp.float32) for table in tables]
            while len(tables) % per_row:
                tables.append(jnp.zeros((1, tok_rows), jnp.float32))
            rows = [
                jnp.concatenate(tables[i : i + per_row], axis=1)
                for i in range(0, len(tables), per_row)
            ]
            rows.append(jnp.zeros((16 - len(rows), feats), jnp.float32))
            out[m, base : base + 16, :] = jnp.concatenate(rows, axis=0).astype(jnp.bfloat16)
        for copy in copies:
            copy.wait()

    return kernel_call(
        body,
        [((micro_n, base + 16, feats), stream.dtype)],
        (seq_ids, bucket_ids),
        hbm=(stream,),
        scratch=[pltpu.SemaphoreType.DMA((n_val * micro_n,))],
        label="batch_parts",
    )[0]


def feature_parts(coords, got, other, low_vectors, high_vectors):
    n_seg, rows, feats = other.shape
    tok_rows = (rows - 16) // 2
    half = tok_rows // 2

    def body(coords, got, other, low_vectors, high_vectors, low, high, *outs):
        is_low = coords[0] == 0

        def sides(seg, stream):
            rows = pl.ds(pl.multiple_of(stream * tok_rows + coords[0] * half, half), half)
            mine, theirs = got[seg, rows, :], other[seg, rows, :]
            return jnp.where(is_low, mine, theirs), jnp.where(is_low, theirs, mine)

        for c in range(n_seg):
            there = pl.ds(c * half, half)
            low[there, :], high[there, :] = sides(c, 1)
        high[n_seg * half :, :] = jnp.concatenate(
            [split_three(v[5:6, :feats])[:8] for v in (low_vectors, high_vectors)], axis=0
        )
        for k in range(4):
            outs[k][:half, :], outs[k][half:, :] = sides(coords[1] ^ k, 0)

    dtype = got.dtype
    low, high, *firsts = kernel_call(
        body,
        [((n_seg * half, feats), dtype), ((n_seg * half + 16, feats), dtype)]
        + [((2 * half, feats), dtype)] * 4,
        (got, other, low_vectors, high_vectors),
        scalars=coords,
        label="feature_parts",
    )
    return low, high, firsts


def first_tokens(coords, parts, vectors, after):
    n_tok, feats = parts[0].shape
    n_own, width = n_tok // 4, 4 * feats

    def body(coords, p0, p1, p2, p3, vectors, stream, *rest):
        gain, shift = vectors[0:1, :], vectors[1:2, :]
        lows, rows_all = rest[:4], rest[4]
        for k, part in enumerate((p0, p1, p2, p3)):
            cols = pl.ds(pl.multiple_of((coords[1] ^ k) * feats, feats), feats)
            for j in range(4):
                rows = pl.ds(pl.multiple_of((coords[1] ^ j) * n_own, n_own), n_own)
                rows_all[pl.ds(j * n_own, n_own), cols] = part[rows, :].astype(jnp.float32)
        stream[...] = rows_all[pl.ds(0, n_own), :]
        for j in range(4):
            scaled, _ = rows_norm(rows_all[pl.ds(j * n_own, n_own), :])
            lows[j][...] = (scaled * gain + shift).astype(jnp.bfloat16)

    stream, *lows = kernel_call(
        body,
        [((n_own, width), jnp.float32)] + [((n_own, width), jnp.bfloat16)] * 4,
        (*parts, vectors),
        scalars=coords,
        after=after,
        scratch=[pltpu.VMEM((n_tok, width), jnp.float32)],
        label="first_tokens",
    )
    return stream, lows


def first_grads(coords, parts):
    n_tok, feats = parts[0].shape
    n_tok = n_tok - 16
    n_own, width = n_tok // 4, 4 * feats

    def body(coords, p0, p1, p2, p3, stream, small, shifts, *lows):
        for k, part in enumerate((p0, p1, p2, p3)):
            cols = pl.ds(pl.multiple_of((coords[1] ^ k) * feats, feats), feats)
            for j in range(4):
                rows = pl.ds(pl.multiple_of((coords[1] ^ j) * n_own, n_own), n_own)
                lows[j][:, cols] = part[rows, :]
            extra = part[pl.ds(n_tok, 16), :].astype(jnp.float32)
            for i in range(2):
                shifts[i : i + 1, cols] = (
                    extra[8 * i : 8 * i + 1, :]
                    + extra[8 * i + 1 : 8 * i + 2, :]
                    + extra[8 * i + 2 : 8 * i + 3, :]
                )
        total = lows[0][...].astype(jnp.float32)
        stream[...] = total
        small[...] = jnp.zeros(small.shape, jnp.float32)
        small[2:3, :] = jnp.sum(total, axis=0, keepdims=True)

    stream, small, shifts, *lows = kernel_call(
        body,
        [
            ((n_own, width), jnp.float32),
            ((8, width), jnp.float32),
            ((2, width), jnp.float32),
        ]
        + [((n_own, width), jnp.bfloat16)] * 4,
        parts,
        scalars=coords,
        label="first_grads",
    )
    return stream, small, shifts, lows


def held_back(values, after):
    n = len(values)

    def body(*refs):
        for i in range(n):
            refs[n + i][...] = refs[i][...]

    return kernel_call(body, [(v.shape, v.dtype) for v in values], values, after=after, label="held_back")


def exchange(parts, axis):
    return lax.all_to_all(parts, axis, split_axis=0, concat_axis=0, tiled=True)


def own_rows(coords, parts):
    half, feats = parts[0].shape[0] // 2, parts[0].shape[1]

    def body(coords, p0, p1, p2, p3, low, high):
        for k, part in enumerate((p0, p1, p2, p3)):
            cols = pl.ds(pl.multiple_of((coords[1] ^ k) * feats, feats), feats)
            low[:, cols] = part[:half, :].astype(jnp.float32)
            high[:, cols] = part[half:, :].astype(jnp.float32)

    return kernel_call(
        body,
        [((half, 4 * feats), jnp.float32)] * 2,
        parts,
        scalars=coords,
        label="own_rows",
    )


def split_two(value):
    first = value.astype(jnp.bfloat16)
    return first, (value - first.astype(jnp.float32)).astype(jnp.bfloat16)


def small_from(part, at, feats):
    pieces = []
    for q in range(4):
        first = part[at + 16 * q : at + 16 * q + 16, :].astype(jnp.float32)
        second = part[at + 64 + 16 * q : at + 64 + 16 * q + 16, :].astype(jnp.float32)
        pieces.append(first + second)
    return jnp.concatenate(pieces, axis=1)


def store_small(out, at, small, feats):
    first, second = split_two(small)
    for q in range(4):
        cols = slice(q * feats, (q + 1) * feats)
        out[at + 16 * q : at + 16 * q + 16, :] = first[:, cols]
        out[at + 64 + 16 * q : at + 64 + 16 * q + 16, :] = second[:, cols]


def stream_home(coords, later, grad, small_low, small_high, after, last_after):
    n_val = len(later)
    half, width = later[0].shape
    feats = width // 4
    base = n_val * half
    tall = 2 * base

    def split_body(coords, *refs):
        sent, kept, small = refs[2 * n_val + 6 :]
        for i in range(n_val):
            low, high = refs[i], refs[n_val + i]
            rows = pl.ds(i * half, half)
            sent[rows, :] = jnp.where(coords[0] == 0, low[...], high[...]).astype(jnp.bfloat16)
            kept[rows, :] = jnp.where(coords[0] == 0, high[...], low[...]).astype(jnp.bfloat16)
        small[...] = jnp.zeros(small.shape, jnp.float32)
        for layer in range(2):
            attn, feed, back = refs[2 * n_val + 3 * layer : 2 * n_val + 3 * layer + 3]
            small[8 * layer : 8 * layer + 2, :] = attn[0:2, :]
            small[8 * layer + 2 : 8 * layer + 4, :] = feed[0:2, :]
            small[8 * layer + 4 : 8 * layer + 5, :] = back[2:3, :]
        first, second = split_two(small[...])
        sent[base : base + 16, :] = first
        sent[base + 16 : base + 32, :] = second

    sent, kept, small = kernel_call(
        split_body,
        [
            ((base + 32, width), jnp.bfloat16),
            ((base, width), jnp.bfloat16),
            ((16, width), jnp.float32),
        ],
        (*later, *grad, *small_low, *small_high),
        scalars=coords,
        label="stream_split",
    )
    got = swap_cores(sent)
    types = [((tall + 128, feats), jnp.bfloat16)] * 4

    def body(coords, kept, small, got, *outs):
        total = small[...] + got[base : base + 16, :].astype(jnp.float32)
        total = total + got[base + 16 : base + 32, :].astype(jnp.float32)
        for k in range(4):
            cols = pl.ds(pl.multiple_of((coords[1] ^ k) * feats, feats), feats)
            for i in range(n_val):
                rows = pl.ds(i * half, half)
                at = 2 * i * half
                there = pl.ds(pl.multiple_of(at + coords[0] * half, half), half)
                outs[k][there, :] = kept[rows, cols]
                there = pl.ds(pl.multiple_of(at + (1 - coords[0]) * half, half), half)
                outs[k][there, :] = got[rows, cols]
            store_small(outs[k], tall, total, feats)

    parts = kernel_call(
        body, types, (kept, small, got), scalars=coords, after=after, label="stream_home"
    )
    parts = [parts[0]] + xor_recv(parts[1:], "head")

    def middle_body(coords, *refs):
        parts, outs = refs[:4], refs[4:]
        total = small_from(parts[0], tall, feats)
        for k in range(1, 4):
            total = total + small_from(parts[k], tall, feats)
        turn = coords[1] ^ coords[2]
        for j in range(4):
            value = parts[j][:tall, :]
            for k in range(1, 4):
                value = jnp.where(turn == k, parts[j ^ k][:tall, :], value)
            outs[j][:tall, :] = value
            store_small(outs[j], tall, total, feats)

    parts = kernel_call(
        middle_body, types, parts, scalars=coords, label="stream_middle"
    )
    parts = [parts[0]] + xor_recv(parts[1:], "rows")

    def last_body(coords, *refs):
        parts = refs[:4]
        stream, attn_gain, attn_shift, ffn_gain, ffn_shift, back, scratch = refs[4:]
        total = small_from(parts[0], tall, feats)
        for k in range(1, 4):
            total = total + small_from(parts[k], tall, feats)
        scratch[...] = jnp.where(coords[0] == 0, total[:8, :], total[8:, :])
        for k in range(4):
            for i in range(n_val):
                rows = pl.ds(2 * i * half, 2 * half)
                stream[i, coords[2] ^ k] = parts[k][rows, :].astype(jnp.float32)
        for i, out in enumerate((attn_gain, attn_shift, ffn_gain, ffn_shift)):
            out[...] = scratch[i : i + 1, :]
        cols = pl.ds(pl.multiple_of(coords[1] * feats, feats), feats)
        back[...] = scratch[4:5, cols]

    return kernel_call(
        last_body,
        [((n_val, 4, 2 * half, feats), jnp.float32)]
        + [((1, width), jnp.float32)] * 4
        + [((1, feats), jnp.float32)],
        parts,
        scalars=coords,
        scratch=[pltpu.VMEM((8, width), jnp.float32)],
        label="stream_last",
        after=last_after,
    )


def order_vectors(coords, own, got):
    def body(coords, own, got, low, high):
        low[...] = jnp.where(coords[0] == 0, own[...], got[...])
        high[...] = jnp.where(coords[0] == 0, got[...], own[...])

    return kernel_call(
        body, [(own.shape, own.dtype)] * 2, (own, got), scalars=coords, label="order_vectors"
    )


def score_masking(coords, got, rounds_n, after):
    n_seg, rows, feats = got.shape
    tok_rows = (rows - 16) // 2
    half = tok_rows // 2
    n_tok = n_seg * tok_rows
    n_blocks = n_tok // BLOCK
    per_row = feats // tok_rows

    def places(coords, shape, dim):
        index = lax.broadcasted_iota(jnp.int32, shape, dim)
        seg = coords[1] ^ ((index // half) % 4)
        side = coords[0] ^ (index // (4 * half))
        return seg * tok_rows + side * half + index % half

    def tables(coords, got, by_lane, by_row):
        natural = []
        for i in range(8):
            if i > rounds_n:
                natural.append(jnp.zeros((1, n_tok), jnp.bfloat16))
                continue
            row, cols = 2 * tok_rows + i // per_row, (i % per_row) * tok_rows
            natural.append(
                jnp.concatenate(
                    [
                        got[c, row : row + 1, cols : cols + tok_rows].astype(jnp.float32)
                        for c in range(n_seg)
                    ],
                    axis=1,
                ).astype(jnp.bfloat16)
            )
        natural = jnp.concatenate([part.astype(jnp.float32) for part in natural], axis=0)
        natural = natural.astype(jnp.bfloat16)
        index = lax.broadcasted_iota(jnp.int32, (n_tok, n_tok), 0)
        moving = (index == places(coords, (n_tok, n_tok), 1)).astype(jnp.float32)
        moving = moving.astype(jnp.bfloat16)
        lane_ints = dot_plain(natural, moving)
        lane_keys = lane_ints[0:1, :] * 1024.0 + lane_ints[1 : 1 + rounds_n, :]
        lane_places = places(coords, (1, n_tok), 1).astype(jnp.float32)
        by_lane[:rounds_n, :] = lane_keys * float(n_tok) + lane_places
        by_lane[rounds_n:, :] = lane_keys
        row_ints = lax.dot_general(
            moving, natural, (((0,), (1,)), ((), ())), preferred_element_type=jnp.float32
        )
        row_keys = row_ints[:, 0:1] * 1024.0 + row_ints[:, 1 : 1 + rounds_n]
        row_places = places(coords, (n_tok, 1), 0).astype(jnp.float32)
        by_row[:, :rounds_n] = row_keys * float(n_tok) + row_places
        by_row[:, rounds_n:] = row_keys

    def body(coords, got, masking, by_lane, by_row):
        tables(coords, got, by_lane, by_row)
        for start in range(0, n_tok, TILE):
            masking[pl.ds(start, TILE), :] = jnp.zeros((TILE, n_tok), jnp.float32)
        for r in range(rounds_n):
            lane_code = by_lane[r : r + 1, :]
            lane_key = by_lane[rounds_n + r : rounds_n + r + 1, :]
            behind = jnp.zeros((1, n_tok), jnp.float32)
            for start in range(0, n_tok, TILE):
                rows = pl.ds(start, TILE)
                less = (lane_code < by_row[rows, r : r + 1]).astype(jnp.float32)
                behind = behind + jnp.sum(less, axis=0, keepdims=True)
            lane_block = jnp.floor((n_tok - 1.0 - behind) * (1.0 / BLOCK))
            lane_place = lane_key * (2.0 * n_blocks) + lane_block
            for start in range(0, n_tok, TILE):
                rows = pl.ds(start, TILE)
                less = lane_code < by_row[rows, r : r + 1]
                rank = jnp.sum(less.astype(jnp.float32), axis=1, keepdims=True)
                row_place = by_row[rows, rounds_n + r : rounds_n + r + 1] * (
                    2.0 * n_blocks
                ) + jnp.floor(rank * (1.0 / BLOCK))
                seen = less & (row_place - lane_place < 1.5)
                masking[rows, :] += seen.astype(jnp.float32)
        for start in range(0, n_tok, TILE):
            rows = pl.ds(start, TILE)
            count = masking[rows, :]
            itself = by_lane[0:1, :] == by_row[rows, 0:1]
            other = jnp.where(itself, -100000.0, -1000000000.0)
            masking[rows, :] = jnp.where(count > 0.5, jnp.log(jnp.maximum(count, 1.0)), other)

    return kernel_call(
        body,
        [((n_tok, n_tok), jnp.float32)],
        (got,),
        scalars=coords,
        after=after,
        scratch=[
            pltpu.VMEM((2 * rounds_n, n_tok), jnp.float32),
            pltpu.VMEM((n_tok, 2 * rounds_n), jnp.float32),
        ],
        label="score_masking",
    )[0]


def parallel_local(
    stream_in,
    attn_gain,
    attn_shift,
    w_qk,
    w_value,
    w_out,
    ffn_gain,
    ffn_shift,
    w_in,
    b_in,
    w_back,
    b_back,
    seq_ids,
    bucket_ids,
    sort_order,
):
    core = lax.axis_index("section")
    col = lax.axis_index("head")
    row = lax.axis_index("rows")
    coords = jnp.stack([core, col, row]).astype(jnp.int32)

    batches = batch_parts(stream_in, seq_ids, bucket_ids)
    batch_got = exchange(batches, "rows")
    qv_mine, qv_other, out_mine, out_other, own_vectors = own_weights(
        w_qk,
        w_value,
        w_out,
        (attn_gain, attn_shift, ffn_gain, ffn_shift, b_in, b_back),
        (batches,),
    )
    vectors = order_vectors(coords, own_vectors, swap_cores(own_vectors))
    low_part, high_part, firsts = feature_parts(
        coords, batch_got, swap_cores(batch_got), *vectors
    )
    qv_pair = (qv_mine, swap_cores(qv_other))
    out_pair = (out_mine, swap_cores(out_other))
    low_parts = gather_four(low_part, "head")
    masking = score_masking(coords, batch_got, bucket_ids.shape[1], (low_part,))
    second, lows = first_tokens(coords, low_parts, vectors[0], (masking,))
    wide_in = (w_in[0], swap_cores(w_in[0]))
    wide_back = (w_back[0], swap_cores(w_back[0]))
    first, grad_first = own_rows(coords, [firsts[0]] + xor_recv(firsts[1:], "head"))

    kept = []
    pieces = both_halves(lows)
    for layer in range(2):
        far_part, near_part, attn_in, qv, prob, mixed = attention_forward(
            layer, pieces, qv_pair, out_pair, masking
        )
        parts = scatter_tokens(far_part, near_part, "head")
        attn_stream = second
        first, low = residual_norm(first, parts, (), vectors[layer], (2, 3))
        if layer == 0:
            (high_part,) = held_back((high_part,), (low,))
            grad_second, small_back, shifts, grad_lows = first_grads(
                coords, gather_four(high_part, "head")
            )
        sent, ffn_in, active, slope = feed_forward(
            layer, gather_four(low, "head"), vectors[layer], 4, wide_in, wide_back
        )
        kept.append((attn_in, qv, prob, mixed, attn_stream, ffn_in, active, slope, first))
        if layer == 0:
            parts = [sent[0]] + xor_recv(sent[1:], "head")
            second, low = residual_norm(second, parts, (), vectors[1], (0, 1), (shifts, 0))
            pieces = gather_tokens(low, "head")
    last_sent = sent

    small_rows = [None] * 2
    feed_first, attn_first, feed_close = (), (), ()
    for layer in (1, 0):
        attn_in, qv, prob, mixed, attn_stream, ffn_in, active, slope, ffn_stream = kept[layer]
        sent, grad_in, dpre = feed_backward(
            layer, grad_lows, slope, wide_in, wide_back, feed_first
        )
        parts = [sent[0]] + xor_recv(sent[1:], "head")
        *feed_out, feed_mark = feed_grads(
            coords, ffn_in, grad_in, active, dpre, layer == 1, tuple(parts[1:]) if layer else ()
        )
        if layer == 0:
            high_heads, heads_mark = add_four(head_arrived, tuple(parts[1:]), "add_heads")
            feed_close = (heads_mark,)
        grad_first, grad_low, feed_small = norm_backward(
            grad_first, parts, ffn_stream, vectors[layer], 2, (feed_mark, *feed_close)
        )
        near = gather_four(grad_low, "head")
        if layer == 1:
            feed_kept, *feed_sent, cores_mark = add_cores(
                feed_out[0], swap_cores(feed_out[1]), tuple(near[1:])
            )
            feed_arrived = [feed_kept] + xor_recv(feed_sent, "rows")
            attn_first = (cores_mark,)
        else:
            low_hidden = lax.psum(feed_out[0], ("section", "rows"))
            attn_first = (mine[3],)
        far_part, near_part, grad_out, dqv = attention_backward(
            layer, both_halves(near), qv_pair, out_pair, qv, prob, attn_first
        )
        parts = scatter_tokens(far_part, near_part, "head")
        *attn_parts, attn_mark = head_grads(
            coords, attn_in, grad_out, mixed, dqv, tuple(parts[1:])
        )
        closing = (attn_mark,)
        if layer == 0:
            high_layer, pack_mark = to_layer(mine, 1, tuple(parts[1:]))
            closing = (attn_mark, pack_mark)
        head_arrived = [attn_parts[0]] + xor_recv(attn_parts[1:], "rows")
        back_small = small_back
        grad_second, grad_low, small_back = norm_backward(
            grad_second, parts, attn_stream, vectors[layer], 0, closing
        )
        small_rows[layer] = (small_back, feed_small, back_small)
        if layer == 1:
            grad_lows = gather_four(grad_low, "head")
            high_own, high_mark = add_four(feed_arrived, tuple(grad_lows[1:]), "add_feed")
            mine = gather_four(high_own, "rows")
            feed_first = (high_mark,)
    last_parts = held_back(tuple(last_sent), (grad_low,))
    last_parts = [last_parts[0]] + xor_recv(last_parts[1:], "head")
    (second,) = residual_norm(second, last_parts, (), vectors[1], None, (shifts, 1))
    low_heads, _ = add_four(head_arrived, (), "add_heads")
    heads = gather_four(pair_heads(coords, low_heads, high_heads), "rows")

    stream_out, *small_out, back_out = stream_home(
        coords, (first, second), (grad_first, grad_second), *small_rows, (), (low_hidden,)
    )
    dim = w_qk.shape[2] // 2
    grad_w_qk, grad_w_value, grad_w_out, heads_mark = place_heads(coords, heads, dim)
    grad_w_in, grad_w_back, grad_b_in = place_hidden(
        coords, low_hidden, high_layer, (back_out, heads_mark)
    )
    return (
        stream_out[None],
        small_out[0],
        small_out[1],
        grad_w_qk[None],
        grad_w_value[None],
        grad_w_out[None],
        small_out[2],
        small_out[3],
        grad_w_in[None],
        grad_b_in,
        grad_w_back[None],
        back_out,
    )


def solution(mesh):
    placed = (
        P("section", None, None, "rows", "head"),
        P("section", None),
        P("section", None),
        P("section", None, "head"),
        P("section", None, "head"),
        P("section", "head", None),
        P("section", None),
        P("section", None),
        P("section", None, "head"),
        P("section", "head"),
        P("section", "head", None),
        P("section", "head"),
        P(None, "rows"),
        P(None, None, "rows"),
        P(None, None, "rows"),
    )
    sizes = mesh.shape
    grid_fits = (sizes["section"], sizes["head"], sizes["rows"]) == (2, 4, 4)
    return jax.shard_map(
        parallel_local if grid_fits else local,
        mesh=mesh,
        in_specs=placed,
        out_specs=(
            P("section", None, None, "rows", "head"),
            P("section", None),
            P("section", None),
            P("section", None, "head"),
            P("section", None, "head"),
            P("section", "head", None),
            P("section", None),
            P("section", None),
            P("section", None, "head"),
            P("section", "head"),
            P("section", "head", None),
            P("section", "head"),
        ),
        check_vma=False,
    )
```

```python
import functools

import jax
import jax.numpy as jnp
from jax import lax
from jax.experimental import pallas as pl
from jax.experimental.pallas import tpu as pltpu
from jax.sharding import PartitionSpec as P

HDIM = 128
BLOCK = 64


def from_behind(x, axis, by):
    length = lax.axis_size(axis)
    pairs = [(i, i + by) for i in range(length) if 0 <= i + by < length]
    return lax.ppermute(x, axis, pairs)


def shortened(x):

    def short(part):
        return part.astype(jnp.bfloat16) if part.dtype == jnp.float32 else part

    return jax.tree.map(short, x)


def dot_plain(left_op, right_op):
    return jnp.dot(left_op, right_op, preferred_element_type=jnp.float32)


def dot_right_t(left_op, right_op):
    return lax.dot_general(
        left_op, right_op, (((1,), (1,)), ((), ())), preferred_element_type=jnp.float32
    )


def dot_left_t(left_op, right_op):
    return lax.dot_general(
        left_op, right_op, (((0,), (0,)), ((), ())), preferred_element_type=jnp.float32
    )


def norm_parts(rows_in, norm_gain, norm_shift):
    centre = jnp.mean(rows_in, axis=-1, keepdims=True)
    centred = rows_in - centre
    inv_std = lax.rsqrt(jnp.mean(centred * centred, axis=-1, keepdims=True) + 1e-05)
    scaled = centred * inv_std
    return (scaled * norm_gain + norm_shift, scaled, inv_std)


def norm_back(grad_out, scaled, inv_std, norm_gain):
    grad_scaled = grad_out * norm_gain
    centred_grad = grad_scaled - jnp.mean(grad_scaled, axis=-1, keepdims=True)
    centred_grad = centred_grad - scaled * jnp.mean(grad_scaled * scaled, axis=-1, keepdims=True)
    return (inv_std * centred_grad, jnp.sum(grad_out * scaled, axis=0), jnp.sum(grad_out, axis=0))


def own_columns(full_rows, col_width):
    return lax.dynamic_slice_in_dim(full_rows, lax.axis_index("head") * col_width, col_width, 1)


def full_features(local_rows):
    return lax.all_gather(local_rows, "head", axis=1, tiled=True)


def head_reduce(partial_rows):
    return lax.psum_scatter(partial_rows, "head", scatter_dimension=1, tiled=True)


def grad_features(local_grad):
    return lax.all_gather(local_grad.astype(jnp.bfloat16), "head", axis=1, tiled=True)


def grad_reduce(partial_grad):
    return lax.psum(partial_grad, "head")


def slot_table(slot_ids, seq_rows):
    return (slot_ids[..., None] == jnp.arange(seq_rows, dtype=jnp.int32)).astype(jnp.float32)


def span_blocks(extended, n_blocks):
    blocks = extended.reshape((extended.shape[0], n_blocks + 1, BLOCK) + extended.shape[2:])
    return jnp.concatenate([blocks[:, :-1], blocks[:, 1:]], axis=2)


def fold_blocks(windows):
    front_half = windows[:, :, :BLOCK]
    back_half = windows[:, :, BLOCK:]
    zero_blk = jnp.zeros_like(front_half[:, :1])
    folded = jnp.concatenate([front_half, zero_blk], axis=1) + jnp.concatenate(
        [zero_blk, back_half], axis=1
    )
    return folded.reshape((folded.shape[0], -1) + folded.shape[3:])


def window_scores(gathered, slots, live_prev):
    qv_all, seq_all, bucket_all = gathered
    rounds_n, extended = slots.shape
    n_blocks = extended // BLOCK - 1
    half_width = qv_all.shape[1] // 2
    heads_here = half_width // HDIM
    picked = qv_all[slots]
    query_ext = picked[..., :half_width].reshape(rounds_n, extended, heads_here, HDIM)
    value_ext = picked[..., half_width:].reshape(rounds_n, extended, heads_here, HDIM)
    query_wide = query_ext.astype(jnp.float32)
    inv_norm = lax.rsqrt(jnp.sum(query_wide * query_wide, axis=-1, keepdims=True) + 1e-06)
    key_win = span_blocks((query_wide * inv_norm).astype(jnp.bfloat16), n_blocks)
    value_win = span_blocks(value_ext, n_blocks)
    query_blocks = query_ext[:, BLOCK:].reshape(rounds_n, n_blocks, BLOCK, heads_here, HDIM)
    seq_ext = seq_all[slots]
    bucket_ext = jnp.take_along_axis(bucket_all, slots, axis=1)
    live_ext = jnp.concatenate(
        [
            jnp.broadcast_to(live_prev, (rounds_n, BLOCK)),
            jnp.ones((rounds_n, extended - BLOCK), jnp.bool_),
        ],
        axis=1,
    )

    def query_part(int_table):
        return int_table[:, BLOCK:].reshape(rounds_n, n_blocks, BLOCK)[..., None]

    def key_part(int_table):
        return span_blocks(int_table, n_blocks)[:, :, None, :]

    same_group = key_part(live_ext) & (key_part(seq_ext) == query_part(seq_ext))
    same_group = same_group & (key_part(bucket_ext) == query_part(bucket_ext))
    allowed = same_group & (key_part(slots) < query_part(slots))
    itself = key_part(live_ext) & (key_part(slots) == query_part(slots))
    masking = jnp.where(allowed, 0.0, jnp.where(itself, -100000.0, -1000000000.0)).astype(
        jnp.float32
    )
    scores = jnp.einsum(
        "rcqhd,rckhd->rchqk", query_blocks, key_win, preferred_element_type=jnp.float32
    )
    scores = scores + masking[:, :, None]
    highest = jnp.max(scores, axis=-1, keepdims=True)
    log_total = highest + jnp.log(jnp.sum(jnp.exp(scores - highest), axis=-1, keepdims=True))
    attn_prob = jnp.exp(scores - log_total)
    return (query_wide, inv_norm, query_blocks, key_win, value_win, attn_prob, log_total)


def sorted_forward(gathered, slots, live_prev):
    query_wide, inv_norm, query_blocks, key_win, value_win, attn_prob, log_total = window_scores(
        gathered, slots, live_prev
    )
    rounds_n = slots.shape[0]
    round_mix = jnp.einsum(
        "rchqk,rckhd->rcqhd",
        attn_prob.astype(jnp.bfloat16),
        value_win,
        preferred_element_type=jnp.float32,
    )
    results = round_mix.reshape(rounds_n, -1, round_mix.shape[3] * HDIM)
    round_stats = jnp.transpose(log_total[..., 0], (0, 1, 3, 2)).reshape(
        rounds_n, results.shape[1], -1
    )
    return (results, round_stats)


def to_owners(results, round_stats, own_slots, rows_n):
    rounds_n, tok_rows, feat_width = results.shape
    seq_rows = rows_n * tok_rows
    placing = slot_table(own_slots, seq_rows)
    joined = jnp.concatenate([results, round_stats], axis=-1)
    spread_all = jnp.einsum("rsp,rsf->rpf", placing, joined, precision=lax.Precision.HIGHEST)
    spread_out = spread_all[..., :feat_width]
    spread_stats = spread_all[..., feat_width:]
    back_out, back_stats = (
        lax.all_to_all(
            spread_out.reshape(rounds_n, rows_n, tok_rows, feat_width),
            "rows",
            split_axis=1,
            concat_axis=1,
            tiled=True,
        ),
        lax.all_to_all(
            spread_stats.reshape(rounds_n, rows_n, tok_rows, -1),
            "rows",
            split_axis=1,
            concat_axis=1,
            tiled=True,
        ),
    )
    return (jnp.sum(back_out, axis=1), jnp.sum(back_stats, axis=1))


def sorted_backward(gathered, slots, live_prev, received):
    query_wide, inv_norm, query_blocks, key_win, value_win, attn_prob, log_total = window_scores(
        gathered, slots, live_prev
    )
    grad_all, share_all, stat_all = received
    own_slots = slots[:, BLOCK:]
    rounds_n, n_blocks, heads_here = (attn_prob.shape[0], attn_prob.shape[1], attn_prob.shape[2])
    grad_pick = grad_all[own_slots].reshape(rounds_n, n_blocks, BLOCK, heads_here, HDIM)
    share_pick = jnp.take_along_axis(share_all, own_slots[..., None], axis=1).reshape(
        rounds_n, n_blocks, BLOCK, heads_here
    )
    stat_pick = jnp.take_along_axis(stat_all, own_slots[..., None], axis=1).reshape(
        rounds_n, n_blocks, BLOCK, heads_here
    )
    grad_round = (share_pick[..., None] * grad_pick).astype(jnp.bfloat16)
    grad_prob = jnp.einsum(
        "rcqhd,rckhd->rchqk", grad_round, value_win, preferred_element_type=jnp.float32
    )
    row_dot = jnp.sum(attn_prob * grad_prob, axis=-1, keepdims=True)
    stat_term = jnp.transpose(stat_pick, (0, 1, 3, 2))[..., None]
    grad_scores = (attn_prob * (grad_prob - row_dot + stat_term)).astype(jnp.bfloat16)
    grad_query = jnp.einsum(
        "rchqk,rckhd->rcqhd", grad_scores, key_win, preferred_element_type=jnp.float32
    )
    grad_key = fold_blocks(
        jnp.einsum(
            "rchqk,rcqhd->rckhd", grad_scores, query_blocks, preferred_element_type=jnp.float32
        )
    )
    grad_value = fold_blocks(
        jnp.einsum(
            "rchqk,rcqhd->rckhd",
            attn_prob.astype(jnp.bfloat16),
            grad_round,
            preferred_element_type=jnp.float32,
        )
    )
    norm_cubed = inv_norm * inv_norm * inv_norm
    grad_query_ext = (
        inv_norm * grad_key
        - norm_cubed * jnp.sum(query_wide * grad_key, axis=-1, keepdims=True) * query_wide
    )
    grad_query_own = grad_query.reshape(rounds_n, n_blocks * BLOCK, heads_here, HDIM)
    grad_query_ext = grad_query_ext + jnp.pad(grad_query_own, ((0, 0), (BLOCK, 0), (0, 0), (0, 0)))
    extended = slots.shape[1]
    stacked = jnp.concatenate(
        [
            grad_query_ext.reshape(rounds_n, extended, -1),
            grad_value.reshape(rounds_n, extended, -1),
        ],
        axis=-1,
    )
    placing = slot_table(slots, share_all.shape[1])
    buffer = jnp.einsum("rep,ref->pf", placing, stacked, precision=lax.Precision.HIGHEST)
    return lax.psum_scatter(buffer, "rows", scatter_dimension=0, tiled=True)


def attention_inputs(second_in, params):
    normed, scaled, inv_std = norm_parts(full_features(second_in), params[0], params[1])
    low_in = normed.astype(jnp.bfloat16)
    qv_pairs = jnp.concatenate(
        [dot_plain(low_in, params[2]), dot_plain(low_in, params[3])], axis=1
    ).astype(jnp.bfloat16)
    return (low_in, scaled, inv_std, qv_pairs)


def attention_rounds(qv_pairs, int_here, live_prev, rows_n):
    seq_here, bucket_here, order_here, prev_here = int_here
    gathered = (
        lax.all_gather(qv_pairs, "rows", axis=0, tiled=True),
        lax.all_gather(seq_here, "rows", axis=0, tiled=True),
        lax.all_gather(bucket_here, "rows", axis=1, tiled=True),
    )
    slots = jnp.concatenate([prev_here, order_here], axis=1)
    results, round_stats = sorted_forward(gathered, slots, live_prev)
    owned_out, owned_stats = to_owners(results, round_stats, order_here, rows_n)
    return (gathered, owned_out, owned_stats)


def combine_rounds(owned_out, owned_stats):
    rounds_n, tok_rows, feat_width = owned_out.shape
    heads_here = owned_stats.shape[2]
    top_stat = jnp.max(owned_stats, axis=0, keepdims=True)
    shares = jnp.exp(owned_stats - top_stat)
    shares = shares / jnp.sum(shares, axis=0, keepdims=True)
    mixed_out = jnp.sum(
        shares[..., None] * owned_out.reshape(rounds_n, tok_rows, heads_here, HDIM), axis=0
    )
    return (mixed_out.reshape(tok_rows, feat_width).astype(jnp.bfloat16), shares)


def ffn_forward(first_out, params):
    normed, scaled, inv_std = norm_parts(full_features(first_out), params[5], params[6])
    low_in = normed.astype(jnp.bfloat16)
    pre_act = dot_plain(low_in, params[7]) + params[8]
    active = jax.nn.gelu(pre_act).astype(jnp.bfloat16)
    branch = head_reduce(dot_plain(active, params[9])) + params[10]
    return (branch, (low_in, scaled, inv_std, pre_act, active))


def layer_forward(first_in, second_in, params, int_here, live_prev, rows_n):
    low_in, scaled, inv_std, qv_pairs = attention_inputs(second_in, params)
    kept_state = attention_rounds(qv_pairs, int_here, live_prev, rows_n)
    mixed_low, shares = combine_rounds(kept_state[1], kept_state[2])
    first_out = first_in + head_reduce(dot_plain(mixed_low, params[4]))
    second_out = second_in + ffn_forward(first_out, params)[0]
    return (first_out, second_out, kept_state)


def layer_backward(first_out, second_out, grad_one, grad_two, params, int_here, live_prev, rows_n):
    ffn_branch, (ffn_low, ffn_scaled, ffn_inv, pre_act, active) = ffn_forward(first_out, params)
    second_in = second_out - ffn_branch
    grad_full = grad_features(grad_two)
    gelu_value, gelu_pull = jax.vjp(jax.nn.gelu, pre_act)
    grad_pre = gelu_pull(dot_right_t(grad_full, params[9]))[0].astype(jnp.bfloat16)
    grad_w_back = dot_left_t(active, grad_full)
    grad_b_back = jnp.sum(grad_two, axis=0)
    grad_w_in = dot_left_t(ffn_low, grad_pre)
    grad_b_in = jnp.sum(grad_pre.astype(jnp.float32), axis=0)
    grad_normed = grad_reduce(dot_right_t(grad_pre, params[7]))
    grad_rows, grad_ffn_gain, grad_ffn_shift = norm_back(
        grad_normed, ffn_scaled, ffn_inv, params[5]
    )
    grad_one = grad_one + own_columns(grad_rows, grad_one.shape[1])
    low_in, scaled, inv_std, qv_pairs = attention_inputs(second_in, params)
    state_here = attention_rounds(qv_pairs, int_here, live_prev, rows_n)
    gathered, owned_out, owned_stats = state_here
    mixed_low, shares = combine_rounds(owned_out, owned_stats)
    first_in = first_out - head_reduce(dot_plain(mixed_low, params[4]))
    grad_full = grad_features(grad_one)
    grad_w_out = dot_left_t(mixed_low, grad_full)
    grad_mixed = dot_right_t(grad_full, params[4]).astype(jnp.bfloat16)
    rounds_n, tok_rows, heads_here = owned_stats.shape
    grad_wide = grad_mixed.astype(jnp.float32)
    per_round = jnp.sum(
        grad_wide.reshape(1, tok_rows, heads_here, HDIM)
        * owned_out.reshape(rounds_n, tok_rows, heads_here, HDIM),
        axis=-1,
    )
    grad_stats = shares * (per_round - jnp.sum(shares * per_round, axis=0, keepdims=True))
    received = (
        lax.all_gather(grad_wide, "rows", axis=0, tiled=True),
        lax.all_gather(shares, "rows", axis=1, tiled=True),
        lax.all_gather(grad_stats, "rows", axis=1, tiled=True),
    )
    slots = jnp.concatenate([int_here[3], int_here[2]], axis=1)
    owned_grad = sorted_backward(gathered, slots, live_prev, received)
    qk_width = grad_mixed.shape[1]
    grad_query = owned_grad[:, :qk_width].astype(jnp.bfloat16)
    grad_value = owned_grad[:, qk_width:].astype(jnp.bfloat16)
    grad_w_qk = dot_left_t(low_in, grad_query)
    grad_w_value = dot_left_t(low_in, grad_value)
    grad_normed = grad_reduce(
        dot_right_t(grad_query, params[2]) + dot_right_t(grad_value, params[3])
    )
    grad_rows, grad_attn_gain, grad_attn_shift = norm_back(grad_normed, scaled, inv_std, params[0])
    grad_second = grad_two + own_columns(grad_rows, grad_two.shape[1])
    grads = (
        grad_attn_gain,
        grad_attn_shift,
        grad_w_qk,
        grad_w_value,
        grad_w_out,
        grad_ffn_gain,
        grad_ffn_shift,
        grad_w_in,
        grad_b_in,
        grad_w_back,
        grad_b_back,
    )
    return (first_in, second_in, grad_one, grad_second, grads)


def local(
    stream_in,
    attn_gain,
    attn_shift,
    w_qk,
    w_value,
    w_out,
    ffn_gain,
    ffn_shift,
    w_in,
    b_in,
    w_back,
    b_back,
    seq_ids,
    bucket_ids,
    sort_order,
):
    section_pos = lax.axis_index("section")
    is_first = section_pos == 0
    rows_n = lax.axis_size("rows")
    live_prev = lax.axis_index("rows") > 0
    micro_n = stream_in.shape[2]
    params = tuple(
        (
            weight_arr[0]
            for weight_arr in (
                attn_gain,
                attn_shift,
                w_qk,
                w_value,
                w_out,
                ffn_gain,
                ffn_shift,
                w_in,
                b_in,
                w_back,
                b_back,
            )
        )
    )
    prev_all = from_behind(sort_order[:, :, sort_order.shape[2] - BLOCK :], "rows", 1)
    own_stream = stream_in[0].astype(jnp.float32)

    def pick_batch(int_table, batch_no):
        return lax.dynamic_index_in_dim(int_table, batch_no, 0, keepdims=False)

    def ints_for(batch_no):
        return (
            pick_batch(seq_ids, batch_no),
            pick_batch(bucket_ids, batch_no),
            pick_batch(sort_order, batch_no),
            pick_batch(prev_all, batch_no),
        )

    message = jnp.zeros_like(own_stream[:, 0])
    outputs_fwd = []
    kept_list = []
    for tick_no in range(micro_n + 1):
        batch_no = jnp.clip(tick_no - section_pos, 0, micro_n - 1)
        source = jnp.where(is_first, own_stream[:, min(tick_no, micro_n - 1)], message)
        first_out, second_out, kept_state = layer_forward(
            source[0], source[1], params, ints_for(batch_no), live_prev, rows_n
        )
        outputs_fwd.append(jnp.stack([first_out, second_out]))
        kept_list.append(kept_state)
        if tick_no < micro_n:
            message = from_behind(outputs_fwd[-1], "section", 1)
    grads_total = tuple((jnp.zeros(weight_arr.shape, jnp.float32) for weight_arr in params))
    back_msg = jnp.zeros((4,) + own_stream.shape[2:], jnp.float32)
    dx_list = []
    for tick_no in range(micro_n + 1):
        batch_raw = tick_no - 1 + section_pos
        is_live = (batch_raw >= 0) & (batch_raw < micro_n)
        batch_no = jnp.clip(batch_raw, 0, micro_n - 1)
        outs_here = jnp.where(is_first, back_msg[:2], outputs_fwd[min(tick_no + 1, micro_n)])
        grads_here = jnp.where(is_first, back_msg[2:], own_stream[:, min(tick_no, micro_n - 1)])
        first_in, second_in, grad_first, grad_second, grads = layer_backward(
            outs_here[0],
            outs_here[1],
            grads_here[0],
            grads_here[1],
            params,
            ints_for(batch_no),
            live_prev,
            rows_n,
        )
        dx_list.append(jnp.stack([grad_first, grad_second]))
        grads = tuple((jnp.where(is_live, grad_one, 0.0) for grad_one in grads))
        grads_total = tuple(
            (total_one + grad_one for total_one, grad_one in zip(grads_total, grads))
        )
        if tick_no < micro_n:
            back_msg = from_behind(
                jnp.stack([first_in, second_in, grad_first, grad_second]), "section", -1
            )
    grads_total = jax.tree.map(
        lambda part: part.astype(jnp.float32), lax.psum(shortened(grads_total), "rows")
    )
    stream_out = jnp.where(
        is_first, jnp.stack(dx_list[1:], axis=1), jnp.stack(outputs_fwd[1:], axis=1)
    )[None]
    return (
        stream_out,
        grads_total[0][None],
        grads_total[1][None],
        grads_total[2][None],
        grads_total[3][None],
        grads_total[4][None],
        grads_total[5][None],
        grads_total[6][None],
        grads_total[7][None],
        grads_total[8][None],
        grads_total[9][None],
        grads_total[10][None],
    )


VMEM_ROOM = 32 * 1024 * 1024
WHOLE_VMEM = 64 * 1024 * 1024
TILE = 128
GELU_C = 0.7978845608
BIAS_ROWS = (5, 6, 7, 13)


def kernel_call(
    body, out_types, args, scalars=None, scratch=(), flops=0, hbm=(), after=(), label=None, mark=False, room=VMEM_ROOM
):
    n_in = len(args) + len(hbm)
    specs = [pl.BlockSpec(memory_space=pltpu.VMEM) for _ in args]
    specs = specs + [pl.BlockSpec(memory_space=pl.ANY) for _ in (*hbm, *after)]
    args = (*args, *hbm, *after)
    if scalars is not None:
        args = (scalars, *args)
        specs = [pl.BlockSpec(memory_space=pltpu.SMEM)] + specs
        n_in += 1
    n_out = len(out_types)
    if mark:
        out_types = [*out_types, ((8, 128), jnp.float32)]
    outs = tuple(jax.ShapeDtypeStruct(shape, dtype) for shape, dtype in out_types)
    moved = sum(a.size * a.dtype.itemsize for a in (*args[: len(args) - len(after)], *outs))

    def run(*refs):
        first_out = n_in + len(after)
        last_out = first_out + n_out
        if mark:
            refs[last_out][...] = jnp.zeros((8, 128), jnp.float32)
        rest = refs[last_out + (1 if mark else 0) :]
        body(*refs[:n_in], *refs[first_out:last_out], *rest)

    return pl.pallas_call(
        run,
        out_shape=outs,
        in_specs=specs,
        out_specs=tuple(pl.BlockSpec(memory_space=pltpu.VMEM) for _ in outs),
        scratch_shapes=list(scratch),
        name=label,
        compiler_params=pltpu.CompilerParams(vmem_limit_bytes=room),
        cost_estimate=pl.CostEstimate(flops=flops, bytes_accessed=moved, transcendentals=0),
    )(*args)


def flip_pairs(n, by):
    return [(i, i ^ by) for i in range(n)]


def swap_cores(x):
    return lax.ppermute(x, "section", [(0, 1), (1, 0)])


def xor_recv(parts, axis):
    return [lax.ppermute(part, axis, flip_pairs(4, k + 1)) for k, part in enumerate(parts)]


def xor_recv_core(parts, core):
    got = []
    for k, part in enumerate(parts):
        pairs = [(core * 4 + i, core * 4 + (i ^ (k + 1))) for i in range(4)]
        got.append(lax.ppermute(part, ("section", "rows"), pairs))
    return got


def gather_four(own, axis):
    return [own] + xor_recv([own] * 3, axis)


def both_halves(near):
    return near + [swap_cores(part) for part in near]


def gather_tokens(own, axis):
    return both_halves(gather_four(own, axis))


def scatter_tokens(far_part, near_part, axis):
    arrived = swap_cores(far_part)
    n_own = near_part.shape[0] // 4
    width = near_part.shape[1]

    def body(near, far, *outs):
        for k in range(4):
            rows = pl.ds(k * n_own, n_own)
            total = near[rows, :].astype(jnp.float32) + far[rows, :].astype(jnp.float32)
            outs[k][...] = total.astype(outs[k].dtype)

    kept, *sent = kernel_call(
        body,
        [((n_own, width), jnp.float32)] + [((n_own, width), jnp.bfloat16)] * 3,
        (near_part, arrived),
        label="scatter_tokens",
    )
    return [kept] + xor_recv(sent, axis)


def rows_norm(rows_in):
    centred = rows_in - jnp.mean(rows_in, axis=-1, keepdims=True)
    inv_std = lax.rsqrt(jnp.mean(centred * centred, axis=-1, keepdims=True) + 1e-05)
    return centred * inv_std, inv_std


def sum_parts(parts):
    total = parts[0][...]
    for part in parts[1:]:
        total = total + part[...].astype(jnp.float32)
    return total


def residual_norm(resid, parts, after, vectors, rows, shifts=None):
    n_own, width = resid.shape
    n_shift = 0 if shifts is None else 1

    def body(resid, vectors, p0, p1, p2, p3, *refs):
        total = resid[...] + sum_parts((p0, p1, p2, p3))
        if n_shift:
            total = total + refs[0][shifts[1] : shifts[1] + 1, :]
        refs[n_shift][...] = total
        if rows is not None:
            scaled, _ = rows_norm(total)
            gain, shift = (vectors[i : i + 1, :] for i in rows)
            refs[n_shift + 1][...] = (scaled * gain + shift).astype(jnp.bfloat16)

    types = [((n_own, width), jnp.float32)]
    if rows is not None:
        types.append(((n_own, width), jnp.bfloat16))
    return kernel_call(
        body,
        types,
        (resid, vectors, *parts) + (() if shifts is None else (shifts[0],)),
        after=after,
        label="residual_norm",
    )


def norm_backward(resid, parts, stream, vectors, row, after):
    n_own, width = resid.shape

    def body(resid, stream, vectors, p0, p1, p2, p3, out, low, small):
        gain = vectors[row : row + 1, :]
        grad_out = sum_parts((p0, p1, p2, p3))
        scaled, inv_std = rows_norm(stream[...])
        grad_scaled = grad_out * gain
        centred = grad_scaled - jnp.mean(grad_scaled, axis=-1, keepdims=True)
        centred = centred - scaled * jnp.mean(grad_scaled * scaled, axis=-1, keepdims=True)
        total = resid[...] + inv_std * centred
        out[...] = total
        low[...] = total.astype(jnp.bfloat16)
        small[0:1, :] = jnp.sum(grad_out * scaled, axis=0, keepdims=True)
        small[1:2, :] = jnp.sum(grad_out, axis=0, keepdims=True)
        small[2:3, :] = jnp.sum(total, axis=0, keepdims=True)
        small[3:8, :] = jnp.zeros((5, width), jnp.float32)

    return kernel_call(
        body,
        [
            ((n_own, width), jnp.float32),
            ((n_own, width), jnp.bfloat16),
            ((8, width), jnp.float32),
        ],
        (resid, stream, vectors, *parts),
        after=after,
        label="norm_backward",
    )


def join_tokens(parts, tokens):
    rows = parts[0].shape[0]
    for k, part in enumerate(parts):
        tokens[pl.ds(k * rows, rows), :] = part[...]


def attention_forward(layer, pieces, qv_pair, out_pair, masking):
    n_own, width = pieces[0].shape
    n_tok = 8 * n_own
    half = n_tok // 2
    dim = out_pair[0].shape[0]

    def body(*refs):
        masking, own_qv, got_qv, own_out, got_out, *refs_out = refs[8:]
        far_part, near_part, tokens, qv, prob, mixed, keys, w_qv, w_out, sems = refs_out
        sources = ((own_qv, got_qv), (own_out, got_out))
        waits = fetch_layer(layer, sources, (w_qv, w_out), sems)
        join_tokens(refs[:8], tokens)
        waits[0].wait()
        for start in range(0, n_tok, TILE):
            rows = pl.ds(start, TILE)
            low = dot_plain(tokens[rows, :], w_qv[...]).astype(jnp.bfloat16)
            qv[rows, :] = low
            query = low[:, :dim].astype(jnp.float32)
            inv = lax.rsqrt(jnp.sum(query * query, axis=-1, keepdims=True) + 1e-06)
            keys[rows, :] = (query * inv).astype(jnp.bfloat16)
        for start in range(0, n_tok, TILE):
            rows = pl.ds(start, TILE)
            scores = dot_right_t(qv[rows, :dim], keys[...]) + masking[rows, :]
            scores = jnp.exp(scores - jnp.max(scores, axis=-1, keepdims=True))
            total = jnp.sum(scores, axis=-1, keepdims=True)
            low = (scores * (1.0 / total)).astype(jnp.bfloat16)
            prob[rows, :] = low
            mix = dot_plain(low, qv[:, dim:]).astype(jnp.bfloat16)
            mixed[rows, :] = mix
            if start == 0:
                waits[1].wait()
            part = dot_plain(mix, w_out[...])
            if start < half:
                near_part[rows, :] = part.astype(jnp.bfloat16)
            else:
                far_part[pl.ds(start - half, TILE), :] = part.astype(jnp.bfloat16)

    return kernel_call(
        body,
        [
            ((half, width), jnp.bfloat16),
            ((half, width), jnp.bfloat16),
            ((n_tok, width), jnp.bfloat16),
            ((n_tok, 2 * dim), jnp.bfloat16),
            ((n_tok, n_tok), jnp.bfloat16),
            ((n_tok, dim), jnp.bfloat16),
        ],
        (*pieces, masking),
        hbm=(*qv_pair, *out_pair),
        scratch=[
            pltpu.VMEM((n_tok, dim), jnp.bfloat16),
            pltpu.VMEM((width, 2 * dim), jnp.bfloat16),
            pltpu.VMEM((dim, width), jnp.bfloat16),
            pltpu.SemaphoreType.DMA((2,)),
        ],
        flops=2 * n_tok * (3 * width * dim + 2 * n_tok * dim),
        label="attention_forward",
    )


def attention_backward(layer, pieces, qv_pair, out_pair, qv, prob, after):
    n_own, width = pieces[0].shape
    n_tok = 8 * n_own
    half = n_tok // 2
    dim = out_pair[0].shape[0]

    def body(*refs):
        qv, prob, own_qv, got_qv, own_out, got_out, *refs_out = refs[8:]
        far_part, near_part, tokens, dqv, keys, dmix, dscore, dquery, w_qv, w_out, sems = refs_out
        sources = ((own_out, got_out), (own_qv, got_qv))
        waits = fetch_layer(layer, sources, (w_out, w_qv), sems)
        join_tokens(refs[:8], tokens)
        waits[0].wait()
        for start in range(0, n_tok, TILE):
            rows = pl.ds(start, TILE)
            dmix[rows, :] = dot_right_t(tokens[rows, :], w_out[...]).astype(jnp.bfloat16)
            query = qv[rows, :dim].astype(jnp.float32)
            inv = lax.rsqrt(jnp.sum(query * query, axis=-1, keepdims=True) + 1e-06)
            keys[rows, :] = (query * inv).astype(jnp.bfloat16)
        for start in range(0, n_tok, TILE):
            rows = pl.ds(start, TILE)
            dprob = dot_right_t(dmix[rows, :], qv[:, dim:])
            weights = prob[rows, :].astype(jnp.float32)
            centre = jnp.sum(weights * dprob, axis=-1, keepdims=True)
            low = (weights * (dprob - centre)).astype(jnp.bfloat16)
            dscore[rows, :] = low
            dquery[rows, :] = dot_plain(low, keys[...])
        waits[1].wait()
        for start in range(0, n_tok, TILE):
            rows = pl.ds(start, TILE)
            dkey = dot_left_t(dscore[:, rows], qv[:, :dim])
            dval = dot_left_t(prob[:, rows], dmix[...])
            query = qv[rows, :dim].astype(jnp.float32)
            inv = lax.rsqrt(jnp.sum(query * query, axis=-1, keepdims=True) + 1e-06)
            along = jnp.sum(query * dkey, axis=-1, keepdims=True)
            total = dquery[rows, :] + inv * dkey - inv * inv * inv * along * query
            low = jnp.concatenate(
                [total.astype(jnp.bfloat16), dval.astype(jnp.bfloat16)], axis=1
            )
            dqv[rows, :] = low
            part = dot_right_t(low, w_qv[...])
            if start < half:
                near_part[rows, :] = part.astype(jnp.bfloat16)
            else:
                far_part[pl.ds(start - half, TILE), :] = part.astype(jnp.bfloat16)

    return kernel_call(
        body,
        [
            ((half, width), jnp.bfloat16),
            ((half, width), jnp.bfloat16),
            ((n_tok, width), jnp.bfloat16),
            ((n_tok, 2 * dim), jnp.bfloat16),
        ],
        (*pieces, qv, prob),
        hbm=(*qv_pair, *out_pair),
        after=after,
        scratch=[
            pltpu.VMEM((n_tok, dim), jnp.bfloat16),
            pltpu.VMEM((n_tok, dim), jnp.bfloat16),
            pltpu.VMEM((n_tok, n_tok), jnp.bfloat16),
            pltpu.VMEM((n_tok, dim), jnp.float32),
            pltpu.VMEM((width, 2 * dim), jnp.bfloat16),
            pltpu.VMEM((dim, width), jnp.bfloat16),
            pltpu.SemaphoreType.DMA((2,)),
        ],
        flops=2 * n_tok * (3 * width * dim + 4 * n_tok * dim),
        label="attention_backward",
    )


def fetch_layer(layer, sources, targets, sems):
    held_here = lax.axis_index("section") == layer

    @pl.when(held_here)
    def _():
        for i, (own, _) in enumerate(sources):
            pltpu.make_async_copy(own, targets[i], sems.at[i]).start()

    @pl.when(jnp.logical_not(held_here))
    def _():
        for i, (_, got) in enumerate(sources):
            pltpu.make_async_copy(got, targets[i], sems.at[i]).start()

    return [
        pltpu.make_async_copy(own, targets[i], sems.at[i]) for i, (own, _) in enumerate(sources)
    ]


def scattered_types(n_own, width):
    return [((n_own, width), jnp.float32)] + [((n_own, width), jnp.bfloat16)] * 3


def store_scattered(outs, start, part):
    n_own = outs[0].shape[0]
    for at in range(0, part.shape[0], n_own):
        out = outs[(start + at) // n_own]
        out[...] = part[at : at + n_own, :].astype(out.dtype)


def feed_forward(layer, pieces, vectors, row, w_in, w_back):
    n_own, width = pieces[0].shape
    n_tok = 4 * n_own
    hidden = w_in[0].shape[1]

    def body(*refs):
        vectors, own_in, got_in, own_back, got_back = refs[4:9]
        bias = vectors[row : row + 1, :]
        outs, (tokens, active, slope, wide_in, wide_back, sems) = refs[9:13], refs[13:]
        sources = ((own_in, got_in), (own_back, got_back))
        waits = fetch_layer(layer, sources, (wide_in, wide_back), sems)
        join_tokens(refs[:4], tokens)
        waits[0].wait()
        for start in range(0, n_tok, TILE):
            rows = pl.ds(start, TILE)
            pre = dot_plain(tokens[rows, :], wide_in[...]) + bias
            square = pre * pre
            bent = jnp.tanh(GELU_C * (pre + 0.044715 * pre * square))
            low = (0.5 * pre * (1.0 + bent)).astype(jnp.bfloat16)
            active[rows, :] = low
            slope[rows, :] = 0.5 * (1.0 + bent) + 0.5 * pre * (1.0 - bent * bent) * (
                GELU_C * (1.0 + 3.0 * 0.044715 * square)
            )
            if start == 0:
                waits[1].wait()
            store_scattered(outs, start, dot_plain(low, wide_back[...]))

    outs = kernel_call(
        body,
        scattered_types(n_own, width)
        + [
            ((n_tok, width), jnp.bfloat16),
            ((n_tok, hidden), jnp.bfloat16),
            ((n_tok, hidden), jnp.float32),
        ],
        (*pieces, vectors),
        hbm=(*w_in, *w_back),
        scratch=[
            pltpu.VMEM((width, hidden), jnp.bfloat16),
            pltpu.VMEM((hidden, width), jnp.bfloat16),
            pltpu.SemaphoreType.DMA((2,)),
        ],
        flops=4 * n_tok * width * hidden,
        label="feed_forward",
    )
    return outs[:4], outs[4], outs[5], outs[6]


def feed_backward(layer, pieces, slope, w_in, w_back, after):
    n_own, width = pieces[0].shape
    n_tok = 4 * n_own
    hidden = slope.shape[1]

    def body(*refs):
        slope, own_in, got_in, own_back, got_back = refs[4:9]
        outs, (tokens, dpre, wide_in, wide_back, sems) = refs[9:13], refs[13:]
        sources = ((own_back, got_back), (own_in, got_in))
        waits = fetch_layer(layer, sources, (wide_back, wide_in), sems)
        join_tokens(refs[:4], tokens)
        waits[0].wait()
        for start in range(0, n_tok, TILE):
            rows = pl.ds(start, TILE)
            grad = dot_right_t(tokens[rows, :], wide_back[...]) * slope[rows, :]
            low = grad.astype(jnp.bfloat16)
            dpre[rows, :] = low
            if start == 0:
                waits[1].wait()
            store_scattered(outs, start, dot_right_t(low, wide_in[...]))

    outs = kernel_call(
        body,
        scattered_types(n_own, width)
        + [((n_tok, width), jnp.bfloat16), ((n_tok, hidden), jnp.bfloat16)],
        (*pieces, slope),
        hbm=(*w_in, *w_back),
        after=after,
        scratch=[
            pltpu.VMEM((width, hidden), jnp.bfloat16),
            pltpu.VMEM((hidden, width), jnp.bfloat16),
            pltpu.SemaphoreType.DMA((2,)),
        ],
        flops=4 * n_tok * width * hidden,
        label="feed_backward",
    )
    return outs[:4], outs[4], outs[5]


def feed_grads(coords, norm_in, grad_in, active, dpre, turned, after):
    n_tok, width = norm_in.shape
    hidden = active.shape[1]
    in_rows, back_rows = width // 8, hidden // 8
    shape = (4, in_rows + back_rows + (16 if turned else 0), width)

    def body(coords, norm_in, grad_in, active, dpre, *outs):
        bias = jnp.sum(dpre[...].astype(jnp.float32), axis=0, keepdims=True)
        tail = jnp.concatenate([bias, jnp.zeros((15, hidden), jnp.float32)], axis=0)
        if not turned:
            outs[1][...] = tail[0:8, :]
        for k in range(4):
            for part in range(2):
                chunk, half = (coords[2] ^ k, coords[0] ^ part) if turned else (k, part)
                at = 2 * chunk + half
                out = outs[part] if turned else outs[0].at[part]
                cols = pl.ds(pl.multiple_of(at * in_rows, in_rows), in_rows)
                out[k, :in_rows, :] = dot_left_t(norm_in[:, cols], dpre[...]).astype(jnp.bfloat16)
                cols = pl.ds(pl.multiple_of(at * back_rows, back_rows), back_rows)
                out[k, in_rows : in_rows + back_rows, :] = dot_left_t(
                    active[:, cols], grad_in[...]
                ).astype(jnp.bfloat16)
                if turned:
                    out[k, in_rows + back_rows :, :] = tail.astype(jnp.bfloat16)

    return kernel_call(
        body,
        [(shape, jnp.bfloat16)] * 2
        if turned
        else [((2,) + shape, jnp.bfloat16), ((8, hidden), jnp.float32)],
        (norm_in, grad_in, active, dpre),
        scalars=coords,
        after=after,
        flops=4 * n_tok * width * hidden,
        label="feed_grads",
        mark=True,
    )


def add_cores(parts, other, after):
    shape = parts.shape[1:]

    def body(parts, other, *outs):
        for k in range(4):
            total = parts[k].astype(jnp.float32) + other[k].astype(jnp.float32)
            outs[k][...] = total.astype(jnp.bfloat16)

    return kernel_call(
        body, [(shape, jnp.bfloat16)] * 4, (parts, other), after=after, label="add_cores", mark=True
    )


def permute_one(x, by):
    return lax.ppermute(x, "rows", flip_pairs(4, by))


def sum_four(parts):
    total = parts[0][...].astype(jnp.float32) + parts[1][...].astype(jnp.float32)
    return total + parts[2][...].astype(jnp.float32) + parts[3][...].astype(jnp.float32)


def add_four(parts, after, label):
    def body(p0, p1, p2, p3, out):
        out[...] = sum_four((p0, p1, p2, p3)).astype(jnp.bfloat16)

    return kernel_call(
        body, [(parts[0].shape, jnp.bfloat16)], parts, after=after, label=label, mark=True
    )


def pair_heads(coords, own_low, own_high):
    shape = own_low.shape

    def split_body(coords, own_low, own_high, kept, sent):
        is_low = coords[0] == 0
        kept[...] = jnp.where(is_low, own_low[...], own_high[...])
        sent[...] = jnp.where(is_low, own_high[...], own_low[...])

    kept, sent = kernel_call(
        split_body,
        [(shape, own_low.dtype)] * 2,
        (own_low, own_high),
        scalars=coords,
        label="split_heads",
    )

    def join_body(coords, kept, got, out):
        out[coords[0]] = kept[...]
        out[1 - coords[0]] = got[...]

    return kernel_call(
        join_body,
        [((2,) + shape, own_low.dtype)],
        (kept, swap_cores(sent)),
        scalars=coords,
        label="join_heads",
    )[0]


def head_grads(coords, norm_in, grad_in, mixed, dqv, after):
    n_tok, width = norm_in.shape
    dim = mixed.shape[1]
    part = width // 4

    def body(coords, norm_in, grad_in, mixed, dqv, *outs):
        for k in range(4):
            cols = pl.ds(pl.multiple_of((coords[2] ^ k) * part, part), part)
            outs[k][:part, :] = dot_left_t(norm_in[:, cols], dqv[...]).astype(jnp.bfloat16)
            outs[k][part:, :] = dot_left_t(mixed[...], grad_in[:, cols]).astype(jnp.bfloat16)

    return kernel_call(
        body,
        [((part + dim, part), jnp.bfloat16)] * 4,
        (norm_in, grad_in, mixed, dqv),
        scalars=coords,
        after=after,
        flops=2 * n_tok * width * 3 * dim,
        label="head_grads",
        mark=True,
    )


def to_layer(parts, layer, after):
    def body(p0, p1, p2, p3, out):
        for k, part in enumerate((p0, p1, p2, p3)):
            out[k] = part[...]

    whole, mark = kernel_call(
        body,
        [((4,) + parts[0].shape, parts[0].dtype)],
        parts,
        after=after,
        label="pack_four",
        mark=True,
    )
    return (whole, lax.ppermute(whole, "section", [(1 - layer, layer)])), mark


def place_heads(coords, parts, dim):
    _, rows, part = parts[0].shape

    def body(coords, p0, p1, p2, p3, w_qk, w_value, w_out):
        for k, piece in enumerate((p0, p1, p2, p3)):
            there = pl.ds(pl.multiple_of((coords[2] ^ k) * part, part), part)
            for head in range(2):
                here = slice(head * dim, (head + 1) * dim)
                value = piece[head].astype(jnp.float32)
                w_qk[there, here] = value[:part, :dim]
                w_value[there, here] = value[:part, dim:]
                w_out[here, there] = value[part:, :]

    f32 = jnp.float32
    return kernel_call(
        body,
        [((4 * part, 2 * dim), f32)] * 2 + [((2 * dim, 4 * part), f32)],
        parts,
        scalars=coords,
        label="place_heads",
        mark=True,
    )


def place_hidden(coords, low_hidden, high_layer, bias_low, after):
    low_rows, width = low_hidden.shape[2:]
    block = low_rows // 2
    feed_rows = low_rows + 16

    def body(coords, bias_low, hidden, *refs):
        high = refs[:2]
        w_in, w_back, b_in, held, wide, in_sems, out_sems = refs[2 + len(after) :]
        is_low = coords[0] == 0

        @pl.when(is_low)
        def _():
            for i in range(8):
                there = held.at[i, pl.ds(0, low_rows)]
                source = hidden.at[i // 4, coords[2] ^ (i % 4)]
                pltpu.make_async_copy(source, there, in_sems.at[i]).start()

        @pl.when(jnp.logical_not(is_low))
        def _():
            for i in range(8):
                there = held.at[i]
                source = high[i // 4].at[i % 4]
                pltpu.make_async_copy(source, there, in_sems.at[i]).start()

        sends = []
        for i in range(8):

            @pl.when(is_low)
            def _():
                there = held.at[i, pl.ds(0, low_rows)]
                pltpu.make_async_copy(hidden.at[0, 0], there, in_sems.at[i]).wait()

            @pl.when(jnp.logical_not(is_low))
            def _():
                pltpu.make_async_copy(high[0].at[0], held.at[i], in_sems.at[i]).wait()

            half = (i // 4) ^ coords[0]
            chunk = coords[2] ^ (i % 4)
            there = pl.ds(pl.multiple_of((2 * chunk + half) * block, block), block)
            for j, out in enumerate((w_in, w_back)):
                wide[i, j] = held[i, pl.ds(j * block, block), :].astype(jnp.float32)
                sends.append(
                    pltpu.make_async_copy(wide.at[i, j], out.at[there, :], out_sems.at[2 * i + j])
                )
                sends[-1].start()
        tail = held[0, pl.ds(2 * block, 16), :].astype(jnp.float32)[0:1, :]
        b_in[...] = jnp.where(is_low, bias_low[...], tail)
        for send in sends:
            send.wait()

    f32 = jnp.float32
    outs = [((width, width), f32), ((8 * block, width), f32), ((1, width), f32)]
    spaces = [pltpu.HBM, pltpu.HBM, pltpu.VMEM]
    return pl.pallas_call(
        body,
        out_shape=tuple(jax.ShapeDtypeStruct(*out) for out in outs),
        in_specs=[
            pl.BlockSpec(memory_space=pltpu.SMEM),
            pl.BlockSpec(memory_space=pltpu.VMEM),
        ]
        + [pl.BlockSpec(memory_space=pltpu.HBM)] * 3
        + [pl.BlockSpec(memory_space=pl.ANY)] * len(after),
        out_specs=tuple(pl.BlockSpec(memory_space=space) for space in spaces),
        scratch_shapes=[
            pltpu.VMEM((8, feed_rows, width), jnp.bfloat16),
            pltpu.VMEM((8, 2, block, width), f32),
            pltpu.SemaphoreType.DMA((8,)),
            pltpu.SemaphoreType.DMA((16,)),
        ],
        name="place_hidden",
        compiler_params=pltpu.CompilerParams(vmem_limit_bytes=WHOLE_VMEM),
    )(coords, bias_low, low_hidden, *high_layer, *after)


def split_three(value):
    first = value.astype(jnp.bfloat16).astype(jnp.float32)
    rest = value - first
    second = rest.astype(jnp.bfloat16).astype(jnp.float32)
    return jnp.concatenate(
        [first, second, rest - second, jnp.zeros((13, value.shape[1]), jnp.float32)], axis=0
    ).astype(jnp.bfloat16)


def own_weights(w_qk, w_value, w_out, rows, after):
    width, cols = w_qk.shape[1:]
    dim = cols // 2
    dtype = w_qk.dtype

    def body(w_qk, w_value, w_out, *refs):
        sources = refs[: len(rows)]
        qv_mine, qv_other, out_mine, out_other, vectors, sems, row_sems = refs[len(rows) :]
        core = lax.axis_index("section")
        copies = []
        for side, (qv, out) in enumerate(((qv_mine, out_mine), (qv_other, out_other))):
            which = core if side == 0 else 1 - core
            here = pl.ds(pl.multiple_of(which * dim, dim), dim)
            for i, (source, target) in enumerate(
                (
                    (w_qk.at[0, :, here], qv.at[:, pl.ds(0, dim)]),
                    (w_value.at[0, :, here], qv.at[:, pl.ds(dim, dim)]),
                    (w_out.at[0, here, :], out),
                )
            ):
                copies.append(pltpu.make_async_copy(source, target, sems.at[3 * side + i]))
        vectors[...] = jnp.zeros(vectors.shape, jnp.float32)
        for i, source in enumerate(sources):
            there = vectors.at[pl.ds(i, 1), pl.ds(0, source.shape[1])]
            copies.append(pltpu.make_async_copy(source, there, row_sems.at[i]))
        for copy in copies:
            copy.start()
        for copy in copies:
            copy.wait()

    return kernel_call(
        body,
        [((width, cols), dtype)] * 2 + [((dim, width), dtype)] * 2 + [((8, width), jnp.float32)],
        (),
        hbm=(w_qk, w_value, w_out, *rows),
        after=after,
        scratch=[pltpu.SemaphoreType.DMA((6,)), pltpu.SemaphoreType.DMA((len(rows),))],
        label="own_weights",
        room=WHOLE_VMEM,
    )


def batch_parts(stream, seq_ids, bucket_ids):
    _, n_val, micro_n, tok_rows, feats = stream.shape
    rounds_n = bucket_ids.shape[1]
    base = n_val * tok_rows
    per_row = feats // tok_rows

    def body(seq_ids, bucket_ids, stream, out, sems):
        copies = []
        for m in range(micro_n):
            for i in range(n_val):
                there = out.at[m, pl.ds(i * tok_rows, tok_rows)]
                copies.append(
                    pltpu.make_async_copy(stream.at[0, i, m], there, sems.at[n_val * m + i])
                )
                copies[-1].start()
        for m in range(micro_n):
            tables = [seq_ids[m : m + 1, :]]
            tables += [bucket_ids[m, r : r + 1, :] for r in range(rounds_n)]
            tables = [table.astype(jnp.float32) for table in tables]
            while len(tables) % per_row:
                tables.append(jnp.zeros((1, tok_rows), jnp.float32))
            rows = [
                jnp.concatenate(tables[i : i + per_row], axis=1)
                for i in range(0, len(tables), per_row)
            ]
            rows.append(jnp.zeros((16 - len(rows), feats), jnp.float32))
            out[m, base : base + 16, :] = jnp.concatenate(rows, axis=0).astype(jnp.bfloat16)
        for copy in copies:
            copy.wait()

    return kernel_call(
        body,
        [((micro_n, base + 16, feats), stream.dtype)],
        (seq_ids, bucket_ids),
        hbm=(stream,),
        scratch=[pltpu.SemaphoreType.DMA((n_val * micro_n,))],
        label="batch_parts",
        room=WHOLE_VMEM,
    )[0]


def feature_parts(coords, got, other, low_vectors, high_vectors):
    n_seg, rows, feats = other.shape
    tok_rows = (rows - 16) // 2
    half = tok_rows // 2

    def body(coords, got, other, low_vectors, high_vectors, low, high, *outs):
        is_low = coords[0] == 0

        def sides(seg, stream):
            rows = pl.ds(pl.multiple_of(stream * tok_rows + coords[0] * half, half), half)
            mine, theirs = got[seg, rows, :], other[seg, rows, :]
            return jnp.where(is_low, mine, theirs), jnp.where(is_low, theirs, mine)

        for c in range(n_seg):
            there = pl.ds(c * half, half)
            low[there, :], high[there, :] = sides(c, 1)
        high[n_seg * half :, :] = jnp.concatenate(
            [split_three(v[5:6, :feats])[:8] for v in (low_vectors, high_vectors)], axis=0
        )
        for k in range(4):
            outs[k][:half, :], outs[k][half:, :] = sides(coords[1] ^ k, 0)

    dtype = got.dtype
    low, high, *firsts = kernel_call(
        body,
        [((n_seg * half, feats), dtype), ((n_seg * half + 16, feats), dtype)]
        + [((2 * half, feats), dtype)] * 4,
        (got, other, low_vectors, high_vectors),
        scalars=coords,
        label="feature_parts",
    )
    return low, high, firsts


def first_tokens(coords, parts, vectors, after):
    n_tok, feats = parts[0].shape
    n_own, width = n_tok // 4, 4 * feats

    def body(coords, p0, p1, p2, p3, vectors, stream, *rest):
        gain, shift = vectors[0:1, :], vectors[1:2, :]
        lows, rows_all = rest[:4], rest[4]
        for k, part in enumerate((p0, p1, p2, p3)):
            cols = pl.ds(pl.multiple_of((coords[1] ^ k) * feats, feats), feats)
            for j in range(4):
                rows = pl.ds(pl.multiple_of((coords[1] ^ j) * n_own, n_own), n_own)
                rows_all[pl.ds(j * n_own, n_own), cols] = part[rows, :].astype(jnp.float32)
        stream[...] = rows_all[pl.ds(0, n_own), :]
        for j in range(4):
            scaled, _ = rows_norm(rows_all[pl.ds(j * n_own, n_own), :])
            lows[j][...] = (scaled * gain + shift).astype(jnp.bfloat16)

    stream, *lows = kernel_call(
        body,
        [((n_own, width), jnp.float32)] + [((n_own, width), jnp.bfloat16)] * 4,
        (*parts, vectors),
        scalars=coords,
        after=after,
        scratch=[pltpu.VMEM((n_tok, width), jnp.float32)],
        label="first_tokens",
    )
    return stream, lows


def first_grads(coords, parts):
    n_tok, feats = parts[0].shape
    n_tok = n_tok - 16
    n_own, width = n_tok // 4, 4 * feats

    def body(coords, p0, p1, p2, p3, stream, small, shifts, *lows):
        for k, part in enumerate((p0, p1, p2, p3)):
            cols = pl.ds(pl.multiple_of((coords[1] ^ k) * feats, feats), feats)
            for j in range(4):
                rows = pl.ds(pl.multiple_of((coords[1] ^ j) * n_own, n_own), n_own)
                lows[j][:, cols] = part[rows, :]
            extra = part[pl.ds(n_tok, 16), :].astype(jnp.float32)
            for i in range(2):
                shifts[i : i + 1, cols] = (
                    extra[8 * i : 8 * i + 1, :]
                    + extra[8 * i + 1 : 8 * i + 2, :]
                    + extra[8 * i + 2 : 8 * i + 3, :]
                )
        total = lows[0][...].astype(jnp.float32)
        stream[...] = total
        small[...] = jnp.zeros(small.shape, jnp.float32)
        small[2:3, :] = jnp.sum(total, axis=0, keepdims=True)

    stream, small, shifts, *lows = kernel_call(
        body,
        [
            ((n_own, width), jnp.float32),
            ((8, width), jnp.float32),
            ((2, width), jnp.float32),
        ]
        + [((n_own, width), jnp.bfloat16)] * 4,
        parts,
        scalars=coords,
        label="first_grads",
    )
    return stream, small, shifts, lows


def held_back(values, after):
    n = len(values)

    def body(*refs):
        for i in range(n):
            refs[n + i][...] = refs[i][...]

    return kernel_call(body, [(v.shape, v.dtype) for v in values], values, after=after, label="held_back")


def exchange(parts, axis):
    return lax.all_to_all(parts, axis, split_axis=0, concat_axis=0, tiled=True)


def own_rows(coords, parts):
    half, feats = parts[0].shape[0] // 2, parts[0].shape[1]

    def body(coords, p0, p1, p2, p3, low, high):
        for k, part in enumerate((p0, p1, p2, p3)):
            cols = pl.ds(pl.multiple_of((coords[1] ^ k) * feats, feats), feats)
            low[:, cols] = part[:half, :].astype(jnp.float32)
            high[:, cols] = part[half:, :].astype(jnp.float32)

    return kernel_call(
        body,
        [((half, 4 * feats), jnp.float32)] * 2,
        parts,
        scalars=coords,
        label="own_rows",
    )


def split_two(value):
    first = value.astype(jnp.bfloat16)
    return first, (value - first.astype(jnp.float32)).astype(jnp.bfloat16)


def small_from(part, at, feats):
    pieces = [part[at + 16 * q : at + 16 * q + 16, :].astype(jnp.float32) for q in range(4)]
    return jnp.concatenate(pieces, axis=1)


def store_small(out, at, small, feats):
    low = small.astype(jnp.bfloat16)
    for q in range(4):
        out[at + 16 * q : at + 16 * q + 16, :] = low[:, q * feats : (q + 1) * feats]


def meet(first, second):
    both = lax.optimization_barrier((*first, *second))
    return list(both[: len(first)]), list(both[len(first) :])


def stream_home(coords, later, grad, small_low, small_high, bias_low, beside):
    n_val = len(later)
    half, width = later[0].shape
    feats = width // 4
    base = n_val * half
    tall = 2 * base

    def split_body(coords, *refs):
        bias_low, sent, kept, small = refs[2 * n_val + 6 :]
        for i in range(n_val):
            low, high = refs[i], refs[n_val + i]
            rows = pl.ds(i * half, half)
            sent[rows, :] = jnp.where(coords[0] == 0, low[...], high[...]).astype(jnp.bfloat16)
            kept[rows, :] = jnp.where(coords[0] == 0, high[...], low[...]).astype(jnp.bfloat16)
        small[...] = jnp.zeros(small.shape, jnp.float32)
        for layer in range(2):
            attn, feed, back = refs[2 * n_val + 3 * layer : 2 * n_val + 3 * layer + 3]
            small[8 * layer : 8 * layer + 2, :] = attn[0:2, :]
            small[8 * layer + 2 : 8 * layer + 4, :] = feed[0:2, :]
            small[8 * layer + 4 : 8 * layer + 5, :] = back[2:3, :]
        for z, row in enumerate(BIAS_ROWS):
            value = jnp.where(coords[1] == z, bias_low[0:1, :], 0.0)
            small[row : row + 1, :] = value
        first, second = split_two(small[...])
        sent[base : base + 16, :] = first
        sent[base + 16 : base + 32, :] = second

    sent, kept, small = kernel_call(
        split_body,
        [
            ((base + 32, width), jnp.bfloat16),
            ((base, width), jnp.bfloat16),
            ((16, width), jnp.float32),
        ],
        (*later, *grad, *small_low, *small_high, bias_low),
        scalars=coords,
        label="stream_split",
    )
    got = swap_cores(sent)
    types = [((tall + 64, feats), jnp.bfloat16)] * 4

    def body(coords, kept, small, got, *outs):
        total = small[...] + got[base : base + 16, :].astype(jnp.float32)
        total = total + got[base + 16 : base + 32, :].astype(jnp.float32)
        for k in range(4):
            cols = pl.ds(pl.multiple_of((coords[1] ^ k) * feats, feats), feats)
            for i in range(n_val):
                rows = pl.ds(i * half, half)
                at = 2 * i * half
                there = pl.ds(pl.multiple_of(at + coords[0] * half, half), half)
                outs[k][there, :] = kept[rows, cols]
                there = pl.ds(pl.multiple_of(at + (1 - coords[0]) * half, half), half)
                outs[k][there, :] = got[rows, cols]
            store_small(outs[k], tall, total, feats)

    parts = kernel_call(body, types, (kept, small, got), scalars=coords, label="stream_home")
    parts, beside[1:] = meet([parts[0]] + xor_recv(parts[1:], "head"), beside[1:])

    def middle_body(coords, *refs):
        parts, outs = refs[:4], refs[4:]
        total = small_from(parts[0], tall, feats)
        for k in range(1, 4):
            total = total + small_from(parts[k], tall, feats)
        turn = coords[1] ^ coords[2]
        for j in range(4):
            value = parts[j][:tall, :]
            for k in range(1, 4):
                value = jnp.where(turn == k, parts[j ^ k][:tall, :], value)
            outs[j][:tall, :] = value
            store_small(outs[j], tall, total, feats)

    parts = kernel_call(
        middle_body, types, parts, scalars=coords, label="stream_middle"
    )
    parts, beside[:1] = meet(list(parts), beside[:1])
    parts = [parts[0]] + xor_recv(parts[1:], "rows")

    def last_body(coords, *refs):
        parts = refs[:4]
        stream, attn_gain, attn_shift, ffn_gain, ffn_shift, back, bias, scratch = refs[4:]
        total = small_from(parts[0], tall, feats)
        for k in range(1, 4):
            total = total + small_from(parts[k], tall, feats)
        scratch[...] = jnp.where(coords[0] == 0, total[:8, :], total[8:, :])
        here = jnp.zeros((1, width), jnp.float32)
        for z, row in enumerate(BIAS_ROWS):
            here = jnp.where(coords[1] == z, total[row : row + 1, :], here)
        bias[...] = here
        for k in range(4):
            for i in range(n_val):
                rows = pl.ds(2 * i * half, 2 * half)
                stream[i, coords[2] ^ k] = parts[k][rows, :].astype(jnp.float32)
        for i, out in enumerate((attn_gain, attn_shift, ffn_gain, ffn_shift)):
            out[...] = scratch[i : i + 1, :]
        cols = pl.ds(pl.multiple_of(coords[1] * feats, feats), feats)
        back[...] = scratch[4:5, cols]

    return beside, kernel_call(
        last_body,
        [((n_val, 4, 2 * half, feats), jnp.float32)]
        + [((1, width), jnp.float32)] * 4
        + [((1, feats), jnp.float32), ((1, width), jnp.float32)],
        parts,
        scalars=coords,
        scratch=[pltpu.VMEM((8, width), jnp.float32)],
        label="stream_last",
    )


def order_vectors(coords, own, got):
    def body(coords, own, got, low, high):
        low[...] = jnp.where(coords[0] == 0, own[...], got[...])
        high[...] = jnp.where(coords[0] == 0, got[...], own[...])

    return kernel_call(
        body, [(own.shape, own.dtype)] * 2, (own, got), scalars=coords, label="order_vectors"
    )


def score_masking(coords, got, rounds_n, after):
    n_seg, rows, feats = got.shape
    tok_rows = (rows - 16) // 2
    half = tok_rows // 2
    n_tok = n_seg * tok_rows
    n_blocks = n_tok // BLOCK
    per_row = feats // tok_rows

    def places(coords, shape, dim):
        index = lax.broadcasted_iota(jnp.int32, shape, dim)
        seg = coords[1] ^ ((index // half) % 4)
        side = coords[0] ^ (index // (4 * half))
        return seg * tok_rows + side * half + index % half

    def tables(coords, got, by_lane, by_row):
        natural = []
        for i in range(8):
            if i > rounds_n:
                natural.append(jnp.zeros((1, n_tok), jnp.bfloat16))
                continue
            row, cols = 2 * tok_rows + i // per_row, (i % per_row) * tok_rows
            natural.append(
                jnp.concatenate(
                    [
                        got[c, row : row + 1, cols : cols + tok_rows].astype(jnp.float32)
                        for c in range(n_seg)
                    ],
                    axis=1,
                ).astype(jnp.bfloat16)
            )
        natural = jnp.concatenate([part.astype(jnp.float32) for part in natural], axis=0)
        natural = natural.astype(jnp.bfloat16)
        index = lax.broadcasted_iota(jnp.int32, (n_tok, n_tok), 0)
        moving = (index == places(coords, (n_tok, n_tok), 1)).astype(jnp.float32)
        moving = moving.astype(jnp.bfloat16)
        lane_ints = dot_plain(natural, moving)
        lane_keys = lane_ints[0:1, :] * 1024.0 + lane_ints[1 : 1 + rounds_n, :]
        lane_places = places(coords, (1, n_tok), 1).astype(jnp.float32)
        by_lane[:rounds_n, :] = lane_keys * float(n_tok) + lane_places
        by_lane[rounds_n:, :] = lane_keys
        row_ints = lax.dot_general(
            moving, natural, (((0,), (1,)), ((), ())), preferred_element_type=jnp.float32
        )
        row_keys = row_ints[:, 0:1] * 1024.0 + row_ints[:, 1 : 1 + rounds_n]
        row_places = places(coords, (n_tok, 1), 0).astype(jnp.float32)
        by_row[:, :rounds_n] = row_keys * float(n_tok) + row_places
        by_row[:, rounds_n:] = row_keys

    def body(coords, got, masking, by_lane, by_row):
        tables(coords, got, by_lane, by_row)
        for start in range(0, n_tok, TILE):
            masking[pl.ds(start, TILE), :] = jnp.zeros((TILE, n_tok), jnp.float32)
        for r in range(rounds_n):
            lane_code = by_lane[r : r + 1, :]
            lane_key = by_lane[rounds_n + r : rounds_n + r + 1, :]
            behind = jnp.zeros((1, n_tok), jnp.float32)
            for start in range(0, n_tok, TILE):
                rows = pl.ds(start, TILE)
                less = (lane_code < by_row[rows, r : r + 1]).astype(jnp.float32)
                behind = behind + jnp.sum(less, axis=0, keepdims=True)
            lane_block = jnp.floor((n_tok - 1.0 - behind) * (1.0 / BLOCK))
            lane_place = lane_key * (2.0 * n_blocks) + lane_block
            for start in range(0, n_tok, TILE):
                rows = pl.ds(start, TILE)
                less = lane_code < by_row[rows, r : r + 1]
                rank = jnp.sum(less.astype(jnp.float32), axis=1, keepdims=True)
                row_place = by_row[rows, rounds_n + r : rounds_n + r + 1] * (
                    2.0 * n_blocks
                ) + jnp.floor(rank * (1.0 / BLOCK))
                seen = less & (row_place - lane_place < 1.5)
                masking[rows, :] += seen.astype(jnp.float32)
        for start in range(0, n_tok, TILE):
            rows = pl.ds(start, TILE)
            count = masking[rows, :]
            itself = by_lane[0:1, :] == by_row[rows, 0:1]
            other = jnp.where(itself, -100000.0, -1000000000.0)
            masking[rows, :] = jnp.where(count > 0.5, jnp.log(jnp.maximum(count, 1.0)), other)

    return kernel_call(
        body,
        [((n_tok, n_tok), jnp.float32)],
        (got,),
        scalars=coords,
        after=after,
        scratch=[
            pltpu.VMEM((2 * rounds_n, n_tok), jnp.float32),
            pltpu.VMEM((n_tok, 2 * rounds_n), jnp.float32),
        ],
        label="score_masking",
    )[0]


def parallel_local(
    stream_in,
    attn_gain,
    attn_shift,
    w_qk,
    w_value,
    w_out,
    ffn_gain,
    ffn_shift,
    w_in,
    b_in,
    w_back,
    b_back,
    seq_ids,
    bucket_ids,
    sort_order,
):
    core = lax.axis_index("section")
    col = lax.axis_index("head")
    row = lax.axis_index("rows")
    coords = jnp.stack([core, col, row]).astype(jnp.int32)

    batches = batch_parts(stream_in, seq_ids, bucket_ids)
    qv_mine, qv_other, out_mine, out_other, own_vectors = own_weights(
        w_qk,
        w_value,
        w_out,
        (attn_gain, attn_shift, ffn_gain, ffn_shift, b_in, b_back),
        (batches,),
    )
    batches, own_vectors = lax.optimization_barrier((batches, own_vectors))
    batch_got = exchange(batches, "rows")
    vectors = order_vectors(coords, own_vectors, swap_cores(own_vectors))
    low_part, high_part, firsts = feature_parts(
        coords, batch_got, swap_cores(batch_got), *vectors
    )
    qv_pair = (qv_mine, swap_cores(qv_other))
    out_pair = (out_mine, swap_cores(out_other))
    low_parts = gather_four(low_part, "head")
    masking = score_masking(coords, batch_got, bucket_ids.shape[1], (low_part,))
    first_vectors, *got_weights = lax.optimization_barrier((vectors[0], qv_pair[1], out_pair[1]))
    qv_pair, out_pair = (qv_mine, got_weights[0]), (out_mine, got_weights[1])
    second, lows = first_tokens(coords, low_parts, first_vectors, (masking,))
    first, grad_first = own_rows(coords, [firsts[0]] + xor_recv(firsts[1:], "head"))

    kept = []
    pieces = both_halves(lows)
    for layer in range(2):
        far_part, near_part, attn_in, qv, prob, mixed = attention_forward(
            layer, pieces, qv_pair, out_pair, masking
        )
        if layer == 0:
            held_in, held_out, far_part = lax.optimization_barrier((w_in[0], w_back[0], far_part))
            wide_in = (w_in[0], swap_cores(held_in))
            wide_back = (w_back[0], swap_cores(held_out))
        parts = scatter_tokens(far_part, near_part, "head")
        attn_stream = second
        first, low = residual_norm(first, parts, (), vectors[layer], (2, 3))
        if layer == 0:
            (high_part,) = held_back((high_part,), (low,))
            grad_second, small_back, shifts, grad_lows = first_grads(
                coords, gather_four(high_part, "head")
            )
        sent, ffn_in, active, slope = feed_forward(
            layer, gather_four(low, "head"), vectors[layer], 4, wide_in, wide_back
        )
        kept.append((attn_in, qv, prob, mixed, attn_stream, ffn_in, active, slope, first))
        if layer == 0:
            parts = [sent[0]] + xor_recv(sent[1:], "head")
            second, low = residual_norm(second, parts, (), vectors[1], (0, 1), (shifts, 0))
            pieces = gather_tokens(low, "head")
    last_sent = sent

    small_rows = [None] * 2
    feed_first, attn_first, feed_close = (), (), ()
    for layer in (1, 0):
        attn_in, qv, prob, mixed, attn_stream, ffn_in, active, slope, ffn_stream = kept[layer]
        sent, grad_in, dpre = feed_backward(
            layer, grad_lows, slope, wide_in, wide_back, feed_first
        )
        parts = [sent[0]] + xor_recv(sent[1:], "head")
        *feed_out, feed_mark = feed_grads(
            coords, ffn_in, grad_in, active, dpre, layer == 1, tuple(parts[1:]) if layer else ()
        )
        if layer == 0:
            high_heads, heads_mark = add_four(head_arrived, tuple(parts[1:]), "add_heads")
            feed_close = (heads_mark,)
        grad_first, grad_low, feed_small = norm_backward(
            grad_first, parts, ffn_stream, vectors[layer], 2, (feed_mark, *feed_close)
        )
        near = gather_four(grad_low, "head")
        if layer == 1:
            feed_kept, *feed_sent, cores_mark = add_cores(
                feed_out[0], swap_cores(feed_out[1]), tuple(near[1:])
            )
            feed_arrived = [feed_kept] + xor_recv(feed_sent, "rows")
            attn_first = (cores_mark,)
        else:
            low_hidden = lax.psum(feed_out[0], ("section", "rows"))
            bias_low = feed_out[1]
            attn_first = (mine[3],)
        far_part, near_part, grad_out, dqv = attention_backward(
            layer, both_halves(near), qv_pair, out_pair, qv, prob, attn_first
        )
        parts = scatter_tokens(far_part, near_part, "head")
        *attn_parts, attn_mark = head_grads(
            coords, attn_in, grad_out, mixed, dqv, tuple(parts[1:])
        )
        closing = (attn_mark,)
        if layer == 0:
            high_layer, pack_mark = to_layer(mine, 1, tuple(parts[1:]))
            closing = (attn_mark, pack_mark)
        head_arrived = [attn_parts[0]] + xor_recv(attn_parts[1:], "rows")
        back_small = small_back
        grad_second, grad_low, small_back = norm_backward(
            grad_second, parts, attn_stream, vectors[layer], 0, closing
        )
        small_rows[layer] = (small_back, feed_small, back_small)
        if layer == 1:
            grad_lows = gather_four(grad_low, "head")
            high_own, high_mark = add_four(feed_arrived, tuple(grad_lows[1:]), "add_feed")
            mine = gather_four(high_own, "rows")
            feed_first = (high_mark,)
    (grad_second,), last_sent = meet([grad_second], last_sent)
    last_got, head_got = meet(xor_recv(last_sent[1:], "head"), head_arrived[1:])
    (second,) = residual_norm(
        second, [last_sent[0]] + last_got, (), vectors[1], None, (shifts, 1)
    )
    low_heads, _ = add_four([head_arrived[0]] + head_got, (), "add_heads")
    heads = gather_four(pair_heads(coords, low_heads, high_heads), "rows")
    (low_hidden, *heads), (stream_out, *small_out, back_out, bias_low) = stream_home(
        coords,
        (first, second),
        (grad_first, grad_second),
        *small_rows,
        bias_low,
        [low_hidden, *heads],
    )
    dim = w_qk.shape[2] // 2
    grad_w_qk, grad_w_value, grad_w_out, heads_mark = place_heads(coords, heads, dim)
    grad_w_in, grad_w_back, grad_b_in = place_hidden(
        coords, low_hidden, high_layer, bias_low, (heads_mark,)
    )
    return (
        stream_out[None],
        small_out[0],
        small_out[1],
        grad_w_qk[None],
        grad_w_value[None],
        grad_w_out[None],
        small_out[2],
        small_out[3],
        grad_w_in[None],
        grad_b_in,
        grad_w_back[None],
        back_out,
    )


def solution(mesh):
    placed = (
        P("section", None, None, "rows", "head"),
        P("section", None),
        P("section", None),
        P("section", None, "head"),
        P("section", None, "head"),
        P("section", "head", None),
        P("section", None),
        P("section", None),
        P("section", None, "head"),
        P("section", "head"),
        P("section", "head", None),
        P("section", "head"),
        P(None, "rows"),
        P(None, None, "rows"),
        P(None, None, "rows"),
    )
    sizes = mesh.shape
    grid_fits = (sizes["section"], sizes["head"], sizes["rows"]) == (2, 4, 4)
    return jax.shard_map(
        parallel_local if grid_fits else local,
        mesh=mesh,
        in_specs=placed,
        out_specs=(
            P("section", None, None, "rows", "head"),
            P("section", None),
            P("section", None),
            P("section", None, "head"),
            P("section", None, "head"),
            P("section", "head", None),
            P("section", None),
            P("section", None),
            P("section", None, "head"),
            P("section", "head"),
            P("section", "head", None),
            P("section", "head"),
        ),
        check_vma=False,
    )
```
